32 devices in a mesh: grp: 8 (over z, y), in: 4 (over x, core).
Axes of the slice: x: 2, y: 2, z: 4, core: 2. Of those that a mesh axis runs over, the one named last changes fastest.
Arguments:
- canvas: bfloat16 [640, 6, 6, 2048], P(('grp', 'in')), may hold values from -6 to 6
- reduce_weight: bfloat16 [2048, 512], replicated, may hold values from -0.125 to 0.125
- gain_first: float32 [512], replicated, may hold values from 0.5 to 1.5
- shift_first: float32 [512], replicated, may hold values from -3 to 3
- spatial_weight: bfloat16 [4608, 512], replicated, may hold values from -0.09375 to 0.09375
- gain_second: float32 [512], replicated, may hold values from 0.5 to 1.5
- shift_second: float32 [512], replicated, may hold values from -3 to 3
- expand_weight: bfloat16 [512, 2048], replicated, may hold values from -0.25 to 0.25
- gain_third: float32 [2048], replicated, may hold values from 0.5 to 1.5
- shift_third: float32 [2048], replicated, may hold values from -3 to 3
- hidden_weight: bfloat16 [2048, 2048], replicated, may hold values from -0.125 to 0.125
- gain_head: float32 [2048], replicated, may hold values from 0.5 to 1.5
- shift_head: float32 [2048], replicated, may hold values from -3 to 3
- embed_weight: bfloat16 [2048, 128], replicated, may hold values from -0.125 to 0.125
- embed_bias: float32 [128], replicated, may hold values from -3 to 3
- prototypes: bfloat16 [3000, 128], replicated, may hold values from -0.75 to 0.75
- queued: bfloat16 [480, 128], P(('grp', 'in')), may hold values from -0.5 to 0.5
- crop_ids: int32 [640, 6, 6], P(('grp', 'in')), may hold values from 0 to 3, as said below
- partner: int32 [640, 4], P(('grp', 'in')), may hold values from 0 to 3, as said below
Outputs:
- crop_loss: float32 [640, 4], P(('grp', 'in'))
- canvas_grad: bfloat16 [640, 6, 6, 2048], P(('grp', 'in'))
- reduce_grad: float32 [2048, 512], P('grp', 'in')
- spatial_grad: float32 [4608, 512], P('grp', 'in')
- expand_grad: float32 [512, 2048], P('grp', 'in')
- hidden_grad: float32 [2048, 2048], P('grp', 'in')
- embed_grad: float32 [2048, 128], P('grp', 'in')
- embed_bias_grad: float32 [128], replicated
- prototypes_grad: float32 [3000, 128], P(None, 'in')
- gain_first_grad: float32 [512], replicated
- shift_first_grad: float32 [512], replicated
- gain_second_grad: float32 [512], replicated
- shift_second_grad: float32 [512], replicated
- gain_third_grad: float32 [2048], replicated
- shift_third_grad: float32 [2048], replicated
- gain_head_grad: float32 [2048], replicated
- shift_head_grad: float32 [2048], replicated
The draws below stay inside these ranges and needn't reach their ends.
Inputs may be any that keep to these rules, and one draw needn't show every extreme that they name: `crop_ids`: each of a canvas's four quadrants of 3 x 3 pixels holds one crop, all pixels of a quadrant carrying the same crop number and the four quadrants carrying four different ones. `partner`: in each canvas the entries name the canvas's other crops and form one cycle through all 4 crops.
All inputs are finite; a program needn't handle non-finite values.
Results may differ from the reference program's by a relative error of at most 0.024.
Values sent between devices are 32-bit elements; how exact they have to be, the bound alone decides.
No kernel may reach another device: no remote copies, remote signals or barrier semaphores. Data moves between devices by JAX's collectives and lax.ppermute only.
A program may use at most 192 MiB of HBM per device.

```python
import jax
import jax.numpy as jnp
from jax import lax

CHANNELS = 2048
NECK = 512
HIDDEN_SIZE = 2048
EMBED = 128
PROTOS = 3000
SIDE = 6
CROPS = 4
ITERS = 3
CANVASES = 640
QUEUE = 480


def draw_crop_ids(key, part):
    key = jax.random.fold_in(key, 11)
    subkeys = jax.random.split(key, CANVASES)
    half_index = jnp.arange(SIDE, dtype=jnp.int32) // (SIDE // 2)
    quadrant = half_index[:, None] * 2 + half_index[None, :]

    def draw_canvas(single):
        labels = jax.random.permutation(single, CROPS).astype(jnp.int32)
        return labels[quadrant]
    return jax.vmap(draw_canvas)(subkeys).reshape(CANVASES, SIDE, SIDE).astype(jnp.int32)


def draw_partner(key, part):
    key = jax.random.fold_in(key, 23)
    subkeys = jax.random.split(key, CANVASES)

    def draw_canvas(single):
        ordering = jax.random.permutation(single, CROPS).astype(jnp.int32)
        following = jnp.roll(ordering, -1)
        return jnp.zeros((CROPS,), jnp.int32).at[ordering].set(following)
    return jax.vmap(draw_canvas)(subkeys).astype(jnp.int32)


def steps_of(own_key, shape, shards, low, largest):
    level = 1.0
    for dim, blocks in shards:
        heights = jax.random.uniform(jax.random.fold_in(jax.random.fold_in(own_key, 6), dim), (blocks,), jnp.float32, low / len(shards), largest / len(shards))
        level = level * jnp.repeat(jnp.exp(heights), shape[dim] // blocks).reshape((-1,) + (1,) * (len(shape) - 1 - dim))
    return level


def gaussian(stream_key, shape, scale, most, pieces=(), kind=jnp.bfloat16):
    values = jax.random.normal(stream_key, shape, jnp.float32) * scale
    if len(pieces) > 0:
        values = steps_of(stream_key, shape, pieces, -0.22, 0.18) * values
    return jnp.clip(values, min=-most, max=most).astype(kind)


def setup_inputs(seed: int = 0) -> dict:
    key_list = jax.random.split(jax.random.key(seed), 20)
    canvas = gaussian(key_list[0], (CANVASES, SIDE, SIDE, CHANNELS), 1.0, 6.0, ((0, 32),))
    reduce_weight = gaussian(key_list[1], (CHANNELS, NECK), CHANNELS ** -0.5, 0.125)
    gain_first = jnp.clip(1.0 + 0.1 * jax.random.normal(key_list[2], (NECK,), jnp.float32), 0.5, 1.5)
    shift_first = gaussian(key_list[3], (NECK,), 0.5, 3.0, (), jnp.float32)
    spatial_weight = gaussian(key_list[4], (9 * NECK, NECK), (9 * NECK) ** -0.5, 0.09375)
    gain_second = jnp.clip(1.0 + 0.1 * jax.random.normal(key_list[5], (NECK,), jnp.float32), 0.5, 1.5)
    shift_second = gaussian(key_list[6], (NECK,), 0.5, 3.0, (), jnp.float32)
    expand_weight = gaussian(key_list[7], (NECK, CHANNELS), NECK ** -0.5, 0.25)
    gain_third = jnp.clip(1.0 + 0.1 * jax.random.normal(key_list[8], (CHANNELS,), jnp.float32), 0.5, 1.5)
    shift_third = gaussian(key_list[9], (CHANNELS,), 0.5, 3.0, (), jnp.float32)
    hidden_weight = gaussian(key_list[10], (CHANNELS, HIDDEN_SIZE), CHANNELS ** -0.5, 0.125)
    gain_head = jnp.clip(1.0 + 0.1 * jax.random.normal(key_list[11], (HIDDEN_SIZE,), jnp.float32), 0.5, 1.5)
    shift_head = gaussian(key_list[12], (HIDDEN_SIZE,), 0.5, 3.0, (), jnp.float32)
    embed_weight = gaussian(key_list[13], (HIDDEN_SIZE, EMBED), HIDDEN_SIZE ** -0.5, 0.125)
    embed_bias = gaussian(key_list[14], (EMBED,), 0.5, 3.0, (), jnp.float32)
    prototypes = gaussian(key_list[15], (PROTOS, EMBED), (EMBED // 2) ** -0.5, 0.75)
    queued = gaussian(key_list[16], (QUEUE, EMBED), EMBED ** -0.5, 0.5, ((0, 32),))
    crop_ids = draw_crop_ids(jax.random.fold_in(key_list[19], 71), 0)
    partner = draw_partner(jax.random.fold_in(key_list[19], 71), 0)
    return {"canvas": canvas, "reduce_weight": reduce_weight, "gain_first": gain_first, "shift_first": shift_first, "spatial_weight": spatial_weight, "gain_second": gain_second, "shift_second": shift_second, "expand_weight": expand_weight, "gain_third": gain_third, "shift_third": shift_third, "hidden_weight": hidden_weight, "gain_head": gain_head, "shift_head": shift_head, "embed_weight": embed_weight, "embed_bias": embed_bias, "prototypes": prototypes, "queued": queued, "crop_ids": crop_ids, "partner": partner}


@jax.custom_vjp
def low(v):
    return lax.optimization_barrier(v.astype(jnp.bfloat16)).astype(jnp.float32)

@jax.custom_vjp
def low_back(v):
    return v

def low_keep(v):
    return (low(v), None)

def low_pass(kept, grad):
    return (grad,)

def back_keep(v):
    return (v, None)

def back_low(kept, grad):
    return (low(grad),)
low.defvjp(low_keep, low_pass)
low_back.defvjp(back_keep, back_low)
BATCH_EPSILON = 1e-05
UNIT_EPSILON = 1e-06
SOFTMAX_WARMTH = 0.1
TRANSPORT_SMOOTH = 0.05
PRECISE = lax.Precision.HIGHEST

def matmul(left, right):
    return jnp.dot(left, right, precision=PRECISE)

def batch_norm(value, gain, shift):
    middle = lax.optimization_barrier(jnp.mean(value, axis=0))
    spread = lax.optimization_barrier(jnp.mean(value * value, axis=0)) - middle * middle
    return (value - middle) * lax.rsqrt(spread + BATCH_EPSILON) * gain + shift

def tile_mask(vertical, lateral):
    tile_side = SIDE // 2
    position = jnp.arange(SIDE, dtype=jnp.int32) % tile_side
    row_valid = ((position + vertical - 1 >= 0) & (position + vertical - 1 < tile_side)).astype(jnp.float32)
    column_valid = ((position + lateral - 1 >= 0) & (position + lateral - 1 < tile_side)).astype(jnp.float32)
    return row_valid[:, None] * column_valid[None, :]

@jax.checkpoint
def spatial(field, weight):
    canvas_grid = field.reshape(-1, SIDE, SIDE, NECK)
    padded = jnp.pad(canvas_grid, ((0, 0), (1, 1), (1, 1), (0, 0)))
    total = jnp.zeros((canvas_grid.shape[0] * SIDE * SIDE, NECK), jnp.float32)
    for window in range(9):
        vertical = window // 3
        lateral = window % 3
        masked = padded[:, vertical:vertical + SIDE, lateral:lateral + SIDE, :] * tile_mask(vertical, lateral)[None, :, :, None]
        total = total + matmul(masked.reshape(-1, NECK), weight[window * NECK:(window + 1) * NECK])
    return total

def normalize_rows(embedded):
    return embedded * lax.rsqrt(lax.optimization_barrier(jnp.sum(embedded * embedded, axis=1, keepdims=True)) + UNIT_EPSILON)

def network(member, canvas, reduce_weight, gain_first, shift_first, spatial_weight, gain_second, shift_second, expand_weight, gain_third, shift_third, hidden_weight, gain_head, shift_head, embed_weight, embed_bias):
    pixels = canvas.reshape(-1, CHANNELS)
    reduced = low_back(matmul(pixels, reduce_weight))
    act_first = low(jax.nn.gelu(batch_norm(reduced, gain_first, shift_first)))
    conved = low_back(spatial(act_first, spatial_weight))
    act_second = low(jax.nn.gelu(batch_norm(conved, gain_second, shift_second)))
    expanded = low_back(matmul(act_second, expand_weight))
    output = jax.nn.gelu(batch_norm(expanded, gain_third, shift_third) + pixels)
    counts = lax.optimization_barrier(jnp.sum(member, axis=1))[:, :, None]
    pooled = jnp.einsum('cpk,cpd->ckd', member, output.reshape(-1, SIDE * SIDE, CHANNELS), precision=PRECISE) / counts
    pooled = low(pooled.reshape(-1, CHANNELS))
    head_pre = low_back(matmul(pooled, hidden_weight))
    act_head = low(jax.nn.gelu(batch_norm(head_pre, gain_head, shift_head)))
    embedded = low_back(matmul(act_head, embed_weight)) + embed_bias
    return normalize_rows(embedded)

def crop_similarity(normalized_features, cluster_centers):
    return low_back(jnp.dot(low(normalized_features), cluster_centers.T, precision=PRECISE))

def balanced_transport(similarity_matrix, queue_similarity):
    crop_probability = jnp.exp(similarity_matrix / TRANSPORT_SMOOTH)
    queue_probability = jnp.exp(queue_similarity / TRANSPORT_SMOOTH)
    for sweep_index in range(ITERS):
        column = lax.optimization_barrier(jnp.sum(crop_probability, axis=0)) + lax.optimization_barrier(jnp.sum(queue_probability, axis=0))
        crop_probability = crop_probability / column
        queue_probability = queue_probability / column
        crop_probability = crop_probability / lax.optimization_barrier(jnp.sum(crop_probability, axis=1, keepdims=True))
        queue_probability = queue_probability / lax.optimization_barrier(jnp.sum(queue_probability, axis=1, keepdims=True))
    return crop_probability

def head_loss(normalized_features, cluster_centers, target):
    scaled_similarity = crop_similarity(normalized_features, cluster_centers) / SOFTMAX_WARMTH
    log_total = jax.nn.logsumexp(scaled_similarity, axis=1, keepdims=True)
    return -lax.optimization_barrier(jnp.sum(target * (scaled_similarity - log_total), axis=1))

def reference(canvas, reduce_weight, gain_first, shift_first, spatial_weight, gain_second, shift_second, expand_weight, gain_third, shift_third, hidden_weight, gain_head, shift_head, embed_weight, embed_bias, prototypes, queued, crop_ids, partner):
    member = (crop_ids.reshape(-1, SIDE * SIDE)[:, :, None] == jnp.arange(CROPS, dtype=jnp.int32)[None, None, :]).astype(jnp.float32)
    floats = [value.astype(jnp.float32) for value in (canvas, reduce_weight, gain_first, shift_first, spatial_weight, gain_second, shift_second, expand_weight, gain_third, shift_third, hidden_weight, gain_head, shift_head, embed_weight, embed_bias)]

    def forward(*params):
        return network(member, *params)
    normalized_features, net_back = jax.vjp(forward, *floats)
    cluster_centers = prototypes.astype(jnp.float32)
    similarity_matrix = jnp.dot(low(normalized_features), cluster_centers.T, precision=PRECISE)
    queue_similarity = jnp.dot(queued.astype(jnp.float32), cluster_centers.T, precision=PRECISE)
    cluster_assignments = balanced_transport(similarity_matrix, queue_similarity)
    select = (partner[:, :, None] == jnp.arange(CROPS, dtype=jnp.int32)[None, None, :]).astype(jnp.float32)
    target = jnp.einsum('cjk,ckp->cjp', select, cluster_assignments.reshape(-1, CROPS, PROTOS), precision=PRECISE).reshape(-1, PROTOS)

    def loss_of(unit_in, proto_in):
        return head_loss(unit_in, proto_in, target)
    losses, loss_back = jax.vjp(loss_of, normalized_features, cluster_centers)
    unit_cot, proto_grad = loss_back(jnp.ones_like(losses))
    grads = net_back(unit_cot)
    return (losses.reshape(-1, CROPS), grads[0].astype(jnp.bfloat16), grads[1], grads[4], grads[7], grads[10], grads[13], grads[14], proto_grad, grads[2], grads[3], grads[5], grads[6], grads[8], grads[9], grads[11], grads[12])
```

```python
import functools

import jax
import jax.numpy as jnp
from jax import lax
from jax.experimental import pallas as pl
from jax.experimental.pallas import tpu as pltpu
from jax.sharding import PartitionSpec as P

SIDE = 6
CROPS = 4
ITERS = 3


BATCH_EPSILON = 1e-05
UNIT_EPSILON = 1e-06
SOFTMAX_WARMTH = 0.1
TRANSPORT_SMOOTH = 0.05
PRECISE = lax.Precision.HIGHEST
ROOT = 0.7978845608028654
CUBIC = 0.044715
VMEM_BYTES = 48 * 1024 * 1024


AXES = ("grp", "in")


def bits_of(axis):
    return lax.axis_size(axis).bit_length() - 1


def swap_bit(value, bit):
    count = lax.axis_size("grp") * lax.axis_size("in")
    return lax.ppermute(value, AXES, [(i, i ^ (1 << bit)) for i in range(count)])


def my_bit(bit):
    index = lax.axis_index("grp") * lax.axis_size("in") + lax.axis_index("in")
    return (index >> bit) & 1


def exchange_sum(block, groups):
    size = len(groups[0])
    spread = jnp.broadcast_to(block[None], (size,) + block.shape)
    moved = lax.all_to_all(spread, AXES, 0, 0, tiled=True, axis_index_groups=groups)
    return jnp.sum(moved, 0)


def all_sum(parts):
    count = lax.axis_size("grp") * lax.axis_size("in")
    sizes = [part.size for part in parts]
    flat = jnp.concatenate([part.reshape(-1) for part in parts])
    total = sum(sizes)
    small = total <= 1536
    unit = 1024 if small else 2048
    rows = -(-total // unit) * unit // 128
    flat = jnp.pad(flat, (0, rows * 128 - total)).reshape(rows, 128)
    if small:
        flat = exchange_sum(flat, [list(range(count))])
    else:
        core = my_bit(0)
        halves = flat.reshape(2, rows // 2, 128)
        mine = lax.dynamic_index_in_dim(halves, core, 0, keepdims=False)
        other = lax.dynamic_index_in_dim(halves, 1 - core, 0, keepdims=False)
        mine = mine + swap_bit(other, 0)
        mine = exchange_sum(mine, [list(range(k, count, 2)) for k in range(2)])
        other = swap_bit(mine, 0)
        flat = jnp.concatenate(
            [jnp.where(core == 0, mine, other), jnp.where(core == 0, other, mine)], 0
        )
    flat = flat.reshape(-1)
    sums = []
    start = 0
    for part, size in zip(parts, sizes):
        sums.append(flat[start : start + size].reshape(part.shape))
        start += size
    return sums


def scatter_sum(blocks, splits=2):
    low = bits_of("in")
    high = bits_of("grp")
    count = low + high
    rows = blocks.shape[2]
    columns = blocks.shape[3]
    inner = list(range(low))
    outer = list(range(low, count))
    orders = [inner + outer, inner[:1] + outer + inner[1:]][:splits]
    chunks = []
    for k, order in enumerate(orders):
        piece = blocks[:, :, k * (rows // splits) : (k + 1) * (rows // splits)]
        chunks.append((piece.reshape((2,) * count + (rows // splits, columns)), order))
    left = [list(inner[::-1] + outer[::-1]) for _ in orders]
    for stage in range(count):
        following = []
        for k, (piece, order) in enumerate(chunks):
            bit = order[stage]
            place = left[k].index(bit)
            left[k].remove(bit)
            mine = lax.dynamic_index_in_dim(piece, my_bit(bit), place, keepdims=False)
            other = lax.dynamic_index_in_dim(piece, 1 - my_bit(bit), place, keepdims=False)
            following.append((mine + swap_bit(other, bit), order))
        chunks = following
    return jnp.concatenate([piece for piece, _ in chunks], 0)


def blocked(grad):
    rows, columns = grad.shape
    inner = lax.axis_size("in")
    outer = lax.axis_size("grp")
    return grad.reshape(outer, rows // outer, inner, columns // inner).transpose(2, 0, 1, 3)


def contract_rows(left, right):
    return lax.dot_general(
        left, right, (((0,), (0,)), ((), ())), preferred_element_type=jnp.float32
    )


def gelu_back(before, upstream):
    ignored, backward = jax.vjp(jax.nn.gelu, before)
    return backward(upstream)[0]


def normalize(value, gain, shift):
    count = value.shape[0] * lax.axis_size("grp") * lax.axis_size("in")
    total, squares = all_sum((jnp.sum(value, 0), jnp.sum(value * value, 0)))
    middle = total / count
    rstd = lax.rsqrt(squares / count - middle * middle + BATCH_EPSILON)
    normed = (value - middle) * rstd
    return (normed, rstd, normed * gain + shift)


def norm_sums(upstream, normed):
    return all_sum((jnp.sum(upstream, 0), jnp.sum(upstream * normed, 0)))


def normalize_back(upstream, normed, rstd, gain, shift_sum, gain_sum):
    count = normed.shape[0] * lax.axis_size("grp") * lax.axis_size("in")
    return gain * rstd * (upstream - shift_sum / count - normed * gain_sum / count)


def tile_mask(vertical, lateral):
    tile_side = SIDE // 2
    position = jnp.arange(SIDE, dtype=jnp.int32) % tile_side
    row_valid = ((position + vertical - 1 >= 0) & (position + vertical - 1 < tile_side)).astype(
        jnp.float32
    )
    column_valid = ((position + lateral - 1 >= 0) & (position + lateral - 1 < tile_side)).astype(
        jnp.float32
    )
    return row_valid[:, None] * column_valid[None, :]


def columns(field, neck_width):
    canvas_grid = field.reshape(-1, SIDE, SIDE, neck_width)
    padded = jnp.pad(canvas_grid, ((0, 0), (1, 1), (1, 1), (0, 0)))
    windows = [
        padded[:, vertical : vertical + SIDE, lateral : lateral + SIDE, :]
        * tile_mask(vertical, lateral).astype(field.dtype)[None, :, :, None]
        for vertical in range(3)
        for lateral in range(3)
    ]
    return jnp.concatenate(windows, axis=-1).reshape(-1, 9 * neck_width)


def columns_back(grad_cols, neck_width):
    canvas_grid = grad_cols.reshape(-1, SIDE, SIDE, 9, neck_width)
    padded = jnp.zeros((canvas_grid.shape[0], SIDE + 2, SIDE + 2, neck_width), jnp.float32)
    for window in range(9):
        vertical = window // 3
        lateral = window % 3
        masked = canvas_grid[:, :, :, window, :] * tile_mask(vertical, lateral)[None, :, :, None]
        padded = padded.at[:, vertical : vertical + SIDE, lateral : lateral + SIDE, :].add(masked)
    return padded[:, 1:-1, 1:-1, :].reshape(-1, neck_width)


def normalize_rows(embedded):
    return embedded * lax.rsqrt(jnp.sum(embedded * embedded, axis=1, keepdims=True) + UNIT_EPSILON)


def on_device(
    canvas,
    reduce_weight,
    gain_first,
    shift_first,
    spatial_weight,
    gain_second,
    shift_second,
    expand_weight,
    gain_third,
    shift_third,
    hidden_weight,
    gain_head,
    shift_head,
    embed_weight,
    embed_bias,
    prototypes,
    queued,
    crop_ids,
    partner,
):
    canvases = canvas.shape[0]
    channels = canvas.shape[-1]
    neck_width = reduce_weight.shape[1]
    pixels = canvas.reshape(-1, channels)
    reduced = jnp.dot(pixels, reduce_weight, preferred_element_type=jnp.float32)
    normed_first, rstd_first, pre_first = normalize(reduced, gain_first, shift_first)
    act_first = jax.nn.gelu(pre_first).astype(jnp.bfloat16)
    cols_first = columns(act_first, neck_width)
    conved = jnp.dot(cols_first, spatial_weight, preferred_element_type=jnp.float32)
    normed_second, rstd_second, pre_second = normalize(conved, gain_second, shift_second)
    act_second = jax.nn.gelu(pre_second).astype(jnp.bfloat16)
    expanded = jnp.dot(act_second, expand_weight, preferred_element_type=jnp.float32)
    normed_third, rstd_third, pre_third = normalize(expanded, gain_third, shift_third)
    pre_out = pre_third + pixels.astype(jnp.float32)
    output = jax.nn.gelu(pre_out)
    member = (
        crop_ids.reshape(canvases, SIDE * SIDE, 1)
        == jnp.arange(CROPS, dtype=jnp.int32)[None, None, :]
    ).astype(jnp.float32)
    counts = jnp.sum(member, axis=1)[:, :, None]
    pooled = (
        jnp.einsum(
            "cpk,cpd->ckd",
            member,
            output.reshape(canvases, SIDE * SIDE, channels),
            precision=PRECISE,
        )
        / counts
    )
    pooled_low = pooled.reshape(-1, channels).astype(jnp.bfloat16)
    head_pre = jnp.dot(pooled_low, hidden_weight, preferred_element_type=jnp.float32)
    normed_head, rstd_head, pre_head = normalize(head_pre, gain_head, shift_head)
    act_head = jax.nn.gelu(pre_head).astype(jnp.bfloat16)
    embedded = jnp.dot(act_head, embed_weight, preferred_element_type=jnp.float32) + embed_bias
    normalized_features, unit_back = jax.vjp(normalize_rows, embedded)
    unit_low = normalized_features.astype(jnp.bfloat16)
    similarity_matrix = jnp.dot(unit_low, prototypes.T, preferred_element_type=jnp.float32)
    queue_similarity = jnp.dot(queued, prototypes.T, preferred_element_type=jnp.float32)
    crop_probability = jnp.exp(similarity_matrix / TRANSPORT_SMOOTH)
    queue_probability = jnp.exp(queue_similarity / TRANSPORT_SMOOTH)
    for sweep_index in range(ITERS):
        column = all_sum(
            (jnp.sum(crop_probability, 0) + jnp.sum(queue_probability, 0),)
        )[0]
        crop_probability = crop_probability / column
        queue_probability = queue_probability / column
        crop_probability = crop_probability / jnp.sum(crop_probability, axis=1, keepdims=True)
        queue_probability = queue_probability / jnp.sum(queue_probability, axis=1, keepdims=True)
    select = (partner[:, :, None] == jnp.arange(CROPS, dtype=jnp.int32)[None, None, :]).astype(
        jnp.float32
    )
    target = jnp.einsum(
        "cjk,ckp->cjp", select, crop_probability.reshape(canvases, CROPS, -1), precision=PRECISE
    ).reshape(-1, crop_probability.shape[1])
    scaled_similarity = similarity_matrix / SOFTMAX_WARMTH
    log_total = jax.nn.logsumexp(scaled_similarity, axis=1, keepdims=True)
    crop_loss = -jnp.sum(target * (scaled_similarity - log_total), axis=1)
    grad_scores = (
        (jnp.exp(scaled_similarity - log_total) * jnp.sum(target, axis=1, keepdims=True) - target)
        / SOFTMAX_WARMTH
    ).astype(jnp.bfloat16)
    grad_unit = jnp.dot(grad_scores, prototypes, preferred_element_type=jnp.float32)
    proto_local = contract_rows(grad_scores, unit_low)
    grad_embedded = unit_back(grad_unit)[0]
    grad_embedded_low = grad_embedded.astype(jnp.bfloat16)
    embed_local = contract_rows(act_head, grad_embedded_low)
    grad_act_head = jnp.dot(grad_embedded_low, embed_weight.T, preferred_element_type=jnp.float32)
    grad_pre_head = gelu_back(pre_head, grad_act_head)
    shift_head_grad, gain_head_grad, embed_bias_grad = all_sum(
        (
            jnp.sum(grad_pre_head, 0),
            jnp.sum(grad_pre_head * normed_head, 0),
            jnp.sum(grad_embedded, 0),
        )
    )
    grad_head = normalize_back(
        grad_pre_head, normed_head, rstd_head, gain_head, shift_head_grad, gain_head_grad
    ).astype(jnp.bfloat16)
    hidden_local = contract_rows(pooled_low, grad_head)
    grad_pooled = jnp.dot(grad_head, hidden_weight.T, preferred_element_type=jnp.float32)
    grad_output = jnp.einsum(
        "cpk,ckd->cpd",
        member,
        grad_pooled.reshape(canvases, CROPS, channels) / counts,
        precision=PRECISE,
    ).reshape(-1, channels)
    grad_pre_out = gelu_back(pre_out, grad_output)
    shift_third_grad, gain_third_grad = norm_sums(grad_pre_out, normed_third)
    grad_expanded = normalize_back(
        grad_pre_out, normed_third, rstd_third, gain_third, shift_third_grad, gain_third_grad
    ).astype(jnp.bfloat16)
    expand_local = contract_rows(act_second, grad_expanded)
    grad_pre_second = gelu_back(
        pre_second, jnp.dot(grad_expanded, expand_weight.T, preferred_element_type=jnp.float32)
    )
    shift_second_grad, gain_second_grad = norm_sums(grad_pre_second, normed_second)
    grad_conved = normalize_back(
        grad_pre_second,
        normed_second,
        rstd_second,
        gain_second,
        shift_second_grad,
        gain_second_grad,
    ).astype(jnp.bfloat16)
    spatial_local = contract_rows(cols_first, grad_conved)
    grad_act_first = columns_back(
        jnp.dot(grad_conved, spatial_weight.T, preferred_element_type=jnp.float32), neck_width
    )
    grad_pre_first = gelu_back(pre_first, grad_act_first)
    shift_first_grad, gain_first_grad = norm_sums(grad_pre_first, normed_first)
    grad_reduced = normalize_back(
        grad_pre_first, normed_first, rstd_first, gain_first, shift_first_grad, gain_first_grad
    ).astype(jnp.bfloat16)
    reduce_local = contract_rows(pixels, grad_reduced)
    canvas_grad = (
        (jnp.dot(grad_reduced, reduce_weight.T, preferred_element_type=jnp.float32) + grad_pre_out)
        .astype(jnp.bfloat16)
        .reshape(canvas.shape)
    )
    proto_part = lax.psum_scatter(proto_local, "in", scatter_dimension=1, tiled=True)
    prototypes_grad = lax.psum(proto_part, "grp")
    embed_grad = lax.psum_scatter(
        lax.psum_scatter(embed_local, "in", scatter_dimension=1, tiled=True),
        "grp",
        scatter_dimension=0,
        tiled=True,
    )
    hidden_grad = scatter_sum(blocked(hidden_local))
    expand_grad = scatter_sum(blocked(expand_local))
    spatial_grad = scatter_sum(blocked(spatial_local))
    reduce_grad = scatter_sum(blocked(reduce_local))
    return (
        crop_loss.reshape(canvases, CROPS),
        canvas_grad,
        reduce_grad,
        spatial_grad,
        expand_grad,
        hidden_grad,
        embed_grad,
        embed_bias_grad,
        prototypes_grad,
        gain_first_grad,
        shift_first_grad,
        gain_second_grad,
        shift_second_grad,
        gain_third_grad,
        shift_third_grad,
        gain_head_grad,
        shift_head_grad,
    )


def fold(value, gain, shift, total, count):
    middle = total[0:1] / count
    rstd = lax.rsqrt(total[1:2] / count - middle * middle + BATCH_EPSILON)
    normed = (value - middle) * rstd
    return normed, rstd, normed * gain + shift


def tanh_part(value):
    return jnp.tanh(ROOT * (value + CUBIC * (value * value * value)))


def gelu_of(value):
    return 0.5 * value * (1.0 + tanh_part(value))


def gelu_slope(value):
    bend = tanh_part(value)
    inner = ROOT * (1.0 + (3.0 * CUBIC) * (value * value))
    return 0.5 * (1.0 + bend) + 0.5 * value * (1.0 - bend * bend) * inner


def dot(left, right, dims=((1,), (0,))):
    return lax.dot_general(left, right, (dims, ((), ())), preferred_element_type=jnp.float32)


def column_sums(first, second):
    return jnp.concatenate(
        [jnp.sum(first, 0, keepdims=True), jnp.sum(second, 0, keepdims=True)], 0
    )


def spread(ref, value):
    ref[...] = jnp.broadcast_to(value[None], ref.shape)


def gathered(ref):
    return jnp.sum(ref[...], 0)


def gathered_pair(mine_ref, other_ref):
    return jnp.sum(mine_ref[...], 0) + jnp.sum(other_ref[...], 0)


def pairs():
    side = SIDE // 2
    for vertical in range(3):
        for lateral in range(3):
            here = []
            there = []
            for i in range(side):
                for j in range(side):
                    k = i + vertical - 1
                    m = j + lateral - 1
                    if 0 <= k < side and 0 <= m < side:
                        here.append(i * side + j)
                        there.append(k * side + m)
            yield 3 * vertical + lateral, here, there


def runs(places):
    out = []
    for place in places:
        if out and out[-1][0] + out[-1][1] == place:
            out[-1][1] += 1
        else:
            out.append([place, 1])
    return out


def take(ref, places, rows):
    parts = [ref[first * rows : (first + size) * rows, :] for first, size in runs(places)]
    return parts[0] if len(parts) == 1 else jnp.concatenate(parts, 0)


def add_rows(ref, places, rows, value):
    start = 0
    for first, size in runs(places):
        ref[first * rows : (first + size) * rows, :] += value[start : start + size * rows, :]
        start += size * rows


def tile_places():
    side = SIDE // 2
    for i in range(side):
        for j in range(side):
            yield i * side + j, [(a * side + i, b * side + j) for a in range(2) for b in range(2)]


def reduce_kernel(canvas_ref, weight_ref, pixels_ref, reduced_ref, sums_ref):
    rows = 4 * canvas_ref.shape[2]
    for place, corners in tile_places():
        pixels_ref[place * rows : (place + 1) * rows, :] = jnp.concatenate(
            [canvas_ref[i, j] for i, j in corners], 0
        )
    reduced = dot(pixels_ref[...], weight_ref[...])
    reduced_ref[...] = reduced
    spread(sums_ref, column_sums(reduced, reduced * reduced))


def spatial_kernel(
    count,
    reduced_ref,
    sums_ref,
    gain_ref,
    shift_ref,
    weight_ref,
    total_ref,
    act_ref,
    wide_ref,
    conved_ref,
    out_ref,
):
    neck = reduced_ref.shape[1]
    rows = reduced_ref.shape[0] // 9
    total = gathered(sums_ref)
    total_ref[...] = total
    pre = fold(reduced_ref[...], gain_ref[...], shift_ref[...], total, count)[2]
    act = gelu_of(pre).astype(jnp.bfloat16)
    act_ref[...] = act
    wide_ref[...] = act.astype(jnp.float32)
    for offset, here, there in sorted(pairs(), key=lambda p: p[0] != 4):
        part = dot(take(act_ref, there, rows), weight_ref[offset * neck : (offset + 1) * neck, :])
        if offset == 4:
            conved_ref[...] = part
        else:
            add_rows(conved_ref, here, rows, part)
    conved = conved_ref[...]
    spread(out_ref, column_sums(conved, conved * conved))


def expand_kernel(
    count, conved_ref, sums_ref, gain_ref, shift_ref, weight_ref, total_ref, act_ref, expanded_ref, out_ref
):
    total = gathered(sums_ref)
    total_ref[...] = total
    pre = fold(conved_ref[...], gain_ref[...], shift_ref[...], total, count)[2]
    act = gelu_of(pre).astype(jnp.bfloat16)
    act_ref[...] = act
    expanded = dot(act, weight_ref[...])
    expanded_ref[...] = expanded
    spread(out_ref, column_sums(expanded, expanded * expanded))


def pool_kernel(
    count,
    expanded_ref,
    mine_ref,
    other_ref,
    gain_ref,
    shift_ref,
    pixels_ref,
    weight_ref,
    total_ref,
    pooled_ref,
    head_ref,
    out_ref,
):
    step = pl.program_id(0)
    rows = expanded_ref.shape[0] // 9
    total = gathered_pair(mine_ref, other_ref)
    total_ref[...] = total
    pooled = None
    for place in range(9):
        block = slice(place * rows, (place + 1) * rows)
        pre = fold(expanded_ref[block, :], gain_ref[...], shift_ref[...], total, count)[2]
        part = gelu_of(pre + pixels_ref[block, :].astype(jnp.float32))
        pooled = part if pooled is None else pooled + part
    pooled = (pooled / 9.0).astype(jnp.bfloat16)
    pooled_ref[...] = pooled.astype(jnp.float32)
    head = dot(pooled, weight_ref[...])

    @pl.when(step == 0)
    def _():
        head_ref[...] = head

    @pl.when(step > 0)
    def _():
        head_ref[...] += head

    @pl.when(step == pl.num_programs(0) - 1)
    def _():
        value = head_ref[...]
        spread(out_ref, column_sums(value, value * value))


def score_kernel(
    count,
    protos,
    head_ref,
    mine_ref,
    other_ref,
    gain_ref,
    shift_ref,
    embed_ref,
    bias_ref,
    proto_ref,
    queued_ref,
    total_ref,
    act_ref,
    embedded_ref,
    scores_ref,
    mass_ref,
    out_ref,
):
    total = gathered_pair(mine_ref, other_ref)
    total_ref[...] = total
    pre = fold(head_ref[...], gain_ref[...], shift_ref[...], total, count)[2]
    act = gelu_of(pre).astype(jnp.bfloat16)
    act_ref[...] = act
    embedded = dot(act, embed_ref[...]) + bias_ref[...]
    embedded_ref[...] = embedded
    rnorm = lax.rsqrt(jnp.sum(embedded * embedded, 1, keepdims=True) + UNIT_EPSILON)
    unit = (embedded * rnorm).astype(jnp.bfloat16)
    crops = unit.shape[0]
    scores = dot(unit, proto_ref[...], ((1,), (1,)))
    scores_ref[...] = scores
    queue = dot(queued_ref[...], proto_ref[...], ((1,), (1,)))
    shape = scores.shape
    inside = lax.broadcasted_iota(jnp.int32, shape, 1) < protos
    mass = jnp.where(inside, jnp.exp(scores / TRANSPORT_SMOOTH), 0.0)
    mass_ref[0:crops, :] = mass
    queue_inside = lax.broadcasted_iota(jnp.int32, queue.shape, 1) < protos
    queue_mass = jnp.where(queue_inside, jnp.exp(queue / TRANSPORT_SMOOTH), 0.0)
    real = queue.shape[0]
    mass_ref[crops:, :] = jnp.zeros((mass_ref.shape[0] - crops, shape[1]), jnp.float32)
    mass_ref[crops : crops + real, :] = queue_mass
    spread(out_ref, jnp.sum(mass, 0, keepdims=True) + jnp.sum(queue_mass, 0, keepdims=True))


def balance(protos, mass, column):
    inside = lax.broadcasted_iota(jnp.int32, column.shape, 1) < protos
    mass = mass / jnp.where(inside, column, 1.0)
    row = jnp.sum(mass, 1, keepdims=True)
    return mass, row


def sweep_kernel(protos, real, mass_ref, mine_ref, other_ref, next_ref, out_ref):
    mass, row = balance(protos, mass_ref[...], gathered_pair(mine_ref, other_ref))
    used = lax.broadcasted_iota(jnp.int32, row.shape, 0) < real
    mass = mass / jnp.where(used, row, 1.0)
    next_ref[...] = mass
    spread(out_ref, jnp.sum(mass, 0, keepdims=True))


def loss_kernel(
    count,
    protos,
    mass_ref,
    mine_ref,
    other_ref,
    here_ref,
    wanted_ref,
    held_ref,
    scores_ref,
    embedded_ref,
    proto_ref,
    act_ref,
    embed_ref,
    head_ref,
    head_total_ref,
    gain_ref,
    shift_ref,
    loss_ref,
    keep_ref,
    send_ref,
    upstream_ref,
    out_ref,
):
    crops = scores_ref.shape[0]
    width = scores_ref.shape[1]
    mass, row = balance(protos, mass_ref[0:crops, :], gathered_pair(mine_ref, other_ref))
    codes = mass / row
    size = crops // CROPS
    row_place = lax.broadcasted_iota(jnp.int32, (crops, crops), 0) % size
    column_place = lax.broadcasted_iota(jnp.int32, (crops, crops), 1) % size
    chosen = (wanted_ref[...] == held_ref[...]) & (row_place == column_place)
    target = lax.dot_general(
        jnp.where(chosen, 1.0, 0.0),
        codes,
        (((1,), (0,)), ((), ())),
        precision=PRECISE,
        preferred_element_type=jnp.float32,
    )
    logits = scores_ref[...] / SOFTMAX_WARMTH
    inside = lax.broadcasted_iota(jnp.int32, logits.shape, 1) < protos
    top = jnp.max(jnp.where(inside, logits, -3.0e38), 1, keepdims=True)
    mass_of = jnp.where(inside, jnp.exp(logits - top), 0.0)
    log_total = jnp.log(jnp.sum(mass_of, 1, keepdims=True)) + top
    loss_ref[...] = -jnp.sum(target * (logits - log_total), 1, keepdims=True)
    share = jnp.sum(target, 1, keepdims=True)
    soft = jnp.where(inside, jnp.exp(logits - log_total), 0.0)
    grad_scores = ((soft * share - target) / SOFTMAX_WARMTH).astype(jnp.bfloat16)
    embedded = embedded_ref[...]
    rnorm = lax.rsqrt(jnp.sum(embedded * embedded, 1, keepdims=True) + UNIT_EPSILON)
    unit = embedded * rnorm
    grad_unit = dot(grad_scores, proto_ref[...])
    grad_embedded = rnorm * (grad_unit - unit * jnp.sum(grad_unit * unit, 1, keepdims=True))
    grad_low = grad_embedded.astype(jnp.bfloat16)
    proto_local = dot(unit.astype(jnp.bfloat16), grad_scores, ((0,), (0,)))
    embed_local = dot(grad_low, act_ref[...], ((0,), (0,)))
    across, outer, rows = keep_ref.shape[:3]
    first = width // outer
    second = embed_local.shape[1] // outer
    flip = here_ref[0] == 1
    for k in range(across):
        lines = [slice((2 * k + c) * rows, (2 * k + c + 1) * rows) for c in range(2)]
        for m in range(outer):
            for value, size, start in ((proto_local, first, 0), (embed_local, second, first)):
                even, odd = (value[line, m * size : (m + 1) * size] for line in lines)
                keep_ref[k, m, :, start : start + size] = jnp.where(flip, odd, even)
                send_ref[k, m, :, start : start + size] = jnp.where(flip, even, odd)
    total = head_total_ref[...]
    normed, _, pre = fold(head_ref[...], gain_ref[...], shift_ref[...], total, count)
    upstream = gelu_slope(pre) * dot(grad_low, embed_ref[...], ((1,), (1,)))
    upstream_ref[...] = upstream
    bias = jnp.sum(grad_embedded, 0, keepdims=True)
    sums = jnp.concatenate([column_sums(upstream, upstream * normed), jnp.concatenate([bias, bias], 0)], 1)
    spread(out_ref, sums)


def split_columns(value, here_ref, near_ref, away_ref):
    part = near_ref.shape[2]
    blocks = [value[:, k * part : (k + 1) * part] for k in range(4)]
    core = here_ref[0] == 1
    chip = here_ref[1] == 1
    for k in range(2):
        first = jnp.where(core, blocks[1 - k], blocks[k])
        second = jnp.where(core, blocks[3 - k], blocks[2 + k])
        near_ref[k] = jnp.where(chip, second, first)
        away_ref[k] = jnp.where(chip, first, second)


def norm_back(upstream, normed, rstd, gain, total, count):
    return gain * rstd * (upstream - total[0:1] / count - normed * (total[1:2] / count))


def head_back_kernel(
    count,
    upstream_ref,
    mine_ref,
    other_ref,
    head_ref,
    head_total_ref,
    gain_ref,
    shift_ref,
    here_ref,
    sums_ref,
    low_ref,
    near_ref,
    away_ref,
):
    total = gathered_pair(mine_ref, other_ref)
    sums_ref[...] = total
    width = head_ref.shape[1]
    stats = head_total_ref[...]
    normed, rstd, _ = fold(head_ref[...], gain_ref[...], shift_ref[...], stats, count)
    grad = norm_back(upstream_ref[...], normed, rstd, gain_ref[...], total[:, 0:width], count)
    low = grad.astype(jnp.bfloat16)
    low_ref[...] = low
    split_columns(grad.astype(jnp.bfloat16).astype(jnp.float32), here_ref, near_ref, away_ref)


def pool_back_kernel(
    count,
    grad_ref,
    weight_ref,
    expanded_ref,
    total_ref,
    gain_ref,
    shift_ref,
    pixels_ref,
    upstream_ref,
    out_ref,
):
    rows = expanded_ref.shape[0] // 9
    total = total_ref[...]
    grad_output = dot(grad_ref[...], weight_ref[...], ((1,), (1,))) / 9.0
    first = None
    second = None
    for place in range(9):
        block = slice(place * rows, (place + 1) * rows)
        normed, _, pre = fold(expanded_ref[block, :], gain_ref[...], shift_ref[...], total, count)
        upstream = gelu_slope(pre + pixels_ref[block, :].astype(jnp.float32)) * grad_output
        upstream_ref[block, :] = upstream
        weighted = upstream * normed
        first = upstream if first is None else first + upstream
        second = weighted if second is None else second + weighted
    spread(out_ref, column_sums(first, second))


def expand_back_kernel(
    count,
    upstream_ref,
    back_mine_ref,
    back_other_ref,
    expanded_ref,
    total_ref,
    gain_ref,
    weight_ref,
    act_ref,
    conved_ref,
    conved_sums_ref,
    conved_gain_ref,
    conved_shift_ref,
    here_ref,
    sums_ref,
    keep_ref,
    send_ref,
    next_ref,
    out_ref,
):
    step = pl.program_id(0)
    back = gathered_pair(back_mine_ref, back_other_ref)
    sums_ref[...] = back
    stats = total_ref[...]
    normed, rstd, _ = fold(expanded_ref[...], gain_ref[...], 0.0, stats, count)
    grad = norm_back(upstream_ref[...], normed, rstd, gain_ref[...], back, count).astype(jnp.bfloat16)
    part = dot(grad, weight_ref[...], ((1,), (1,)))
    value = dot(act_ref[...], grad, ((0,), (0,)))
    half = value.shape[1] // 2
    flip = here_ref[0] == 1
    keep_ref[0] = jnp.where(flip, value[:, half:], value[:, :half])
    send_ref[0] = jnp.where(flip, value[:, :half], value[:, half:])

    @pl.when(step == 0)
    def _():
        next_ref[...] = part

    @pl.when(step > 0)
    def _():
        next_ref[...] += part

    @pl.when(step == pl.num_programs(0) - 1)
    def _():
        conved, _, pre = fold(
            conved_ref[...], conved_gain_ref[...], conved_shift_ref[...], conved_sums_ref[...], count
        )
        upstream = gelu_slope(pre) * next_ref[...]
        next_ref[...] = upstream
        spread(out_ref, column_sums(upstream, upstream * conved))


def spatial_back_kernel(
    count,
    upstream_ref,
    back_ref,
    conved_ref,
    sums_ref,
    gain_ref,
    weight_ref,
    reduced_ref,
    reduced_sums_ref,
    reduced_gain_ref,
    reduced_shift_ref,
    here_ref,
    total_ref,
    near_ref,
    away_ref,
    next_ref,
    out_ref,
    low_ref,
):
    neck = conved_ref.shape[1]
    rows = conved_ref.shape[0] // 9
    back = gathered(back_ref)
    total_ref[...] = back
    normed, rstd, _ = fold(conved_ref[...], gain_ref[...], 0.0, sums_ref[...], count)
    low = norm_back(upstream_ref[...], normed, rstd, gain_ref[...], back, count).astype(jnp.bfloat16)
    low_ref[...] = low
    split_columns(low.astype(jnp.float32), here_ref, near_ref, away_ref)
    for offset, here, there in sorted(pairs(), key=lambda p: p[0] != 4):
        value = dot(
            take(low_ref, here, rows), weight_ref[offset * neck : (offset + 1) * neck, :], ((1,), (1,))
        )
        if offset == 4:
            next_ref[...] = value
        else:
            add_rows(next_ref, there, rows, value)
    reduced, _, pre = fold(
        reduced_ref[...], reduced_gain_ref[...], reduced_shift_ref[...], reduced_sums_ref[...], count
    )
    upstream = gelu_slope(pre) * next_ref[...]
    next_ref[...] = upstream
    spread(out_ref, column_sums(upstream, upstream * reduced))


def spatial_weight_kernel(
    here_ref, act_ref, near_ref, away_ref, core_ref, keep_ref, send_ref, left_ref, right_ref
):
    devices = act_ref.shape[0]
    rows = act_ref.shape[1] // 9
    neck = act_ref.shape[2]
    me = here_ref[0] + 2 * here_ref[1]
    grads = (near_ref, core_ref, away_ref, core_ref)
    for k in range(devices):
        source = me ^ k
        for place in range(9):
            block = slice(place * rows, (place + 1) * rows)
            goal = slice((place * devices + k) * rows, (place * devices + k + 1) * rows)
            left_ref[goal, :] = act_ref[source, block, :].astype(jnp.bfloat16)
            right_ref[goal, :] = grads[k][k // 2 if k % 2 else 0, block, :].astype(jnp.bfloat16)
    size = keep_ref.shape[1]
    mine = here_ref[2]
    for offset, here, there in pairs():
        value = dot(
            take(left_ref, there, rows * devices), take(right_ref, here, rows * devices), ((0,), (0,))
        )
        start = offset * neck
        end = start + neck
        while start < end:
            owner = start // size
            stop = min(end, (owner + 1) * size)
            piece = value[start - offset * neck : stop - offset * neck, :]
            lines = slice(start - owner * size, stop - owner * size)

            @pl.when(mine == owner % 2)
            def _():
                keep_ref[owner // 2, lines, :] = piece

            @pl.when(mine != owner % 2)
            def _():
                send_ref[owner // 2, lines, :] = piece

            start = stop


def hidden_weight_kernel(
    here_ref, pooled_ref, near_ref, y_ref, x_ref, xy_ref, core_ref, *out_refs
):
    rows = near_ref.shape[1]
    size = out_refs[0].shape[0]
    me = here_ref[0] + 2 * here_ref[1] + 4 * here_ref[2]
    places = [(0, near_ref, 0), (4, y_ref, 0), (2, x_ref, 0), (6, xy_ref, 0)]
    places += [(1, core_ref, 0), (5, core_ref, 1), (3, core_ref, 2), (7, core_ref, 3)]
    right = jnp.concatenate([ref[k].astype(jnp.bfloat16) for _, ref, k in places], 0)
    for m, out_ref in enumerate(out_refs):
        start = pl.multiple_of((2 * (here_ref[3] ^ m) + here_ref[2]) * size, size)
        left = jnp.concatenate(
            [pooled_ref[me ^ mask, :, pl.ds(start, size)].astype(jnp.bfloat16) for mask, _, _ in places], 0
        )
        out_ref[...] = dot(left, right, ((0,), (0,)))


def across_kernel(here_ref, keep_ref, come_ref, *out_refs):
    deep = out_refs[0].shape[0]
    for m, out_ref in enumerate(out_refs):
        column = here_ref[1] ^ (m & 1)
        side = here_ref[2] ^ (m >> 1)
        for k in range(deep):
            out_ref[k] = keep_ref[column, 2 * k + side] + come_ref[column, 2 * k + side]


def along_kernel(here_ref, *refs):
    deep = refs[0].shape[0]
    ins, outs = refs[:-deep], refs[-deep:]
    for m, out_ref in enumerate(outs):
        place = here_ref[3] ^ m
        total = ins[0][place]
        for ref in ins[1:]:
            total = total + ref[place]
        out_ref[...] = total


def reduce_back_kernel(
    count,
    upstream_ref,
    back_ref,
    reduced_ref,
    sums_ref,
    gain_ref,
    pixels_ref,
    here_ref,
    total_ref,
    low_ref,
    keep_ref,
    send_ref,
):
    back = gathered(back_ref)
    total_ref[...] = back
    normed, rstd, _ = fold(reduced_ref[...], gain_ref[...], 0.0, sums_ref[...], count)
    low = norm_back(upstream_ref[...], normed, rstd, gain_ref[...], back, count).astype(jnp.bfloat16)
    low_ref[...] = low
    part = keep_ref.shape[2]
    value = dot(pixels_ref[...], low, ((0,), (0,)))
    flip = here_ref[0] == 1
    for k in range(keep_ref.shape[0]):
        even = value[:, 2 * k * part : (2 * k + 1) * part]
        odd = value[:, (2 * k + 1) * part : (2 * k + 2) * part]
        keep_ref[k] = jnp.where(flip, odd, even)
        send_ref[k] = jnp.where(flip, even, odd)


def canvas_kernel(low_ref, weight_ref, upstream_ref, out_ref):
    rows = low_ref.shape[0] // 9
    size = out_ref.shape[2]
    value = (dot(low_ref[...], weight_ref[...], ((1,), (1,))) + upstream_ref[...]).astype(jnp.bfloat16)
    for place, corners in tile_places():
        for k, (i, j) in enumerate(corners):
            start = place * rows + k * size
            out_ref[i, j] = value[start : start + size, :]


SCALARS = pl.BlockSpec(memory_space=pltpu.SMEM)
ARRAY = pl.BlockSpec(memory_space=pltpu.VMEM)


def run(kernel, outs, args, scratch=(), flops=0, moved=0, after=(), **grid):
    if "grid" not in grid:
        kinds = [SCALARS if a.ndim == 1 and a.dtype == jnp.int32 else ARRAY for a in args]
        grid["in_specs"] = kinds
    if len(after) > 0:
        inner = kernel
        count = len(args)
        grid["in_specs"] = list(grid["in_specs"]) + [pl.BlockSpec(memory_space=pl.ANY)] * len(after)
        args = tuple(args) + tuple(after)
        skip = len(after)

        def kernel(*refs):
            inner(*refs[:count], *refs[count + skip :])

    loose = grid.pop("loose", ())
    args = [
        a
        if (a.ndim == 1 and a.dtype == jnp.int32)
        or any(a is other for other in (*loose, *after))
        else pltpu.with_memory_space_constraint(a, pltpu.HBM)
        for a in args
    ]
    outs = jax.tree.map(lambda out: pltpu.HBM(out.shape, out.dtype), outs)
    return pl.pallas_call(
        kernel,
        out_shape=outs,
        scratch_shapes=list(scratch),
        compiler_params=pltpu.CompilerParams(vmem_limit_bytes=VMEM_BYTES),
        cost_estimate=pl.CostEstimate(flops=flops, bytes_accessed=moved, transcendentals=0),
        **grid,
    )(*args)


def f32(*shape):
    return jax.ShapeDtypeStruct(shape, jnp.float32)


def b16(*shape):
    return jax.ShapeDtypeStruct(shape, jnp.bfloat16)


def to_all(block):
    return lax.all_to_all(block, AXES, 0, 0, tiled=True)


def to_all_pair(block):
    count = lax.axis_size("grp") * lax.axis_size("in")
    groups = [list(range(k, count, 2)) for k in range(2)]
    mine = lax.all_to_all(block, AXES, 0, 0, tiled=True, axis_index_groups=groups)
    return mine, swap_bit(mine, 0)


def pick(value, bit, axis=0):
    mine = lax.dynamic_index_in_dim(value, my_bit(bit), axis, keepdims=False)
    other = lax.dynamic_index_in_dim(value, 1 - my_bit(bit), axis, keepdims=False)
    return mine, other


def teams(bits):
    count = lax.axis_size("grp") * lax.axis_size("in")
    spans = [0]
    for bit in bits:
        spans = spans + [m | (1 << bit) for m in spans]
    used = sum(1 << bit for bit in bits)
    return [[base | m for m in sorted(spans)] for base in range(count) if base & used == 0]


def swap_mask(value, mask):
    count = lax.axis_size("grp") * lax.axis_size("in")
    return lax.ppermute(value, AXES, [(i, i ^ mask) for i in range(count)])


def spread_plane(here, keep, come):
    deep = keep.shape[1] // 2
    parts = run(across_kernel, (f32(deep, *keep.shape[2:]),) * 4, (here, keep, come), moved=4 * keep.size * 3, loose=(come,))
    return [parts[0]] + [
        swap_mask(pltpu.with_memory_space_constraint(parts[m], pltpu.HBM), 2 * m) for m in range(1, 4)
    ]


def spread_line(here, parts):
    deep = parts[0].shape[0]
    shape = parts[0].shape[1:]
    cut = run(
        along_kernel,
        (f32(*shape),) * deep,
        (here, *parts),
        moved=4 * parts[0].size * (len(parts) + 1),
        loose=parts[1:],
    )
    return [cut[0]] + [swap_mask(cut[m], 8 * m) for m in range(1, deep)]


def total_of(parts):
    value = parts[0]
    for part in parts[1:]:
        value = value + part
    return value


def fast(
    canvas,
    reduce_weight,
    gain_first,
    shift_first,
    spatial_weight,
    gain_second,
    shift_second,
    expand_weight,
    gain_third,
    shift_third,
    hidden_weight,
    gain_head,
    shift_head,
    embed_weight,
    embed_bias,
    prototypes,
    queued,
    crop_ids,
    partner,
):
    inner = lax.axis_size("in")
    outer = lax.axis_size("grp")
    devices = inner * outer
    low_bits = bits_of("in")
    canvases = canvas.shape[0]
    channels = canvas.shape[-1]
    neck = reduce_weight.shape[1]
    hidden = hidden_weight.shape[1]
    width = embed_weight.shape[1]
    rows = canvases * SIDE * SIDE
    crops = canvases * CROPS
    protos = prototypes.shape[0]
    wide = -(-protos // (128 * outer)) * 128 * outer
    count = float(rows * devices)
    crop_count = float(crops * devices)
    gain_first, shift_first, gain_second, shift_second = (
        v.reshape(1, -1) for v in (gain_first, shift_first, gain_second, shift_second)
    )
    gain_third, shift_third, gain_head, shift_head, embed_bias = (
        v.reshape(1, -1) for v in (gain_third, shift_third, gain_head, shift_head, embed_bias)
    )
    proto_wide = jnp.pad(prototypes, ((0, wide - protos), (0, 0)))
    field = canvas.transpose(1, 2, 0, 3)

    index = lax.axis_index("grp") * inner + lax.axis_index("in")
    here = jnp.stack([index & 1, (index >> 1) & 1, (index >> 2) & 1, index >> 3]).astype(jnp.int32)
    quadrants = crop_ids[:, :: SIDE // 2, :: SIDE // 2].reshape(canvases, CROPS).T
    wanted = jnp.sum(
        (quadrants[:, None, :] == jnp.arange(CROPS, dtype=jnp.int32)[None, :, None])
        * partner.T[None, :, :],
        1,
    ).reshape(crops, 1)
    held = quadrants.reshape(1, crops)

    pixels, reduced, sums = run(
        reduce_kernel,
        (b16(rows, channels), f32(rows, neck), f32(devices, 2, neck)),
        (field, reduce_weight),
        flops=2 * rows * channels * neck,
        moved=12_000_000,
    )
    first_sums = to_all(sums)
    first_total, act_first, act_wide, conved, sums = run(
        functools.partial(spatial_kernel, count),
        (f32(2, neck), b16(rows, neck), f32(rows, neck), f32(rows, neck), f32(devices, 2, neck)),
        (reduced, first_sums, gain_first, shift_first, spatial_weight),
        loose=(first_sums,),
        flops=11 * rows * neck * neck,
        moved=12_000_000,
    )
    act_all = lax.all_gather(act_wide, "in")
    second_sums = to_all(sums)
    second_total, act_second, expanded, sums = run(
        functools.partial(expand_kernel, count),
        (f32(2, neck), b16(rows, neck), f32(rows, channels), f32(devices // 2, 2, channels)),
        (conved, second_sums, gain_second, shift_second, expand_weight),
        loose=(second_sums,),
        flops=2 * rows * channels * neck,
        moved=12_000_000,
    )
    third_mine, third_other = to_all_pair(sums)
    block = channels // outer
    chunk = 2 * block
    chunks = channels // chunk
    columns = lambda n: pl.BlockSpec((n, chunk), lambda k: (0, k))
    stats = lambda n: pl.BlockSpec((n, 2, chunk), lambda k: (0, 0, k))
    whole = lambda *shape: pl.BlockSpec(shape, lambda k: (0,) * len(shape))
    third_total, pooled, head_pre, sums = run(
        functools.partial(pool_kernel, count),
        (f32(2, channels), f32(crops, channels), f32(crops, hidden), f32(devices // 2, 2, hidden)),
        (expanded, third_mine, third_other, gain_third, shift_third, pixels, hidden_weight),
        loose=(third_mine, third_other),
        flops=2 * crops * channels * hidden,
        moved=18_000_000,
        grid=(chunks,),
        in_specs=[
            columns(rows),
            stats(devices // 2),
            stats(devices // 2),
            columns(1),
            columns(1),
            columns(rows),
            pl.BlockSpec((chunk, hidden), lambda k: (k, 0)),
        ],
        out_specs=[
            columns(2),
            columns(crops),
            whole(crops, hidden),
            whole(devices // 2, 2, hidden),
        ],
    )
    pooled_all = lax.all_gather(pooled, AXES, axis_index_groups=teams(range(low_bits + 1)))
    head_mine, head_other = to_all_pair(sums)
    real = crops + queued.shape[0]
    mass_rows = -(-real // 8) * 8
    head_total, act_head, embedded, scores, mass, sums = run(
        functools.partial(score_kernel, crop_count, protos),
        (
            f32(2, hidden),
            b16(crops, hidden),
            f32(crops, width),
            f32(crops, wide),
            f32(mass_rows, wide),
            f32(devices // 2, 1, wide),
        ),
        (
            head_pre,
            head_mine,
            head_other,
            gain_head,
            shift_head,
            embed_weight,
            embed_bias,
            proto_wide,
            queued,
        ),
        loose=(head_mine, head_other),
        flops=2 * crops * width * (hidden + wide),
        moved=6_000_000,
    )
    for _ in range(ITERS - 1):
        column_mine, column_other = to_all_pair(sums)
        mass, sums = run(
            functools.partial(sweep_kernel, protos, real),
            (f32(mass_rows, wide), f32(devices // 2, 1, wide)),
            (mass, column_mine, column_other),
            loose=(column_mine, column_other),
            moved=3_000_000,
        )
    column_mine, column_other = to_all_pair(sums)
    loss, small_keep, small_send, upstream, sums = run(
        functools.partial(loss_kernel, crop_count, protos),
        (
            f32(crops, 1),
            f32(inner // 2, outer, width // inner, (wide + hidden) // outer),
            f32(inner // 2, outer, width // inner, (wide + hidden) // outer),
            f32(crops, hidden),
            f32(devices // 2, 2, hidden + width),
        ),
        (
            mass,
            column_mine,
            column_other,
            here,
            wanted,
            held,
            scores,
            embedded,
            proto_wide,
            act_head,
            embed_weight,
            head_pre,
            head_total,
            gain_head,
            shift_head,
        ),
        loose=(column_mine, column_other),
        flops=6 * crops * width * (hidden + wide),
        moved=9_000_000,
    )
    back_mine, back_other = to_all_pair(sums)
    small = spread_plane(here, small_keep, swap_mask(small_send, 1))
    head_sums, grad_head, head_near, head_away = run(
        functools.partial(head_back_kernel, crop_count),
        (
            f32(2, hidden + width),
            b16(crops, hidden),
            f32(2, crops, hidden // inner),
            f32(2, crops, hidden // inner),
        ),
        (upstream, back_mine, back_other, head_pre, head_total, gain_head, shift_head, here),
        loose=(back_mine, back_other),
        moved=3_000_000,
    )
    moved = [head_near] + [
        swap_mask(part, mask) for part, mask in ((head_near, 4), (head_away, 2), (head_away, 6))
    ]
    grad_pre_out, sums = run(
        functools.partial(pool_back_kernel, count),
        (f32(rows, channels), f32(devices // 2, 2, channels)),
        (
            grad_head,
            hidden_weight,
            expanded,
            third_total,
            gain_third,
            shift_third,
            pixels,
        ),
        flops=2 * crops * channels * hidden,
        moved=24_000_000,
        after=(small[0],),
        grid=(chunks,),
        in_specs=[
            whole(crops, hidden),
            pl.BlockSpec((chunk, hidden), lambda k: (k, 0)),
            columns(rows),
            columns(2),
            columns(1),
            columns(1),
            columns(rows),
        ],
        out_specs=[columns(rows), stats(devices // 2)],
    )
    back_mine, back_other = to_all_pair(sums)
    part = channels // inner
    columns = lambda n: pl.BlockSpec((n, 2 * part), lambda k: (0, k))
    stats = lambda n: pl.BlockSpec((n, 2, 2 * part), lambda k: (0, 0, k))
    def joined(keep, send, size):
        shape = (inner // 2, outer, size // outer, -1)
        return keep.reshape(shape), swap_mask(send, 1).reshape(shape)

    third_back, expand_keep, expand_send, upstream, sums = run(
        functools.partial(expand_back_kernel, count),
        (
            f32(2, channels),
            f32(inner // 2, neck, part),
            f32(inner // 2, neck, part),
            f32(rows, neck),
            f32(devices, 2, neck),
        ),
        (
            grad_pre_out,
            back_mine,
            back_other,
            expanded,
            third_total,
            gain_third,
            expand_weight,
            act_second,
            conved,
            second_total,
            gain_second,
            shift_second,
            here,
        ),
        flops=4 * rows * channels * neck,
        moved=22_000_000,
        loose=(back_mine, back_other),
        after=small[1:] + moved[1:],
        grid=(inner // 2,),
        in_specs=[
            columns(rows),
            stats(devices // 2),
            stats(devices // 2),
            columns(rows),
            columns(2),
            columns(1),
            columns(neck),
            whole(rows, neck),
            whole(rows, neck),
            whole(2, neck),
            whole(1, neck),
            whole(1, neck),
            SCALARS,
        ],
        out_specs=[
            columns(2),
            pl.BlockSpec((1, neck, part), lambda k: (k, 0, 0)),
            pl.BlockSpec((1, neck, part), lambda k: (k, 0, 0)),
            whole(rows, neck),
            whole(devices, 2, neck),
        ],
    )
    back = to_all(sums)
    small = spread_line(here, small)
    core = swap_mask(jnp.stack([part[1] for part in moved]), 1)
    hidden_parts = run(
        hidden_weight_kernel,
        (f32(channels // outer, hidden // inner),) * (outer // 2),
        (here, pooled_all, *moved, core),
        loose=(*moved[1:], core),
        flops=crops * 2 * inner * channels * hidden // inner,
        moved=7_000_000,
    )
    expand_parts = spread_plane(here, *joined(expand_keep, expand_send, neck))
    second_back, conved_near, conved_away, upstream, sums = run(
        functools.partial(spatial_back_kernel, count),
        (
            f32(2, neck),
            f32(2, rows, neck // inner),
            f32(2, rows, neck // inner),
            f32(rows, neck),
            f32(devices, 2, neck),
        ),
        (
            upstream,
            back,
            conved,
            second_total,
            gain_second,
            spatial_weight,
            reduced,
            first_total,
            gain_first,
            shift_first,
            here,
        ),
        scratch=[pltpu.VMEM((rows, neck), jnp.bfloat16)],
        flops=11 * rows * neck * neck,
        moved=14_000_000,
        loose=(back,),
        after=(small[0], hidden_parts[0], expand_parts[0]),
    )
    back = to_all(sums)
    small = total_of(small)
    hidden_grad = total_of(
        [hidden_parts[0]] + [swap_mask(hidden_parts[m], 8 * m) for m in range(1, outer // 2)]
    )
    away = swap_mask(conved_away, 2)
    core = swap_mask(jnp.stack([conved_near[1], away[1]]), 1)
    first_back, grad_reduced, reduce_keep, reduce_send = run(
        functools.partial(reduce_back_kernel, count),
        (
            f32(2, neck),
            b16(rows, neck),
            f32(inner // 2, channels, neck // inner),
            f32(inner // 2, channels, neck // inner),
        ),
        (upstream, back, reduced, first_total, gain_first, pixels, here),
        loose=(back,),
        flops=2 * rows * channels * neck,
        moved=12_000_000,
        after=expand_parts[1:] + [small],
    )
    canvas_grad = run(
        canvas_kernel,
        b16(SIDE, SIDE, canvases, channels),
        (grad_reduced, reduce_weight, grad_pre_out),
        flops=2 * rows * channels * neck,
        moved=15_000_000,
    ).transpose(2, 0, 1, 3)

    first = wide // outer
    embed_grad = small[:, first:].T
    sent = jnp.broadcast_to(small[None, :, :first], (outer, width // inner, first))
    sent = lax.all_to_all(sent, "grp", 0, 0, tiled=True)
    prototypes_grad = sent.transpose(1, 0, 2).reshape(width // inner, wide)[:, :protos].T
    spatial_keep, spatial_send = run(
        spatial_weight_kernel,
        (f32(outer // 2, 9 * neck // outer, neck // inner),) * 2,
        (here, act_all, conved_near, away, core),
        loose=(away, core),
        scratch=[
            pltpu.VMEM((rows * inner, neck), jnp.bfloat16),
            pltpu.VMEM((rows * inner, neck // inner), jnp.bfloat16),
        ],
        flops=11 * rows * neck * neck,
        moved=10_000_000,
    )
    spatial_grad = total_of(spread_line(here, [spatial_keep, swap_mask(spatial_send, 4)]))
    expand_grad = total_of(spread_line(here, expand_parts))
    reduce_grad = total_of(spread_line(here, spread_plane(here, *joined(reduce_keep, reduce_send, channels))))
    ids = jnp.arange(CROPS, dtype=jnp.int32)
    crop_loss = jnp.sum(
        (quadrants.T[:, None, :] == ids[None, :, None]) * loss.reshape(CROPS, canvases).T[:, None, :], 2
    )
    return (
        crop_loss,
        canvas_grad,
        reduce_grad,
        spatial_grad,
        expand_grad,
        hidden_grad,
        embed_grad,
        head_sums[0, hidden:],
        prototypes_grad,
        first_back[1],
        first_back[0],
        second_back[1],
        second_back[0],
        third_back[1],
        third_back[0],
        head_sums[1, :hidden],
        head_sums[0, :hidden],
    )


def solution(mesh):
    placed = (
        P(("grp", "in"), None, None, None),
        P(),
        P(),
        P(),
        P(),
        P(),
        P(),
        P(),
        P(),
        P(),
        P(),
        P(),
        P(),
        P(),
        P(),
        P(),
        P(("grp", "in"), None),
        P(("grp", "in"), None, None),
        P(("grp", "in"), None),
    )
    lanes = 128 * mesh.shape["grp"]
    aligned = mesh.shape["in"] * 128 <= 512 and lanes * 2 <= 2048
    return jax.shard_map(
        fast if aligned else on_device,
        mesh=mesh,
        in_specs=placed,
        out_specs=(
            P(("grp", "in"), None),
            P(("grp", "in"), None, None, None),
            P("grp", "in"),
            P("grp", "in"),
            P("grp", "in"),
            P("grp", "in"),
            P("grp", "in"),
            P(),
            P(None, "in"),
            P(),
            P(),
            P(),
            P(),
            P(),
            P(),
            P(),
            P(),
        ),
        check_vma=False,
    )
```

```python
import functools

import jax
import jax.numpy as jnp
from jax import lax
from jax.experimental import pallas as pl
from jax.experimental.pallas import tpu as pltpu
from jax.sharding import PartitionSpec as P

SIDE = 6
CROPS = 4
ITERS = 3


BATCH_EPSILON = 1e-05
UNIT_EPSILON = 1e-06
SOFTMAX_WARMTH = 0.1
TRANSPORT_SMOOTH = 0.05
PRECISE = lax.Precision.HIGHEST
ROOT = 0.7978845608028654
CUBIC = 0.044715
VMEM_BYTES = 48 * 1024 * 1024


AXES = ("grp", "in")


def bits_of(axis):
    return lax.axis_size(axis).bit_length() - 1


def swap_bit(value, bit):
    count = lax.axis_size("grp") * lax.axis_size("in")
    return lax.ppermute(value, AXES, [(i, i ^ (1 << bit)) for i in range(count)])


def my_bit(bit):
    index = lax.axis_index("grp") * lax.axis_size("in") + lax.axis_index("in")
    return (index >> bit) & 1


def exchange_sum(block, groups):
    size = len(groups[0])
    spread = jnp.broadcast_to(block[None], (size,) + block.shape)
    moved = lax.all_to_all(spread, AXES, 0, 0, tiled=True, axis_index_groups=groups)
    return jnp.sum(moved, 0)


def all_sum(parts):
    count = lax.axis_size("grp") * lax.axis_size("in")
    sizes = [part.size for part in parts]
    flat = jnp.concatenate([part.reshape(-1) for part in parts])
    total = sum(sizes)
    small = total <= 1536
    unit = 1024 if small else 2048
    rows = -(-total // unit) * unit // 128
    flat = jnp.pad(flat, (0, rows * 128 - total)).reshape(rows, 128)
    if small:
        flat = exchange_sum(flat, [list(range(count))])
    else:
        core = my_bit(0)
        halves = flat.reshape(2, rows // 2, 128)
        mine = lax.dynamic_index_in_dim(halves, core, 0, keepdims=False)
        other = lax.dynamic_index_in_dim(halves, 1 - core, 0, keepdims=False)
        mine = mine + swap_bit(other, 0)
        mine = exchange_sum(mine, [list(range(k, count, 2)) for k in range(2)])
        other = swap_bit(mine, 0)
        flat = jnp.concatenate(
            [jnp.where(core == 0, mine, other), jnp.where(core == 0, other, mine)], 0
        )
    flat = flat.reshape(-1)
    sums = []
    start = 0
    for part, size in zip(parts, sizes):
        sums.append(flat[start : start + size].reshape(part.shape))
        start += size
    return sums


def scatter_sum(blocks, splits=2):
    low = bits_of("in")
    high = bits_of("grp")
    count = low + high
    rows = blocks.shape[2]
    columns = blocks.shape[3]
    inner = list(range(low))
    outer = list(range(low, count))
    orders = [inner + outer, inner[:1] + outer + inner[1:]][:splits]
    chunks = []
    for k, order in enumerate(orders):
        piece = blocks[:, :, k * (rows // splits) : (k + 1) * (rows // splits)]
        chunks.append((piece.reshape((2,) * count + (rows // splits, columns)), order))
    left = [list(inner[::-1] + outer[::-1]) for _ in orders]
    for stage in range(count):
        following = []
        for k, (piece, order) in enumerate(chunks):
            bit = order[stage]
            place = left[k].index(bit)
            left[k].remove(bit)
            mine = lax.dynamic_index_in_dim(piece, my_bit(bit), place, keepdims=False)
            other = lax.dynamic_index_in_dim(piece, 1 - my_bit(bit), place, keepdims=False)
            following.append((mine + swap_bit(other, bit), order))
        chunks = following
    return jnp.concatenate([piece for piece, _ in chunks], 0)


def blocked(grad):
    rows, columns = grad.shape
    inner = lax.axis_size("in")
    outer = lax.axis_size("grp")
    return grad.reshape(outer, rows // outer, inner, columns // inner).transpose(2, 0, 1, 3)


def contract_rows(left, right):
    return lax.dot_general(
        left, right, (((0,), (0,)), ((), ())), preferred_element_type=jnp.float32
    )


def gelu_back(before, upstream):
    ignored, backward = jax.vjp(jax.nn.gelu, before)
    return backward(upstream)[0]


def normalize(value, gain, shift):
    count = value.shape[0] * lax.axis_size("grp") * lax.axis_size("in")
    total, squares = all_sum((jnp.sum(value, 0), jnp.sum(value * value, 0)))
    middle = total / count
    rstd = lax.rsqrt(squares / count - middle * middle + BATCH_EPSILON)
    normed = (value - middle) * rstd
    return (normed, rstd, normed * gain + shift)


def norm_sums(upstream, normed):
    return all_sum((jnp.sum(upstream, 0), jnp.sum(upstream * normed, 0)))


def normalize_back(upstream, normed, rstd, gain, shift_sum, gain_sum):
    count = normed.shape[0] * lax.axis_size("grp") * lax.axis_size("in")
    return gain * rstd * (upstream - shift_sum / count - normed * gain_sum / count)


def tile_mask(vertical, lateral):
    tile_side = SIDE // 2
    position = jnp.arange(SIDE, dtype=jnp.int32) % tile_side
    row_valid = ((position + vertical - 1 >= 0) & (position + vertical - 1 < tile_side)).astype(
        jnp.float32
    )
    column_valid = ((position + lateral - 1 >= 0) & (position + lateral - 1 < tile_side)).astype(
        jnp.float32
    )
    return row_valid[:, None] * column_valid[None, :]


def columns(field, neck_width):
    canvas_grid = field.reshape(-1, SIDE, SIDE, neck_width)
    padded = jnp.pad(canvas_grid, ((0, 0), (1, 1), (1, 1), (0, 0)))
    windows = [
        padded[:, vertical : vertical + SIDE, lateral : lateral + SIDE, :]
        * tile_mask(vertical, lateral).astype(field.dtype)[None, :, :, None]
        for vertical in range(3)
        for lateral in range(3)
    ]
    return jnp.concatenate(windows, axis=-1).reshape(-1, 9 * neck_width)


def columns_back(grad_cols, neck_width):
    canvas_grid = grad_cols.reshape(-1, SIDE, SIDE, 9, neck_width)
    padded = jnp.zeros((canvas_grid.shape[0], SIDE + 2, SIDE + 2, neck_width), jnp.float32)
    for window in range(9):
        vertical = window // 3
        lateral = window % 3
        masked = canvas_grid[:, :, :, window, :] * tile_mask(vertical, lateral)[None, :, :, None]
        padded = padded.at[:, vertical : vertical + SIDE, lateral : lateral + SIDE, :].add(masked)
    return padded[:, 1:-1, 1:-1, :].reshape(-1, neck_width)


def normalize_rows(embedded):
    return embedded * lax.rsqrt(jnp.sum(embedded * embedded, axis=1, keepdims=True) + UNIT_EPSILON)


def on_device(
    canvas,
    reduce_weight,
    gain_first,
    shift_first,
    spatial_weight,
    gain_second,
    shift_second,
    expand_weight,
    gain_third,
    shift_third,
    hidden_weight,
    gain_head,
    shift_head,
    embed_weight,
    embed_bias,
    prototypes,
    queued,
    crop_ids,
    partner,
):
    canvases = canvas.shape[0]
    channels = canvas.shape[-1]
    neck_width = reduce_weight.shape[1]
    pixels = canvas.reshape(-1, channels)
    reduced = jnp.dot(pixels, reduce_weight, preferred_element_type=jnp.float32)
    normed_first, rstd_first, pre_first = normalize(reduced, gain_first, shift_first)
    act_first = jax.nn.gelu(pre_first).astype(jnp.bfloat16)
    cols_first = columns(act_first, neck_width)
    conved = jnp.dot(cols_first, spatial_weight, preferred_element_type=jnp.float32)
    normed_second, rstd_second, pre_second = normalize(conved, gain_second, shift_second)
    act_second = jax.nn.gelu(pre_second).astype(jnp.bfloat16)
    expanded = jnp.dot(act_second, expand_weight, preferred_element_type=jnp.float32)
    normed_third, rstd_third, pre_third = normalize(expanded, gain_third, shift_third)
    pre_out = pre_third + pixels.astype(jnp.float32)
    output = jax.nn.gelu(pre_out)
    member = (
        crop_ids.reshape(canvases, SIDE * SIDE, 1)
        == jnp.arange(CROPS, dtype=jnp.int32)[None, None, :]
    ).astype(jnp.float32)
    counts = jnp.sum(member, axis=1)[:, :, None]
    pooled = (
        jnp.einsum(
            "cpk,cpd->ckd",
            member,
            output.reshape(canvases, SIDE * SIDE, channels),
            precision=PRECISE,
        )
        / counts
    )
    pooled_low = pooled.reshape(-1, channels).astype(jnp.bfloat16)
    head_pre = jnp.dot(pooled_low, hidden_weight, preferred_element_type=jnp.float32)
    normed_head, rstd_head, pre_head = normalize(head_pre, gain_head, shift_head)
    act_head = jax.nn.gelu(pre_head).astype(jnp.bfloat16)
    embedded = jnp.dot(act_head, embed_weight, preferred_element_type=jnp.float32) + embed_bias
    normalized_features, unit_back = jax.vjp(normalize_rows, embedded)
    unit_low = normalized_features.astype(jnp.bfloat16)
    similarity_matrix = jnp.dot(unit_low, prototypes.T, preferred_element_type=jnp.float32)
    queue_similarity = jnp.dot(queued, prototypes.T, preferred_element_type=jnp.float32)
    crop_probability = jnp.exp(similarity_matrix / TRANSPORT_SMOOTH)
    queue_probability = jnp.exp(queue_similarity / TRANSPORT_SMOOTH)
    for sweep_index in range(ITERS):
        column = all_sum(
            (jnp.sum(crop_probability, 0) + jnp.sum(queue_probability, 0),)
        )[0]
        crop_probability = crop_probability / column
        queue_probability = queue_probability / column
        crop_probability = crop_probability / jnp.sum(crop_probability, axis=1, keepdims=True)
        queue_probability = queue_probability / jnp.sum(queue_probability, axis=1, keepdims=True)
    select = (partner[:, :, None] == jnp.arange(CROPS, dtype=jnp.int32)[None, None, :]).astype(
        jnp.float32
    )
    target = jnp.einsum(
        "cjk,ckp->cjp", select, crop_probability.reshape(canvases, CROPS, -1), precision=PRECISE
    ).reshape(-1, crop_probability.shape[1])
    scaled_similarity = similarity_matrix / SOFTMAX_WARMTH
    log_total = jax.nn.logsumexp(scaled_similarity, axis=1, keepdims=True)
    crop_loss = -jnp.sum(target * (scaled_similarity - log_total), axis=1)
    grad_scores = (
        (jnp.exp(scaled_similarity - log_total) * jnp.sum(target, axis=1, keepdims=True) - target)
        / SOFTMAX_WARMTH
    ).astype(jnp.bfloat16)
    grad_unit = jnp.dot(grad_scores, prototypes, preferred_element_type=jnp.float32)
    proto_local = contract_rows(grad_scores, unit_low)
    grad_embedded = unit_back(grad_unit)[0]
    grad_embedded_low = grad_embedded.astype(jnp.bfloat16)
    embed_local = contract_rows(act_head, grad_embedded_low)
    grad_act_head = jnp.dot(grad_embedded_low, embed_weight.T, preferred_element_type=jnp.float32)
    grad_pre_head = gelu_back(pre_head, grad_act_head)
    shift_head_grad, gain_head_grad, embed_bias_grad = all_sum(
        (
            jnp.sum(grad_pre_head, 0),
            jnp.sum(grad_pre_head * normed_head, 0),
            jnp.sum(grad_embedded, 0),
        )
    )
    grad_head = normalize_back(
        grad_pre_head, normed_head, rstd_head, gain_head, shift_head_grad, gain_head_grad
    ).astype(jnp.bfloat16)
    hidden_local = contract_rows(pooled_low, grad_head)
    grad_pooled = jnp.dot(grad_head, hidden_weight.T, preferred_element_type=jnp.float32)
    grad_output = jnp.einsum(
        "cpk,ckd->cpd",
        member,
        grad_pooled.reshape(canvases, CROPS, channels) / counts,
        precision=PRECISE,
    ).reshape(-1, channels)
    grad_pre_out = gelu_back(pre_out, grad_output)
    shift_third_grad, gain_third_grad = norm_sums(grad_pre_out, normed_third)
    grad_expanded = normalize_back(
        grad_pre_out, normed_third, rstd_third, gain_third, shift_third_grad, gain_third_grad
    ).astype(jnp.bfloat16)
    expand_local = contract_rows(act_second, grad_expanded)
    grad_pre_second = gelu_back(
        pre_second, jnp.dot(grad_expanded, expand_weight.T, preferred_element_type=jnp.float32)
    )
    shift_second_grad, gain_second_grad = norm_sums(grad_pre_second, normed_second)
    grad_conved = normalize_back(
        grad_pre_second,
        normed_second,
        rstd_second,
        gain_second,
        shift_second_grad,
        gain_second_grad,
    ).astype(jnp.bfloat16)
    spatial_local = contract_rows(cols_first, grad_conved)
    grad_act_first = columns_back(
        jnp.dot(grad_conved, spatial_weight.T, preferred_element_type=jnp.float32), neck_width
    )
    grad_pre_first = gelu_back(pre_first, grad_act_first)
    shift_first_grad, gain_first_grad = norm_sums(grad_pre_first, normed_first)
    grad_reduced = normalize_back(
        grad_pre_first, normed_first, rstd_first, gain_first, shift_first_grad, gain_first_grad
    ).astype(jnp.bfloat16)
    reduce_local = contract_rows(pixels, grad_reduced)
    canvas_grad = (
        (jnp.dot(grad_reduced, reduce_weight.T, preferred_element_type=jnp.float32) + grad_pre_out)
        .astype(jnp.bfloat16)
        .reshape(canvas.shape)
    )
    proto_part = lax.psum_scatter(proto_local, "in", scatter_dimension=1, tiled=True)
    prototypes_grad = lax.psum(proto_part, "grp")
    embed_grad = lax.psum_scatter(
        lax.psum_scatter(embed_local, "in", scatter_dimension=1, tiled=True),
        "grp",
        scatter_dimension=0,
        tiled=True,
    )
    hidden_grad = scatter_sum(blocked(hidden_local))
    expand_grad = scatter_sum(blocked(expand_local))
    spatial_grad = scatter_sum(blocked(spatial_local))
    reduce_grad = scatter_sum(blocked(reduce_local))
    return (
        crop_loss.reshape(canvases, CROPS),
        canvas_grad,
        reduce_grad,
        spatial_grad,
        expand_grad,
        hidden_grad,
        embed_grad,
        embed_bias_grad,
        prototypes_grad,
        gain_first_grad,
        shift_first_grad,
        gain_second_grad,
        shift_second_grad,
        gain_third_grad,
        shift_third_grad,
        gain_head_grad,
        shift_head_grad,
    )


def fold(value, gain, shift, total, count):
    middle = total[0:1] / count
    rstd = lax.rsqrt(total[1:2] / count - middle * middle + BATCH_EPSILON)
    normed = (value - middle) * rstd
    return normed, rstd, normed * gain + shift


def tanh_part(value):
    return jnp.tanh(ROOT * (value + CUBIC * (value * value * value)))


def gelu_of(value):
    return 0.5 * value * (1.0 + tanh_part(value))


def gelu_slope(value):
    bend = tanh_part(value)
    inner = ROOT * (1.0 + (3.0 * CUBIC) * (value * value))
    return 0.5 * (1.0 + bend) + 0.5 * value * (1.0 - bend * bend) * inner


def dot(left, right, dims=((1,), (0,))):
    return lax.dot_general(left, right, (dims, ((), ())), preferred_element_type=jnp.float32)


def column_sums(first, second):
    return jnp.concatenate(
        [jnp.sum(first, 0, keepdims=True), jnp.sum(second, 0, keepdims=True)], 0
    )


def spread(ref, value):
    ref[...] = jnp.broadcast_to(value[None], ref.shape)


def gathered(ref):
    return jnp.sum(ref[...], 0)


def gathered_pair(mine_ref, other_ref):
    return jnp.sum(mine_ref[...], 0) + jnp.sum(other_ref[...], 0)


def pairs():
    side = SIDE // 2
    for vertical in range(3):
        for lateral in range(3):
            here = []
            there = []
            for i in range(side):
                for j in range(side):
                    k = i + vertical - 1
                    m = j + lateral - 1
                    if 0 <= k < side and 0 <= m < side:
                        here.append(i * side + j)
                        there.append(k * side + m)
            yield 3 * vertical + lateral, here, there


def runs(places):
    out = []
    for place in places:
        if out and out[-1][0] + out[-1][1] == place:
            out[-1][1] += 1
        else:
            out.append([place, 1])
    return out


def take(ref, places, rows):
    parts = [ref[first * rows : (first + size) * rows, :] for first, size in runs(places)]
    return parts[0] if len(parts) == 1 else jnp.concatenate(parts, 0)


def add_rows(ref, places, rows, value):
    start = 0
    for first, size in runs(places):
        ref[first * rows : (first + size) * rows, :] += value[start : start + size * rows, :]
        start += size * rows


def tile_places():
    side = SIDE // 2
    for i in range(side):
        for j in range(side):
            yield i * side + j, [(a * side + i, b * side + j) for a in range(2) for b in range(2)]


def reduce_kernel(canvas_ref, weight_ref, pixels_ref, reduced_ref, sums_ref):
    rows = 4 * canvas_ref.shape[2]
    for place, corners in tile_places():
        pixels_ref[place * rows : (place + 1) * rows, :] = jnp.concatenate(
            [canvas_ref[i, j] for i, j in corners], 0
        )
    reduced = dot(pixels_ref[...], weight_ref[...])
    reduced_ref[...] = reduced
    spread(sums_ref, column_sums(reduced, reduced * reduced))


def spatial_kernel(
    count,
    reduced_ref,
    sums_ref,
    gain_ref,
    shift_ref,
    weight_ref,
    total_ref,
    wide_ref,
    conved_ref,
    out_ref,
    act_ref,
):
    neck = reduced_ref.shape[1]
    rows = reduced_ref.shape[0] // 9
    total = gathered(sums_ref)
    total_ref[...] = total
    pre = fold(reduced_ref[...], gain_ref[...], shift_ref[...], total, count)[2]
    act = gelu_of(pre).astype(jnp.bfloat16)
    act_ref[...] = act
    wide_ref[...] = act.astype(jnp.float32)
    for offset, here, there in sorted(pairs(), key=lambda p: p[0] != 4):
        part = dot(take(act_ref, there, rows), weight_ref[offset * neck : (offset + 1) * neck, :])
        if offset == 4:
            conved_ref[...] = part
        else:
            add_rows(conved_ref, here, rows, part)
    conved = conved_ref[...]
    spread(out_ref, column_sums(conved, conved * conved))


def expand_kernel(
    count, conved_ref, sums_ref, gain_ref, shift_ref, weight_ref, total_ref, act_ref, expanded_ref, out_ref
):
    total = gathered(sums_ref)
    total_ref[...] = total
    pre = fold(conved_ref[...], gain_ref[...], shift_ref[...], total, count)[2]
    act = gelu_of(pre).astype(jnp.bfloat16)
    act_ref[...] = act
    expanded = dot(act, weight_ref[...])
    expanded_ref[...] = expanded
    spread(out_ref, column_sums(expanded, expanded * expanded))


def pool_kernel(
    count,
    expanded_ref,
    mine_ref,
    other_ref,
    gain_ref,
    shift_ref,
    pixels_ref,
    weight_ref,
    total_ref,
    pooled_ref,
    head_ref,
    out_ref,
):
    step = pl.program_id(0)
    rows = expanded_ref.shape[0] // 9
    total = gathered_pair(mine_ref, other_ref)
    total_ref[...] = total
    pooled = None
    for place in range(9):
        block = slice(place * rows, (place + 1) * rows)
        pre = fold(expanded_ref[block, :], gain_ref[...], shift_ref[...], total, count)[2]
        part = gelu_of(pre + pixels_ref[block, :].astype(jnp.float32))
        pooled = part if pooled is None else pooled + part
    pooled = (pooled / 9.0).astype(jnp.bfloat16)
    pooled_ref[...] = pooled.astype(jnp.float32)
    head = dot(pooled, weight_ref[...])

    @pl.when(step == 0)
    def _():
        head_ref[...] = head

    @pl.when(step > 0)
    def _():
        head_ref[...] += head

    @pl.when(step == pl.num_programs(0) - 1)
    def _():
        value = head_ref[...]
        spread(out_ref, column_sums(value, value * value))


def score_kernel(
    count,
    protos,
    head_ref,
    mine_ref,
    other_ref,
    gain_ref,
    shift_ref,
    embed_ref,
    bias_ref,
    proto_ref,
    queued_ref,
    total_ref,
    act_ref,
    embedded_ref,
    scores_ref,
    mass_ref,
    out_ref,
):
    total = gathered_pair(mine_ref, other_ref)
    total_ref[...] = total
    pre = fold(head_ref[...], gain_ref[...], shift_ref[...], total, count)[2]
    act = gelu_of(pre).astype(jnp.bfloat16)
    act_ref[...] = act
    embedded = dot(act, embed_ref[...]) + bias_ref[...]
    embedded_ref[...] = embedded
    rnorm = lax.rsqrt(jnp.sum(embedded * embedded, 1, keepdims=True) + UNIT_EPSILON)
    unit = (embedded * rnorm).astype(jnp.bfloat16)
    crops = unit.shape[0]
    scores = dot(unit, proto_ref[...], ((1,), (1,)))
    scores_ref[...] = scores
    queue = dot(queued_ref[...], proto_ref[...], ((1,), (1,)))
    shape = scores.shape
    inside = lax.broadcasted_iota(jnp.int32, shape, 1) < protos
    mass = jnp.where(inside, jnp.exp(scores / TRANSPORT_SMOOTH), 0.0)
    mass_ref[0:crops, :] = mass
    queue_inside = lax.broadcasted_iota(jnp.int32, queue.shape, 1) < protos
    queue_mass = jnp.where(queue_inside, jnp.exp(queue / TRANSPORT_SMOOTH), 0.0)
    real = queue.shape[0]
    mass_ref[crops:, :] = jnp.zeros((mass_ref.shape[0] - crops, shape[1]), jnp.float32)
    mass_ref[crops : crops + real, :] = queue_mass
    spread(out_ref, jnp.sum(mass, 0, keepdims=True) + jnp.sum(queue_mass, 0, keepdims=True))


def balance(protos, mass, column):
    inside = lax.broadcasted_iota(jnp.int32, column.shape, 1) < protos
    mass = mass / jnp.where(inside, column, 1.0)
    row = jnp.sum(mass, 1, keepdims=True)
    return mass, row


def sweep_kernel(protos, real, mass_ref, mine_ref, other_ref, next_ref, out_ref):
    mass, row = balance(protos, mass_ref[...], gathered_pair(mine_ref, other_ref))
    used = lax.broadcasted_iota(jnp.int32, row.shape, 0) < real
    mass = mass / jnp.where(used, row, 1.0)
    next_ref[...] = mass
    spread(out_ref, jnp.sum(mass, 0, keepdims=True))


def loss_kernel(
    count,
    protos,
    mass_ref,
    mine_ref,
    other_ref,
    here_ref,
    wanted_ref,
    held_ref,
    scores_ref,
    embedded_ref,
    proto_ref,
    act_ref,
    embed_ref,
    head_ref,
    head_total_ref,
    gain_ref,
    shift_ref,
    loss_ref,
    keep_ref,
    send_ref,
    upstream_ref,
    out_ref,
):
    crops = scores_ref.shape[0]
    width = scores_ref.shape[1]
    mass, row = balance(protos, mass_ref[0:crops, :], gathered_pair(mine_ref, other_ref))
    codes = mass / row
    size = crops // CROPS
    row_place = lax.broadcasted_iota(jnp.int32, (crops, crops), 0) % size
    column_place = lax.broadcasted_iota(jnp.int32, (crops, crops), 1) % size
    chosen = (wanted_ref[...] == held_ref[...]) & (row_place == column_place)
    target = lax.dot_general(
        jnp.where(chosen, 1.0, 0.0),
        codes,
        (((1,), (0,)), ((), ())),
        precision=PRECISE,
        preferred_element_type=jnp.float32,
    )
    logits = scores_ref[...] / SOFTMAX_WARMTH
    inside = lax.broadcasted_iota(jnp.int32, logits.shape, 1) < protos
    top = jnp.max(jnp.where(inside, logits, -3.0e38), 1, keepdims=True)
    mass_of = jnp.where(inside, jnp.exp(logits - top), 0.0)
    log_total = jnp.log(jnp.sum(mass_of, 1, keepdims=True)) + top
    loss_ref[...] = -jnp.sum(target * (logits - log_total), 1, keepdims=True)
    share = jnp.sum(target, 1, keepdims=True)
    soft = jnp.where(inside, jnp.exp(logits - log_total), 0.0)
    grad_scores = ((soft * share - target) / SOFTMAX_WARMTH).astype(jnp.bfloat16)
    embedded = embedded_ref[...]
    rnorm = lax.rsqrt(jnp.sum(embedded * embedded, 1, keepdims=True) + UNIT_EPSILON)
    unit = embedded * rnorm
    grad_unit = dot(grad_scores, proto_ref[...])
    grad_embedded = rnorm * (grad_unit - unit * jnp.sum(grad_unit * unit, 1, keepdims=True))
    grad_low = grad_embedded.astype(jnp.bfloat16)
    proto_local = dot(unit.astype(jnp.bfloat16), grad_scores, ((0,), (0,)))
    embed_local = dot(grad_low, act_ref[...], ((0,), (0,)))
    across, outer, rows = keep_ref.shape[:3]
    first = width // outer
    second = embed_local.shape[1] // outer
    flip = here_ref[0] == 1
    for k in range(across):
        lines = [slice((2 * k + c) * rows, (2 * k + c + 1) * rows) for c in range(2)]
        for m in range(outer):
            for value, size, start in ((proto_local, first, 0), (embed_local, second, first)):
                even, odd = (value[line, m * size : (m + 1) * size] for line in lines)
                keep_ref[k, m, :, start : start + size] = jnp.where(flip, odd, even)
                send_ref[k, m, :, start : start + size] = jnp.where(flip, even, odd)
    total = head_total_ref[...]
    normed, _, pre = fold(head_ref[...], gain_ref[...], shift_ref[...], total, count)
    upstream = gelu_slope(pre) * dot(grad_low, embed_ref[...], ((1,), (1,)))
    upstream_ref[...] = upstream
    bias = jnp.sum(grad_embedded, 0, keepdims=True)
    sums = jnp.concatenate([column_sums(upstream, upstream * normed), jnp.concatenate([bias, bias], 0)], 1)
    spread(out_ref, sums)


def split_columns(value, here_ref, near_ref, away_ref):
    part = near_ref.shape[2]
    blocks = [value[:, k * part : (k + 1) * part] for k in range(4)]
    core = here_ref[0] == 1
    chip = here_ref[1] == 1
    for k in range(2):
        first = jnp.where(core, blocks[1 - k], blocks[k])
        second = jnp.where(core, blocks[3 - k], blocks[2 + k])
        near_ref[k] = jnp.where(chip, second, first)
        away_ref[k] = jnp.where(chip, first, second)


def norm_back(upstream, normed, rstd, gain, total, count):
    return gain * rstd * (upstream - total[0:1] / count - normed * (total[1:2] / count))


def head_back_kernel(
    count,
    upstream_ref,
    mine_ref,
    other_ref,
    head_ref,
    head_total_ref,
    gain_ref,
    shift_ref,
    here_ref,
    sums_ref,
    low_ref,
    near_ref,
    away_ref,
):
    total = gathered_pair(mine_ref, other_ref)
    sums_ref[...] = total
    width = head_ref.shape[1]
    stats = head_total_ref[...]
    normed, rstd, _ = fold(head_ref[...], gain_ref[...], shift_ref[...], stats, count)
    grad = norm_back(upstream_ref[...], normed, rstd, gain_ref[...], total[:, 0:width], count)
    low = grad.astype(jnp.bfloat16)
    low_ref[...] = low
    split_columns(low.astype(jnp.float32), here_ref, near_ref, away_ref)


def pool_back_kernel(
    count,
    grad_ref,
    weight_ref,
    expanded_ref,
    total_ref,
    gain_ref,
    shift_ref,
    pixels_ref,
    upstream_ref,
    out_ref,
):
    rows = expanded_ref.shape[0] // 9
    total = total_ref[...]
    grad_output = dot(grad_ref[...], weight_ref[...], ((1,), (1,))) / 9.0
    first = None
    second = None
    for place in range(9):
        block = slice(place * rows, (place + 1) * rows)
        normed, _, pre = fold(expanded_ref[block, :], gain_ref[...], shift_ref[...], total, count)
        upstream = gelu_slope(pre + pixels_ref[block, :].astype(jnp.float32)) * grad_output
        upstream_ref[block, :] = upstream.astype(jnp.bfloat16)
        weighted = upstream * normed
        first = upstream if first is None else first + upstream
        second = weighted if second is None else second + weighted
    spread(out_ref, column_sums(first, second))


def expand_back_kernel(
    count,
    upstream_ref,
    back_mine_ref,
    back_other_ref,
    expanded_ref,
    total_ref,
    gain_ref,
    weight_ref,
    act_ref,
    conved_ref,
    conved_sums_ref,
    conved_gain_ref,
    conved_shift_ref,
    here_ref,
    sums_ref,
    keep_ref,
    send_ref,
    next_ref,
    out_ref,
):
    step = pl.program_id(0)
    back = gathered_pair(back_mine_ref, back_other_ref)
    sums_ref[...] = back
    stats = total_ref[...]
    normed, rstd, _ = fold(expanded_ref[...], gain_ref[...], 0.0, stats, count)
    grad = norm_back(
        upstream_ref[...].astype(jnp.float32), normed, rstd, gain_ref[...], back, count
    ).astype(jnp.bfloat16)
    part = dot(grad, weight_ref[...], ((1,), (1,)))
    value = dot(act_ref[...], grad, ((0,), (0,)))
    half = value.shape[1] // 2
    flip = here_ref[0] == 1
    keep_ref[0] = jnp.where(flip, value[:, half:], value[:, :half])
    send_ref[0] = jnp.where(flip, value[:, :half], value[:, half:])

    @pl.when(step == 0)
    def _():
        next_ref[...] = part

    @pl.when(step > 0)
    def _():
        next_ref[...] += part

    @pl.when(step == pl.num_programs(0) - 1)
    def _():
        conved, _, pre = fold(
            conved_ref[...], conved_gain_ref[...], conved_shift_ref[...], conved_sums_ref[...], count
        )
        upstream = gelu_slope(pre) * next_ref[...]
        next_ref[...] = upstream
        spread(out_ref, column_sums(upstream, upstream * conved))


def conved_back_kernel(
    count,
    upstream_ref,
    back_ref,
    conved_ref,
    sums_ref,
    gain_ref,
    here_ref,
    total_ref,
    low_ref,
    near_ref,
    away_ref,
):
    back = gathered(back_ref)
    total_ref[...] = back
    normed, rstd, _ = fold(conved_ref[...], gain_ref[...], 0.0, sums_ref[...], count)
    low = norm_back(upstream_ref[...], normed, rstd, gain_ref[...], back, count).astype(jnp.bfloat16)
    low_ref[...] = low
    split_columns(low.astype(jnp.float32), here_ref, near_ref, away_ref)


def spatial_back_kernel(
    count,
    low_ref,
    weight_ref,
    reduced_ref,
    reduced_sums_ref,
    reduced_gain_ref,
    reduced_shift_ref,
    next_ref,
    out_ref,
):
    neck = reduced_ref.shape[1]
    rows = reduced_ref.shape[0] // 9
    for offset, here, there in sorted(pairs(), key=lambda p: p[0] != 4):
        value = dot(
            take(low_ref, here, rows), weight_ref[offset * neck : (offset + 1) * neck, :], ((1,), (1,))
        )
        if offset == 4:
            next_ref[...] = value
        else:
            add_rows(next_ref, there, rows, value)
    reduced, _, pre = fold(
        reduced_ref[...], reduced_gain_ref[...], reduced_shift_ref[...], reduced_sums_ref[...], count
    )
    upstream = gelu_slope(pre) * next_ref[...]
    next_ref[...] = upstream
    spread(out_ref, column_sums(upstream, upstream * reduced))


def spatial_weight_kernel(
    here_ref, act_ref, near_ref, away_ref, core_ref, keep_ref, send_ref, left_ref, right_ref
):
    devices = act_ref.shape[0]
    rows = act_ref.shape[1] // 9
    neck = act_ref.shape[2]
    me = here_ref[0] + 2 * here_ref[1]
    grads = (near_ref, core_ref, away_ref, core_ref)
    for k in range(devices):
        source = me ^ k
        for place in range(9):
            block = slice(place * rows, (place + 1) * rows)
            goal = slice((place * devices + k) * rows, (place * devices + k + 1) * rows)
            left_ref[goal, :] = act_ref[source, block, :].astype(jnp.bfloat16)
            right_ref[goal, :] = grads[k][k // 2 if k % 2 else 0, block, :].astype(jnp.bfloat16)
    size = keep_ref.shape[1]
    mine = here_ref[2]
    for offset, here, there in pairs():
        value = dot(
            take(right_ref, here, rows * devices), take(left_ref, there, rows * devices), ((0,), (0,))
        ).T
        start = offset * neck
        end = start + neck
        while start < end:
            owner = start // size
            stop = min(end, (owner + 1) * size)
            piece = value[start - offset * neck : stop - offset * neck, :]
            lines = slice(start - owner * size, stop - owner * size)

            @pl.when(mine == owner % 2)
            def _():
                keep_ref[owner // 2, lines, :] = piece

            @pl.when(mine != owner % 2)
            def _():
                send_ref[owner // 2, lines, :] = piece

            start = stop


def hidden_weight_kernel(here_ref, pooled_ref, near_ref, y_ref, x_ref, xy_ref, core_ref, out_ref):
    deep, size, _ = out_ref.shape
    me = here_ref[0] + 2 * here_ref[1] + 4 * here_ref[2]
    places = [(0, near_ref, 0), (4, y_ref, 0), (2, x_ref, 0), (6, xy_ref, 0)]
    places += [(1, core_ref, 0), (5, core_ref, 1), (3, core_ref, 2), (7, core_ref, 3)]
    right = jnp.concatenate([ref[k].astype(jnp.bfloat16) for _, ref, k in places], 0)
    for m in range(deep):
        start = pl.multiple_of((2 * m + here_ref[2]) * size, size)
        left = jnp.concatenate(
            [pooled_ref[me ^ mask, :, pl.ds(start, size)].astype(jnp.bfloat16) for mask, _, _ in places], 0
        )
        out_ref[m] = dot(left, right, ((0,), (0,)))


def half_kernel(here_ref, keep_ref, come_ref, mine_ref, other_ref):
    mine = here_ref[1]
    mine_ref[...] = keep_ref[mine] + come_ref[mine]
    other_ref[...] = keep_ref[1 - mine] + come_ref[1 - mine]


def cut_kernel(here_ref, keep_ref, come_ref, mine_ref, *other_refs):
    mine = here_ref[2]
    for x, other_ref in enumerate(other_refs):
        for k in range(mine_ref.shape[1]):
            mine_ref[x, k] = keep_ref[x, 2 * k + mine] + come_ref[x, 2 * k + mine]
            other_ref[k] = keep_ref[x, 2 * k + 1 - mine] + come_ref[x, 2 * k + 1 - mine]


def join_kernel(here_ref, keep_ref, first_ref, second_ref, mine_ref, other_ref):
    mine = here_ref[1]
    flip = mine == 1
    first = first_ref[...]
    second = second_ref[...]
    mine_ref[...] = keep_ref[mine] + jnp.where(flip, second, first)
    other_ref[...] = keep_ref[1 - mine] + jnp.where(flip, first, second)


def side_kernel(here_ref, keep_ref, come_ref, mine_ref, other_ref):
    mine = here_ref[2]
    for k in range(mine_ref.shape[0]):
        mine_ref[k] = keep_ref[2 * k + mine] + come_ref[2 * k + mine]
        other_ref[k] = keep_ref[2 * k + 1 - mine] + come_ref[2 * k + 1 - mine]


def across_kernel(here_ref, keep_ref, come_ref, *out_refs):
    deep = out_refs[0].shape[0]
    for m, out_ref in enumerate(out_refs):
        column = here_ref[1] ^ (m & 1)
        side = here_ref[2] ^ (m >> 1)
        for k in range(deep):
            out_ref[k] = keep_ref[column, 2 * k + side] + come_ref[column, 2 * k + side]


def along_kernel(here_ref, *refs):
    deep = refs[0].shape[0]
    ins, outs = refs[:-deep], refs[-deep:]
    for m, out_ref in enumerate(outs):
        place = here_ref[3] ^ m
        total = ins[0][place]
        for ref in ins[1:]:
            total = total + ref[place]
        out_ref[...] = total


def reduce_back_kernel(
    count,
    upstream_ref,
    back_ref,
    reduced_ref,
    sums_ref,
    gain_ref,
    pixels_ref,
    here_ref,
    total_ref,
    low_ref,
    keep_ref,
    send_ref,
):
    back = gathered(back_ref)
    total_ref[...] = back
    normed, rstd, _ = fold(reduced_ref[...], gain_ref[...], 0.0, sums_ref[...], count)
    low = norm_back(upstream_ref[...], normed, rstd, gain_ref[...], back, count).astype(jnp.bfloat16)
    low_ref[...] = low
    part = keep_ref.shape[2]
    value = dot(pixels_ref[...], low, ((0,), (0,)))
    flip = here_ref[0] == 1
    for k in range(keep_ref.shape[0]):
        even = value[:, 2 * k * part : (2 * k + 1) * part]
        odd = value[:, (2 * k + 1) * part : (2 * k + 2) * part]
        keep_ref[k] = jnp.where(flip, odd, even)
        send_ref[k] = jnp.where(flip, even, odd)


def canvas_kernel(low_ref, weight_ref, upstream_ref, out_ref):
    rows = low_ref.shape[0] // 9
    size = out_ref.shape[2]
    value = dot(low_ref[...], weight_ref[...], ((1,), (1,))) + upstream_ref[...].astype(jnp.float32)
    value = value.astype(jnp.bfloat16)
    for place, corners in tile_places():
        for k, (i, j) in enumerate(corners):
            start = place * rows + k * size
            out_ref[i, j] = value[start : start + size, :]


MADE = []
SCALARS = pl.BlockSpec(memory_space=pltpu.SMEM)
ARRAY = pl.BlockSpec(memory_space=pltpu.VMEM)


def run(kernel, outs, args, scratch=(), flops=0, moved=0, after=(), free=(), **grid):
    if "grid" not in grid:
        kinds = [SCALARS if a.ndim == 1 and a.dtype == jnp.int32 else ARRAY for a in args]
        grid["in_specs"] = kinds
    if len(after) > 0:
        inner = kernel
        count = len(args)
        grid["in_specs"] = list(grid["in_specs"]) + [pl.BlockSpec(memory_space=pl.ANY)] * len(after)
        args = tuple(args) + tuple(after)
        skip = len(after)

        def kernel(*refs):
            inner(*refs[:count], *refs[count + skip :])

    loose = grid.pop("loose", ())
    args = [
        a
        if (a.ndim == 1 and a.dtype == jnp.int32)
        or any(a is other for other in (*loose, *after))
        or any(a is other for other in MADE)
        else pinned(a)
        for a in args
    ]
    made = pl.pallas_call(
        kernel,
        out_shape=outs,
        scratch_shapes=list(scratch),
        compiler_params=pltpu.CompilerParams(vmem_limit_bytes=VMEM_BYTES),
        cost_estimate=pl.CostEstimate(flops=1, bytes_accessed=1, transcendentals=0),
        **grid,
    )(*args)
    MADE.extend(made if isinstance(made, (tuple, list)) else [made])
    return made


def f32(*shape):
    return pltpu.HBM(shape, jnp.float32)


def b16(*shape):
    return pltpu.HBM(shape, jnp.bfloat16)


def near32(*shape):
    return pltpu.VMEM(shape, jnp.float32)


def near16(*shape):
    return pltpu.VMEM(shape, jnp.bfloat16)


def to_all(block):
    return lax.all_to_all(block, AXES, 0, 0, tiled=True)


def to_all_pair(block):
    count = lax.axis_size("grp") * lax.axis_size("in")
    groups = [list(range(k, count, 2)) for k in range(2)]
    mine = lax.all_to_all(block, AXES, 0, 0, tiled=True, axis_index_groups=groups)
    return mine, swap_bit(mine, 0)


def pick(value, bit, axis=0):
    mine = lax.dynamic_index_in_dim(value, my_bit(bit), axis, keepdims=False)
    other = lax.dynamic_index_in_dim(value, 1 - my_bit(bit), axis, keepdims=False)
    return mine, other


def teams(bits):
    count = lax.axis_size("grp") * lax.axis_size("in")
    spans = [0]
    for bit in bits:
        spans = spans + [m | (1 << bit) for m in spans]
    used = sum(1 << bit for bit in bits)
    return [[base | m for m in sorted(spans)] for base in range(count) if base & used == 0]


def pinned(value):
    return pltpu.with_memory_space_constraint(value, pltpu.HBM)


def swap_mask(value, mask):
    count = lax.axis_size("grp") * lax.axis_size("in")
    return lax.ppermute(value, AXES, [(i, i ^ mask) for i in range(count)])


def spread_plane(here, keep, come):
    deep = keep.shape[1] // 2
    parts = run(across_kernel, (f32(deep, *keep.shape[2:]),) * 4, (here, keep, come), moved=4 * keep.size * 3, loose=(come,))
    return [parts[0]] + [
        swap_mask(pinned(parts[m]), 2 * m) for m in range(1, 4)
    ]


def spread_line(here, parts):
    deep = parts[0].shape[0]
    shape = parts[0].shape[1:]
    cut = run(
        along_kernel,
        (f32(*shape),) * deep,
        (here, *parts),
        moved=4 * parts[0].size * (len(parts) + 1),
        loose=parts[1:],
    )
    return [cut[0]] + [swap_mask(cut[m], 8 * m) for m in range(1, deep)]


def together(*values):
    return lax.optimization_barrier(values)


def total_of(parts):
    value = parts[0]
    for part in parts[1:]:
        value = value + part
    return value


def fast(
    canvas,
    reduce_weight,
    gain_first,
    shift_first,
    spatial_weight,
    gain_second,
    shift_second,
    expand_weight,
    gain_third,
    shift_third,
    hidden_weight,
    gain_head,
    shift_head,
    embed_weight,
    embed_bias,
    prototypes,
    queued,
    crop_ids,
    partner,
):
    MADE.clear()
    inner = lax.axis_size("in")
    outer = lax.axis_size("grp")
    devices = inner * outer
    low_bits = bits_of("in")
    canvases = canvas.shape[0]
    channels = canvas.shape[-1]
    neck = reduce_weight.shape[1]
    hidden = hidden_weight.shape[1]
    width = embed_weight.shape[1]
    rows = canvases * SIDE * SIDE
    crops = canvases * CROPS
    protos = prototypes.shape[0]
    wide = -(-protos // (128 * outer)) * 128 * outer
    count = float(rows * devices)
    crop_count = float(crops * devices)
    gain_first, shift_first, gain_second, shift_second = (
        v.reshape(1, -1) for v in (gain_first, shift_first, gain_second, shift_second)
    )
    gain_third, shift_third, gain_head, shift_head, embed_bias = (
        v.reshape(1, -1) for v in (gain_third, shift_third, gain_head, shift_head, embed_bias)
    )
    proto_wide = jnp.pad(prototypes, ((0, wide - protos), (0, 0)))
    field = canvas.transpose(1, 2, 0, 3)

    index = lax.axis_index("grp") * inner + lax.axis_index("in")
    here = jnp.stack([index & 1, (index >> 1) & 1, (index >> 2) & 1, index >> 3]).astype(jnp.int32)
    quadrants = crop_ids[:, :: SIDE // 2, :: SIDE // 2].reshape(canvases, CROPS).T
    wanted = jnp.sum(
        (quadrants[:, None, :] == jnp.arange(CROPS, dtype=jnp.int32)[None, :, None])
        * partner.T[None, :, :],
        1,
    ).reshape(crops, 1)
    held = quadrants.reshape(1, crops)

    pixels, reduced, sums = run(
        reduce_kernel,
        (near16(rows, channels), f32(rows, neck), near32(devices, 2, neck)),
        (field, reduce_weight),
        flops=2 * rows * channels * neck,
        moved=12_000_000,
    )
    first_sums = to_all(sums)
    first_total, act_wide, conved, sums = run(
        functools.partial(spatial_kernel, count),
        (near32(2, neck), f32(rows, neck), f32(rows, neck), near32(devices, 2, neck)),
        (reduced, first_sums, gain_first, shift_first, spatial_weight),
        loose=(first_sums, spatial_weight),
        scratch=[pltpu.VMEM((rows, neck), jnp.bfloat16)],
        flops=11 * rows * neck * neck,
        moved=12_000_000,
    )
    act_all = lax.all_gather(act_wide, "in")
    second_sums = to_all(sums)
    second_total, act_second, expanded, sums = run(
        functools.partial(expand_kernel, count),
        (near32(2, neck), near16(rows, neck), f32(rows, channels), near32(devices // 2, 2, channels)),
        (conved, second_sums, gain_second, shift_second, expand_weight),
        loose=(second_sums, expand_weight),
        flops=2 * rows * channels * neck,
        moved=12_000_000,
    )
    third_mine, third_other = to_all_pair(sums)
    block = channels // outer
    chunk = 2 * block
    chunks = channels // chunk
    columns = lambda n: pl.BlockSpec((n, chunk), lambda k: (0, k))
    stats = lambda n: pl.BlockSpec((n, 2, chunk), lambda k: (0, 0, k))
    whole = lambda *shape: pl.BlockSpec(shape, lambda k: (0,) * len(shape))
    third_total, pooled, head_pre, sums = run(
        functools.partial(pool_kernel, count),
        (near32(2, channels), f32(crops, channels), f32(crops, hidden), near32(devices // 2, 2, hidden)),
        (expanded, third_mine, third_other, gain_third, shift_third, pixels, hidden_weight),
        loose=(third_mine, third_other),
        flops=2 * crops * channels * hidden,
        moved=18_000_000,
        grid=(chunks,),
        in_specs=[
            columns(rows),
            stats(devices // 2),
            stats(devices // 2),
            columns(1),
            columns(1),
            columns(rows),
            pl.BlockSpec((chunk, hidden), lambda k: (k, 0)),
        ],
        out_specs=[
            columns(2),
            columns(crops),
            whole(crops, hidden),
            whole(devices // 2, 2, hidden),
        ],
    )
    pooled_all = lax.all_gather(pooled, AXES, axis_index_groups=teams(range(low_bits + 1)))
    head_mine, head_other = to_all_pair(sums)
    real = crops + queued.shape[0]
    mass_rows = -(-real // 8) * 8
    head_total, act_head, embedded, scores, mass, sums = run(
        functools.partial(score_kernel, crop_count, protos),
        (
            near32(2, hidden),
            near16(crops, hidden),
            near32(crops, width),
            f32(crops, wide),
            near32(mass_rows, wide),
            near32(devices // 2, 1, wide),
        ),
        (
            head_pre,
            head_mine,
            head_other,
            gain_head,
            shift_head,
            embed_weight,
            embed_bias,
            proto_wide,
            queued,
        ),
        loose=(head_mine, head_other, embed_weight, proto_wide),
        flops=2 * crops * width * (hidden + wide),
        moved=6_000_000,
    )
    for _ in range(ITERS - 1):
        column_mine, column_other = to_all_pair(sums)
        mass, sums = run(
            functools.partial(sweep_kernel, protos, real),
            (near32(mass_rows, wide), near32(devices // 2, 1, wide)),
            (mass, column_mine, column_other),
            loose=(column_mine, column_other, mass),
            moved=3_000_000,
        )
    column_mine, column_other = to_all_pair(sums)
    loss, small_keep, small_send, upstream, sums = run(
        functools.partial(loss_kernel, crop_count, protos),
        (
            f32(crops, 1),
            f32(inner // 2, outer, width // inner, (wide + hidden) // outer),
            f32(inner // 2, outer, width // inner, (wide + hidden) // outer),
            near32(crops, hidden),
            near32(devices // 2, 2, hidden + width),
        ),
        (
            mass,
            column_mine,
            column_other,
            here,
            wanted,
            held,
            scores,
            embedded,
            proto_wide,
            act_head,
            embed_weight,
            head_pre,
            head_total,
            gain_head,
            shift_head,
        ),
        loose=(column_mine, column_other, mass),
        flops=6 * crops * width * (hidden + wide),
        moved=9_000_000,
    )
    back_mine, back_other = to_all_pair(sums)
    small = spread_plane(here, small_keep, swap_mask(small_send, 1))
    part = hidden // inner
    head_sums, grad_head, head_near, head_away = run(
        functools.partial(head_back_kernel, crop_count),
        (f32(2, hidden + width), near16(crops, hidden), f32(2, crops, part), f32(2, crops, part)),
        (upstream, back_mine, back_other, head_pre, head_total, gain_head, shift_head, here),
        loose=(upstream, back_mine, back_other),
        after=(small[0],),
        moved=3_000_000,
    )
    grad_pre_out, sums = run(
        functools.partial(pool_back_kernel, count),
        (near16(rows, channels), near32(devices // 2, 2, channels)),
        (
            grad_head,
            hidden_weight,
            expanded,
            third_total,
            gain_third,
            shift_third,
            pixels,
        ),
        flops=2 * crops * channels * hidden,
        moved=20_000_000,
        after=(small[0],),
        grid=(chunks,),
        in_specs=[
            whole(crops, hidden),
            pl.BlockSpec((chunk, hidden), lambda k: (k, 0)),
            columns(rows),
            columns(2),
            columns(1),
            columns(1),
            columns(rows),
        ],
        out_specs=[columns(rows), stats(devices // 2)],
    )
    back_mine, back_other = to_all_pair(together(sums, *small[1:])[0])
    part = channels // inner
    columns = lambda n: pl.BlockSpec((n, 2 * part), lambda k: (0, k))
    stats = lambda n: pl.BlockSpec((n, 2, 2 * part), lambda k: (0, 0, k))
    def joined(keep, send, size):
        shape = (inner // 2, outer, size // outer, -1)
        return keep.reshape(shape), swap_mask(send, 1).reshape(shape)

    third_back, expand_keep, expand_send, upstream, sums = run(
        functools.partial(expand_back_kernel, count),
        (
            f32(2, channels),
            f32(inner // 2, neck, part),
            f32(inner // 2, neck, part),
            near32(rows, neck),
            near32(devices, 2, neck),
        ),
        (
            grad_pre_out,
            back_mine,
            back_other,
            expanded,
            third_total,
            gain_third,
            expand_weight,
            act_second,
            conved,
            second_total,
            gain_second,
            shift_second,
            here,
        ),
        flops=4 * rows * channels * neck,
        moved=22_000_000,
        loose=(back_mine, back_other),
        grid=(inner // 2,),
        in_specs=[
            columns(rows),
            stats(devices // 2),
            stats(devices // 2),
            columns(rows),
            columns(2),
            columns(1),
            columns(neck),
            whole(rows, neck),
            whole(rows, neck),
            whole(2, neck),
            whole(1, neck),
            whole(1, neck),
            SCALARS,
        ],
        out_specs=[
            columns(2),
            pl.BlockSpec((1, neck, part), lambda k: (k, 0, 0)),
            pl.BlockSpec((1, neck, part), lambda k: (k, 0, 0)),
            whole(rows, neck),
            whole(devices, 2, neck),
        ],
    )
    back = to_all(sums)
    moved = [head_near] + [
        swap_mask(v, mask) for v, mask in ((head_near, 4), (head_away, 2), (head_away, 6))
    ]
    core_grads = swap_mask(jnp.stack([v[1] for v in moved]), 1)
    keep, come = joined(expand_keep, expand_send, neck)
    shape = (outer // 2, *keep.shape[2:])
    expand_kept, *expand_sent = run(
        cut_kernel, (f32(inner // 2, *shape), f32(*shape), f32(*shape)), (here, keep, come), loose=(come,)
    )
    expand_first = swap_mask(pinned(expand_sent[0]), 4)
    second_back, grad_conved, conved_near, conved_away = run(
        functools.partial(conved_back_kernel, count),
        (
            f32(2, neck),
            near16(rows, neck),
            f32(2, rows, neck // inner),
            f32(2, rows, neck // inner),
        ),
        (upstream, back, conved, second_total, gain_second, here),
        loose=(back, upstream),
        after=(expand_sent[0], *moved[1:]),
    )
    away = swap_mask(conved_away, 2)
    expand_second = swap_mask(pinned(expand_sent[1]), 4)
    upstream, sums = run(
        functools.partial(spatial_back_kernel, count),
        (near32(rows, neck), near32(devices, 2, neck)),
        (
            grad_conved,
            spatial_weight,
            reduced,
            first_total,
            gain_first,
            shift_first,
        ),
        loose=(spatial_weight,),
    )
    small = spread_line(here, small)
    hidden_local = run(
        hidden_weight_kernel,
        f32(outer // 2, channels // outer, hidden // inner),
        (here, pooled_all, *moved, core_grads),
        loose=(*moved[1:], core_grads),
        flops=crops * 2 * inner * channels * hidden // inner,
        moved=7_000_000,
    )
    sums, away, expand_first, expand_second, hidden_local, *small = together(
        sums, away, expand_first, expand_second, hidden_local, *small
    )
    small = total_of(small)
    hidden_grad = lax.psum_scatter(
        hidden_local, "grp", axis_index_groups=[list(range(k, outer, 2)) for k in range(2)]
    )
    back = to_all(sums)
    expand_kept, sent = run(
        join_kernel,
        (f32(*expand_kept.shape[1:]),) * 2,
        (here, expand_kept, expand_first, expand_second),
        loose=(expand_first, expand_second),
    )
    expand_come = swap_mask(pinned(sent), 2)
    core = swap_mask(jnp.stack([conved_near[1], away[1]]), 1)
    spatial_keep, spatial_send = run(
        spatial_weight_kernel,
        (f32(outer // 2, 9 * neck // outer, neck // inner),) * 2,
        (here, act_all, conved_near, away, core),
        loose=(away, core),
        scratch=[
            pltpu.VMEM((rows * inner, neck), jnp.bfloat16),
            pltpu.VMEM((rows * inner, neck // inner), jnp.bfloat16),
        ],
        after=(sent,),
    )
    spatial_come = swap_mask(pinned(spatial_send), 4)
    first_back, grad_reduced, reduce_keep, reduce_send = run(
        functools.partial(reduce_back_kernel, count),
        (
            f32(2, neck),
            near16(rows, neck),
            f32(inner // 2, channels, neck // inner),
            f32(inner // 2, channels, neck // inner),
        ),
        (upstream, back, reduced, first_total, gain_first, pixels, here),
        loose=(back, upstream),
        flops=2 * rows * channels * neck,
        moved=12_000_000,
        after=(spatial_send,),
    )
    reduce_send, expand_come = together(reduce_send, expand_come)
    keep, come = joined(reduce_keep, reduce_send, channels)
    kept, sent = run(half_kernel, (f32(*keep.shape[1:]),) * 2, (here, keep, come), loose=(come,))
    come = swap_mask(pinned(sent), 2)
    expand_parts = spread_line(here, [expand_kept, expand_come])
    canvas_grad = run(
        canvas_kernel,
        b16(SIDE, SIDE, canvases, channels),
        (grad_reduced, reduce_weight, grad_pre_out),
        after=(sent, expand_parts[0]),
    )
    first = wide // outer
    sent = jnp.broadcast_to(small[None, :, :first], (outer, width // inner, first))
    sent, _ = together(sent, kept)
    sent = lax.all_to_all(sent, "grp", 0, 0, tiled=True)
    come, spatial_come, canvas_grad, sent, hidden_grad, *expand_parts = together(
        come, spatial_come, canvas_grad, sent, hidden_grad, *expand_parts
    )
    kept, other = run(
        side_kernel,
        (f32(kept.shape[0] // 2, *kept.shape[1:]),) * 2,
        (here, kept, come),
        loose=(come,),
    )
    come = swap_mask(pinned(other), 4)
    spatial_parts = spread_line(here, [spatial_keep, spatial_come])
    reduce_parts = spread_line(here, [kept, come])
    ends = together(*reduce_parts, *spatial_parts, *expand_parts)
    deep = outer // 2
    reduce_parts, spatial_parts, expand_parts = ends[:deep], ends[deep : 2 * deep], ends[2 * deep :]
    spatial_grad = total_of(spatial_parts)
    expand_grad = total_of(expand_parts)
    reduce_grad = total_of(reduce_parts)
    canvas_grad = canvas_grad.transpose(2, 0, 1, 3)
    embed_grad = small[:, first:].T
    prototypes_grad = sent.transpose(1, 0, 2).reshape(width // inner, wide)[:, :protos].T
    ids = jnp.arange(CROPS, dtype=jnp.int32)
    crop_loss = jnp.sum(
        (quadrants.T[:, None, :] == ids[None, :, None]) * loss.reshape(CROPS, canvases).T[:, None, :], 2
    )
    return (
        crop_loss,
        canvas_grad,
        reduce_grad,
        spatial_grad,
        expand_grad,
        hidden_grad,
        embed_grad,
        head_sums[0, hidden:],
        prototypes_grad,
        first_back[1],
        first_back[0],
        second_back[1],
        second_back[0],
        third_back[1],
        third_back[0],
        head_sums[1, :hidden],
        head_sums[0, :hidden],
    )


def solution(mesh):
    placed = (
        P(("grp", "in"), None, None, None),
        P(),
        P(),
        P(),
        P(),
        P(),
        P(),
        P(),
        P(),
        P(),
        P(),
        P(),
        P(),
        P(),
        P(),
        P(),
        P(("grp", "in"), None),
        P(("grp", "in"), None, None),
        P(("grp", "in"), None),
    )
    lanes = 128 * mesh.shape["grp"]
    aligned = mesh.shape["in"] * 128 <= 512 and lanes * 2 <= 2048
    return jax.shard_map(
        fast if aligned else on_device,
        mesh=mesh,
        in_specs=placed,
        out_specs=(
            P(("grp", "in"), None),
            P(("grp", "in"), None, None, None),
            P("grp", "in"),
            P("grp", "in"),
            P("grp", "in"),
            P("grp", "in"),
            P("grp", "in"),
            P(),
            P(None, "in"),
            P(),
            P(),
            P(),
            P(),
            P(),
            P(),
            P(),
            P(),
        ),
        check_vma=False,
    )
```

```python
import functools

import jax
import jax.numpy as jnp
from jax import lax
from jax.experimental import pallas as pl
from jax.experimental.pallas import tpu as pltpu
from jax.sharding import PartitionSpec as P

SIDE = 6
CROPS = 4
ITERS = 3


BATCH_EPSILON = 1e-05
UNIT_EPSILON = 1e-06
SOFTMAX_WARMTH = 0.1
TRANSPORT_SMOOTH = 0.05
PRECISE = lax.Precision.HIGHEST
ROOT = 0.7978845608028654
CUBIC = 0.044715
VMEM_BYTES = 48 * 1024 * 1024


AXES = ("grp", "in")


def bits_of(axis):
    return lax.axis_size(axis).bit_length() - 1


def swap_bit(value, bit):
    count = lax.axis_size("grp") * lax.axis_size("in")
    return lax.ppermute(value, AXES, [(i, i ^ (1 << bit)) for i in range(count)])


def my_bit(bit):
    index = lax.axis_index("grp") * lax.axis_size("in") + lax.axis_index("in")
    return (index >> bit) & 1


def exchange_sum(block, groups):
    size = len(groups[0])
    spread = jnp.broadcast_to(block[None], (size,) + block.shape)
    moved = lax.all_to_all(spread, AXES, 0, 0, tiled=True, axis_index_groups=groups)
    return jnp.sum(moved, 0)


def all_sum(parts):
    count = lax.axis_size("grp") * lax.axis_size("in")
    sizes = [part.size for part in parts]
    flat = jnp.concatenate([part.reshape(-1) for part in parts])
    total = sum(sizes)
    small = total <= 1536
    unit = 1024 if small else 2048
    rows = -(-total // unit) * unit // 128
    flat = jnp.pad(flat, (0, rows * 128 - total)).reshape(rows, 128)
    if small:
        flat = exchange_sum(flat, [list(range(count))])
    else:
        core = my_bit(0)
        halves = flat.reshape(2, rows // 2, 128)
        mine = lax.dynamic_index_in_dim(halves, core, 0, keepdims=False)
        other = lax.dynamic_index_in_dim(halves, 1 - core, 0, keepdims=False)
        mine = mine + swap_bit(other, 0)
        mine = exchange_sum(mine, [list(range(k, count, 2)) for k in range(2)])
        other = swap_bit(mine, 0)
        flat = jnp.concatenate(
            [jnp.where(core == 0, mine, other), jnp.where(core == 0, other, mine)], 0
        )
    flat = flat.reshape(-1)
    sums = []
    start = 0
    for part, size in zip(parts, sizes):
        sums.append(flat[start : start + size].reshape(part.shape))
        start += size
    return sums


def scatter_sum(blocks, splits=2):
    low = bits_of("in")
    high = bits_of("grp")
    count = low + high
    rows = blocks.shape[2]
    columns = blocks.shape[3]
    inner = list(range(low))
    outer = list(range(low, count))
    orders = [inner + outer, inner[:1] + outer + inner[1:]][:splits]
    chunks = []
    for k, order in enumerate(orders):
        piece = blocks[:, :, k * (rows // splits) : (k + 1) * (rows // splits)]
        chunks.append((piece.reshape((2,) * count + (rows // splits, columns)), order))
    left = [list(inner[::-1] + outer[::-1]) for _ in orders]
    for stage in range(count):
        following = []
        for k, (piece, order) in enumerate(chunks):
            bit = order[stage]
            place = left[k].index(bit)
            left[k].remove(bit)
            mine = lax.dynamic_index_in_dim(piece, my_bit(bit), place, keepdims=False)
            other = lax.dynamic_index_in_dim(piece, 1 - my_bit(bit), place, keepdims=False)
            following.append((mine + swap_bit(other, bit), order))
        chunks = following
    return jnp.concatenate([piece for piece, _ in chunks], 0)


def blocked(grad):
    rows, columns = grad.shape
    inner = lax.axis_size("in")
    outer = lax.axis_size("grp")
    return grad.reshape(outer, rows // outer, inner, columns // inner).transpose(2, 0, 1, 3)


def contract_rows(left, right):
    return lax.dot_general(
        left, right, (((0,), (0,)), ((), ())), preferred_element_type=jnp.float32
    )


def gelu_back(before, upstream):
    ignored, backward = jax.vjp(jax.nn.gelu, before)
    return backward(upstream)[0]


def normalize(value, gain, shift):
    count = value.shape[0] * lax.axis_size("grp") * lax.axis_size("in")
    total, squares = all_sum((jnp.sum(value, 0), jnp.sum(value * value, 0)))
    middle = total / count
    rstd = lax.rsqrt(squares / count - middle * middle + BATCH_EPSILON)
    normed = (value - middle) * rstd
    return (normed, rstd, normed * gain + shift)


def norm_sums(upstream, normed):
    return all_sum((jnp.sum(upstream, 0), jnp.sum(upstream * normed, 0)))


def normalize_back(upstream, normed, rstd, gain, shift_sum, gain_sum):
    count = normed.shape[0] * lax.axis_size("grp") * lax.axis_size("in")
    return gain * rstd * (upstream - shift_sum / count - normed * gain_sum / count)


def tile_mask(vertical, lateral):
    tile_side = SIDE // 2
    position = jnp.arange(SIDE, dtype=jnp.int32) % tile_side
    row_valid = ((position + vertical - 1 >= 0) & (position + vertical - 1 < tile_side)).astype(
        jnp.float32
    )
    column_valid = ((position + lateral - 1 >= 0) & (position + lateral - 1 < tile_side)).astype(
        jnp.float32
    )
    return row_valid[:, None] * column_valid[None, :]


def columns(field, neck_width):
    canvas_grid = field.reshape(-1, SIDE, SIDE, neck_width)
    padded = jnp.pad(canvas_grid, ((0, 0), (1, 1), (1, 1), (0, 0)))
    windows = [
        padded[:, vertical : vertical + SIDE, lateral : lateral + SIDE, :]
        * tile_mask(vertical, lateral).astype(field.dtype)[None, :, :, None]
        for vertical in range(3)
        for lateral in range(3)
    ]
    return jnp.concatenate(windows, axis=-1).reshape(-1, 9 * neck_width)


def columns_back(grad_cols, neck_width):
    canvas_grid = grad_cols.reshape(-1, SIDE, SIDE, 9, neck_width)
    padded = jnp.zeros((canvas_grid.shape[0], SIDE + 2, SIDE + 2, neck_width), jnp.float32)
    for window in range(9):
        vertical = window // 3
        lateral = window % 3
        masked = canvas_grid[:, :, :, window, :] * tile_mask(vertical, lateral)[None, :, :, None]
        padded = padded.at[:, vertical : vertical + SIDE, lateral : lateral + SIDE, :].add(masked)
    return padded[:, 1:-1, 1:-1, :].reshape(-1, neck_width)


def normalize_rows(embedded):
    return embedded * lax.rsqrt(jnp.sum(embedded * embedded, axis=1, keepdims=True) + UNIT_EPSILON)


def on_device(
    canvas,
    reduce_weight,
    gain_first,
    shift_first,
    spatial_weight,
    gain_second,
    shift_second,
    expand_weight,
    gain_third,
    shift_third,
    hidden_weight,
    gain_head,
    shift_head,
    embed_weight,
    embed_bias,
    prototypes,
    queued,
    crop_ids,
    partner,
):
    canvases = canvas.shape[0]
    channels = canvas.shape[-1]
    neck_width = reduce_weight.shape[1]
    pixels = canvas.reshape(-1, channels)
    reduced = jnp.dot(pixels, reduce_weight, preferred_element_type=jnp.float32)
    normed_first, rstd_first, pre_first = normalize(reduced, gain_first, shift_first)
    act_first = jax.nn.gelu(pre_first).astype(jnp.bfloat16)
    cols_first = columns(act_first, neck_width)
    conved = jnp.dot(cols_first, spatial_weight, preferred_element_type=jnp.float32)
    normed_second, rstd_second, pre_second = normalize(conved, gain_second, shift_second)
    act_second = jax.nn.gelu(pre_second).astype(jnp.bfloat16)
    expanded = jnp.dot(act_second, expand_weight, preferred_element_type=jnp.float32)
    normed_third, rstd_third, pre_third = normalize(expanded, gain_third, shift_third)
    pre_out = pre_third + pixels.astype(jnp.float32)
    output = jax.nn.gelu(pre_out)
    member = (
        crop_ids.reshape(canvases, SIDE * SIDE, 1)
        == jnp.arange(CROPS, dtype=jnp.int32)[None, None, :]
    ).astype(jnp.float32)
    counts = jnp.sum(member, axis=1)[:, :, None]
    pooled = (
        jnp.einsum(
            "cpk,cpd->ckd",
            member,
            output.reshape(canvases, SIDE * SIDE, channels),
            precision=PRECISE,
        )
        / counts
    )
    pooled_low = pooled.reshape(-1, channels).astype(jnp.bfloat16)
    head_pre = jnp.dot(pooled_low, hidden_weight, preferred_element_type=jnp.float32)
    normed_head, rstd_head, pre_head = normalize(head_pre, gain_head, shift_head)
    act_head = jax.nn.gelu(pre_head).astype(jnp.bfloat16)
    embedded = jnp.dot(act_head, embed_weight, preferred_element_type=jnp.float32) + embed_bias
    normalized_features, unit_back = jax.vjp(normalize_rows, embedded)
    unit_low = normalized_features.astype(jnp.bfloat16)
    similarity_matrix = jnp.dot(unit_low, prototypes.T, preferred_element_type=jnp.float32)
    queue_similarity = jnp.dot(queued, prototypes.T, preferred_element_type=jnp.float32)
    crop_probability = jnp.exp(similarity_matrix / TRANSPORT_SMOOTH)
    queue_probability = jnp.exp(queue_similarity / TRANSPORT_SMOOTH)
    for sweep_index in range(ITERS):
        column = all_sum(
            (jnp.sum(crop_probability, 0) + jnp.sum(queue_probability, 0),)
        )[0]
        crop_probability = crop_probability / column
        queue_probability = queue_probability / column
        crop_probability = crop_probability / jnp.sum(crop_probability, axis=1, keepdims=True)
        queue_probability = queue_probability / jnp.sum(queue_probability, axis=1, keepdims=True)
    select = (partner[:, :, None] == jnp.arange(CROPS, dtype=jnp.int32)[None, None, :]).astype(
        jnp.float32
    )
    target = jnp.einsum(
        "cjk,ckp->cjp", select, crop_probability.reshape(canvases, CROPS, -1), precision=PRECISE
    ).reshape(-1, crop_probability.shape[1])
    scaled_similarity = similarity_matrix / SOFTMAX_WARMTH
    log_total = jax.nn.logsumexp(scaled_similarity, axis=1, keepdims=True)
    crop_loss = -jnp.sum(target * (scaled_similarity - log_total), axis=1)
    grad_scores = (
        (jnp.exp(scaled_similarity - log_total) * jnp.sum(target, axis=1, keepdims=True) - target)
        / SOFTMAX_WARMTH
    ).astype(jnp.bfloat16)
    grad_unit = jnp.dot(grad_scores, prototypes, preferred_element_type=jnp.float32)
    proto_local = contract_rows(grad_scores, unit_low)
    grad_embedded = unit_back(grad_unit)[0]
    grad_embedded_low = grad_embedded.astype(jnp.bfloat16)
    embed_local = contract_rows(act_head, grad_embedded_low)
    grad_act_head = jnp.dot(grad_embedded_low, embed_weight.T, preferred_element_type=jnp.float32)
    grad_pre_head = gelu_back(pre_head, grad_act_head)
    shift_head_grad, gain_head_grad, embed_bias_grad = all_sum(
        (
            jnp.sum(grad_pre_head, 0),
            jnp.sum(grad_pre_head * normed_head, 0),
            jnp.sum(grad_embedded, 0),
        )
    )
    grad_head = normalize_back(
        grad_pre_head, normed_head, rstd_head, gain_head, shift_head_grad, gain_head_grad
    ).astype(jnp.bfloat16)
    hidden_local = contract_rows(pooled_low, grad_head)
    grad_pooled = jnp.dot(grad_head, hidden_weight.T, preferred_element_type=jnp.float32)
    grad_output = jnp.einsum(
        "cpk,ckd->cpd",
        member,
        grad_pooled.reshape(canvases, CROPS, channels) / counts,
        precision=PRECISE,
    ).reshape(-1, channels)
    grad_pre_out = gelu_back(pre_out, grad_output)
    shift_third_grad, gain_third_grad = norm_sums(grad_pre_out, normed_third)
    grad_expanded = normalize_back(
        grad_pre_out, normed_third, rstd_third, gain_third, shift_third_grad, gain_third_grad
    ).astype(jnp.bfloat16)
    expand_local = contract_rows(act_second, grad_expanded)
    grad_pre_second = gelu_back(
        pre_second, jnp.dot(grad_expanded, expand_weight.T, preferred_element_type=jnp.float32)
    )
    shift_second_grad, gain_second_grad = norm_sums(grad_pre_second, normed_second)
    grad_conved = normalize_back(
        grad_pre_second,
        normed_second,
        rstd_second,
        gain_second,
        shift_second_grad,
        gain_second_grad,
    ).astype(jnp.bfloat16)
    spatial_local = contract_rows(cols_first, grad_conved)
    grad_act_first = columns_back(
        jnp.dot(grad_conved, spatial_weight.T, preferred_element_type=jnp.float32), neck_width
    )
    grad_pre_first = gelu_back(pre_first, grad_act_first)
    shift_first_grad, gain_first_grad = norm_sums(grad_pre_first, normed_first)
    grad_reduced = normalize_back(
        grad_pre_first, normed_first, rstd_first, gain_first, shift_first_grad, gain_first_grad
    ).astype(jnp.bfloat16)
    reduce_local = contract_rows(pixels, grad_reduced)
    canvas_grad = (
        (jnp.dot(grad_reduced, reduce_weight.T, preferred_element_type=jnp.float32) + grad_pre_out)
        .astype(jnp.bfloat16)
        .reshape(canvas.shape)
    )
    proto_part = lax.psum_scatter(proto_local, "in", scatter_dimension=1, tiled=True)
    prototypes_grad = lax.psum(proto_part, "grp")
    embed_grad = lax.psum_scatter(
        lax.psum_scatter(embed_local, "in", scatter_dimension=1, tiled=True),
        "grp",
        scatter_dimension=0,
        tiled=True,
    )
    hidden_grad = scatter_sum(blocked(hidden_local))
    expand_grad = scatter_sum(blocked(expand_local))
    spatial_grad = scatter_sum(blocked(spatial_local))
    reduce_grad = scatter_sum(blocked(reduce_local))
    return (
        crop_loss.reshape(canvases, CROPS),
        canvas_grad,
        reduce_grad,
        spatial_grad,
        expand_grad,
        hidden_grad,
        embed_grad,
        embed_bias_grad,
        prototypes_grad,
        gain_first_grad,
        shift_first_grad,
        gain_second_grad,
        shift_second_grad,
        gain_third_grad,
        shift_third_grad,
        gain_head_grad,
        shift_head_grad,
    )


def fold(value, gain, shift, total, count):
    middle = total[0:1] / count
    rstd = lax.rsqrt(total[1:2] / count - middle * middle + BATCH_EPSILON)
    normed = (value - middle) * rstd
    return normed, rstd, normed * gain + shift


def tanh_part(value):
    return jnp.tanh(ROOT * (value + CUBIC * (value * value * value)))


def gelu_of(value):
    return 0.5 * value * (1.0 + tanh_part(value))


def gelu_slope(value):
    bend = tanh_part(value)
    inner = ROOT * (1.0 + (3.0 * CUBIC) * (value * value))
    return 0.5 * (1.0 + bend) + 0.5 * value * (1.0 - bend * bend) * inner


def dot(left, right, dims=((1,), (0,))):
    return lax.dot_general(left, right, (dims, ((), ())), preferred_element_type=jnp.float32)


def column_sums(first, second):
    return jnp.concatenate(
        [jnp.sum(first, 0, keepdims=True), jnp.sum(second, 0, keepdims=True)], 0
    )


def spread(ref, value):
    ref[...] = jnp.broadcast_to(value[None], ref.shape)


def gathered(ref):
    return jnp.sum(ref[...], 0)


def gathered_pair(mine_ref, other_ref):
    return jnp.sum(mine_ref[...], 0) + jnp.sum(other_ref[...], 0)


def pairs():
    side = SIDE // 2
    for vertical in range(3):
        for lateral in range(3):
            here = []
            there = []
            for i in range(side):
                for j in range(side):
                    k = i + vertical - 1
                    m = j + lateral - 1
                    if 0 <= k < side and 0 <= m < side:
                        here.append(i * side + j)
                        there.append(k * side + m)
            yield 3 * vertical + lateral, here, there


def runs(places):
    out = []
    for place in places:
        if out and out[-1][0] + out[-1][1] == place:
            out[-1][1] += 1
        else:
            out.append([place, 1])
    return out


def take(ref, places, rows):
    parts = [ref[first * rows : (first + size) * rows, :] for first, size in runs(places)]
    return parts[0] if len(parts) == 1 else jnp.concatenate(parts, 0)


def add_rows(ref, places, rows, value):
    start = 0
    for first, size in runs(places):
        ref[first * rows : (first + size) * rows, :] += value[start : start + size * rows, :]
        start += size * rows


def tile_places():
    side = SIDE // 2
    for i in range(side):
        for j in range(side):
            yield i * side + j, [(a * side + i, b * side + j) for a in range(2) for b in range(2)]


def reduce_kernel(canvas_ref, weight_ref, pixels_ref, reduced_ref, sums_ref):
    rows = 4 * canvas_ref.shape[2]
    for place, corners in tile_places():
        pixels_ref[place * rows : (place + 1) * rows, :] = jnp.concatenate(
            [canvas_ref[i, j] for i, j in corners], 0
        )
    reduced = dot(pixels_ref[...], weight_ref[...])
    reduced_ref[...] = reduced
    spread(sums_ref, column_sums(reduced, reduced * reduced))


def spatial_kernel(
    count,
    reduced_ref,
    sums_ref,
    gain_ref,
    shift_ref,
    weight_ref,
    total_ref,
    wide_ref,
    conved_ref,
    out_ref,
    act_ref,
):
    neck = reduced_ref.shape[1]
    rows = reduced_ref.shape[0] // 9
    total = gathered(sums_ref)
    total_ref[...] = total
    pre = fold(reduced_ref[...], gain_ref[...], shift_ref[...], total, count)[2]
    act = gelu_of(pre).astype(jnp.bfloat16)
    act_ref[...] = act
    wide_ref[...] = act.astype(jnp.float32)
    for offset, here, there in sorted(pairs(), key=lambda p: p[0] != 4):
        part = dot(take(act_ref, there, rows), weight_ref[offset * neck : (offset + 1) * neck, :])
        if offset == 4:
            conved_ref[...] = part
        else:
            add_rows(conved_ref, here, rows, part)
    conved = conved_ref[...]
    spread(out_ref, column_sums(conved, conved * conved))


def expand_kernel(
    count, conved_ref, sums_ref, gain_ref, shift_ref, weight_ref, total_ref, act_ref, expanded_ref, out_ref
):
    total = gathered(sums_ref)
    total_ref[...] = total
    pre = fold(conved_ref[...], gain_ref[...], shift_ref[...], total, count)[2]
    act = gelu_of(pre).astype(jnp.bfloat16)
    act_ref[...] = act
    expanded = dot(act, weight_ref[...])
    expanded_ref[...] = expanded
    spread(out_ref, column_sums(expanded, expanded * expanded))


def pool_kernel(
    count,
    expanded_ref,
    mine_ref,
    other_ref,
    gain_ref,
    shift_ref,
    pixels_ref,
    weight_ref,
    total_ref,
    pooled_ref,
    head_ref,
    out_ref,
):
    step = pl.program_id(0)
    rows = expanded_ref.shape[0] // 9
    total = gathered_pair(mine_ref, other_ref)
    total_ref[...] = total
    pooled = None
    for place in range(9):
        block = slice(place * rows, (place + 1) * rows)
        pre = fold(expanded_ref[block, :], gain_ref[...], shift_ref[...], total, count)[2]
        part = gelu_of(pre + pixels_ref[block, :].astype(jnp.float32))
        pooled = part if pooled is None else pooled + part
    pooled = (pooled / 9.0).astype(jnp.bfloat16)
    pooled_ref[...] = pooled.astype(jnp.float32)
    head = dot(pooled, weight_ref[...])

    @pl.when(step == 0)
    def _():
        head_ref[...] = head

    @pl.when(step > 0)
    def _():
        head_ref[...] += head

    @pl.when(step == pl.num_programs(0) - 1)
    def _():
        value = head_ref[...]
        spread(out_ref, column_sums(value, value * value))


def score_kernel(
    count,
    protos,
    head_ref,
    mine_ref,
    other_ref,
    gain_ref,
    shift_ref,
    embed_ref,
    bias_ref,
    proto_ref,
    queued_ref,
    total_ref,
    act_ref,
    embedded_ref,
    scores_ref,
    mass_ref,
    out_ref,
):
    total = gathered_pair(mine_ref, other_ref)
    total_ref[...] = total
    pre = fold(head_ref[...], gain_ref[...], shift_ref[...], total, count)[2]
    act = gelu_of(pre).astype(jnp.bfloat16)
    act_ref[...] = act
    embedded = dot(act, embed_ref[...]) + bias_ref[...]
    embedded_ref[...] = embedded
    rnorm = lax.rsqrt(jnp.sum(embedded * embedded, 1, keepdims=True) + UNIT_EPSILON)
    unit = (embedded * rnorm).astype(jnp.bfloat16)
    crops = unit.shape[0]
    scores = dot(unit, proto_ref[...], ((1,), (1,)))
    scores_ref[...] = scores
    queue = dot(queued_ref[...], proto_ref[...], ((1,), (1,)))
    shape = scores.shape
    inside = lax.broadcasted_iota(jnp.int32, shape, 1) < protos
    mass = jnp.where(inside, jnp.exp(scores / TRANSPORT_SMOOTH), 0.0)
    mass_ref[0:crops, :] = mass
    queue_inside = lax.broadcasted_iota(jnp.int32, queue.shape, 1) < protos
    queue_mass = jnp.where(queue_inside, jnp.exp(queue / TRANSPORT_SMOOTH), 0.0)
    real = queue.shape[0]
    mass_ref[crops:, :] = jnp.zeros((mass_ref.shape[0] - crops, shape[1]), jnp.float32)
    mass_ref[crops : crops + real, :] = queue_mass
    spread(out_ref, jnp.sum(mass, 0, keepdims=True) + jnp.sum(queue_mass, 0, keepdims=True))


def balance(protos, mass, column):
    inside = lax.broadcasted_iota(jnp.int32, column.shape, 1) < protos
    mass = mass / jnp.where(inside, column, 1.0)
    row = jnp.sum(mass, 1, keepdims=True)
    return mass, row


def sweep_kernel(protos, real, mass_ref, mine_ref, other_ref, next_ref, out_ref):
    mass, row = balance(protos, mass_ref[...], gathered_pair(mine_ref, other_ref))
    used = lax.broadcasted_iota(jnp.int32, row.shape, 0) < real
    mass = mass / jnp.where(used, row, 1.0)
    next_ref[...] = mass
    spread(out_ref, jnp.sum(mass, 0, keepdims=True))


def loss_kernel(
    count,
    protos,
    mass_ref,
    mine_ref,
    other_ref,
    here_ref,
    wanted_ref,
    held_ref,
    scores_ref,
    embedded_ref,
    proto_ref,
    act_ref,
    embed_ref,
    head_ref,
    head_total_ref,
    gain_ref,
    shift_ref,
    loss_ref,
    keep_ref,
    send_ref,
    upstream_ref,
    out_ref,
):
    crops = scores_ref.shape[0]
    width = scores_ref.shape[1]
    mass, row = balance(protos, mass_ref[0:crops, :], gathered_pair(mine_ref, other_ref))
    codes = mass / row
    size = crops // CROPS
    row_place = lax.broadcasted_iota(jnp.int32, (crops, crops), 0) % size
    column_place = lax.broadcasted_iota(jnp.int32, (crops, crops), 1) % size
    chosen = (wanted_ref[...] == held_ref[...]) & (row_place == column_place)
    target = lax.dot_general(
        jnp.where(chosen, 1.0, 0.0),
        codes,
        (((1,), (0,)), ((), ())),
        precision=PRECISE,
        preferred_element_type=jnp.float32,
    )
    logits = scores_ref[...] / SOFTMAX_WARMTH
    inside = lax.broadcasted_iota(jnp.int32, logits.shape, 1) < protos
    top = jnp.max(jnp.where(inside, logits, -3.0e38), 1, keepdims=True)
    mass_of = jnp.where(inside, jnp.exp(logits - top), 0.0)
    log_total = jnp.log(jnp.sum(mass_of, 1, keepdims=True)) + top
    loss_ref[...] = -jnp.sum(target * (logits - log_total), 1, keepdims=True)
    share = jnp.sum(target, 1, keepdims=True)
    soft = jnp.where(inside, jnp.exp(logits - log_total), 0.0)
    grad_scores = ((soft * share - target) / SOFTMAX_WARMTH).astype(jnp.bfloat16)
    embedded = embedded_ref[...]
    rnorm = lax.rsqrt(jnp.sum(embedded * embedded, 1, keepdims=True) + UNIT_EPSILON)
    unit = embedded * rnorm
    grad_unit = dot(grad_scores, proto_ref[...])
    grad_embedded = rnorm * (grad_unit - unit * jnp.sum(grad_unit * unit, 1, keepdims=True))
    grad_low = grad_embedded.astype(jnp.bfloat16)
    proto_local = dot(unit.astype(jnp.bfloat16), grad_scores, ((0,), (0,)))
    embed_local = dot(grad_low, act_ref[...], ((0,), (0,)))
    across, outer, rows = keep_ref.shape[:3]
    first = width // outer
    second = embed_local.shape[1] // outer
    flip = here_ref[0] == 1
    for k in range(across):
        lines = [slice((2 * k + c) * rows, (2 * k + c + 1) * rows) for c in range(2)]
        for m in range(outer):
            for value, size, start in ((proto_local, first, 0), (embed_local, second, first)):
                even, odd = (value[line, m * size : (m + 1) * size] for line in lines)
                keep_ref[k, m, :, start : start + size] = jnp.where(flip, odd, even)
                send_ref[k, m, :, start : start + size] = jnp.where(flip, even, odd)
    total = head_total_ref[...]
    normed, _, pre = fold(head_ref[...], gain_ref[...], shift_ref[...], total, count)
    upstream = gelu_slope(pre) * dot(grad_low, embed_ref[...], ((1,), (1,)))
    upstream_ref[...] = upstream
    bias = jnp.sum(grad_embedded, 0, keepdims=True)
    sums = jnp.concatenate([column_sums(upstream, upstream * normed), jnp.concatenate([bias, bias], 0)], 1)
    spread(out_ref, sums)


def split_columns(value, here_ref, near_ref, away_ref):
    part = near_ref.shape[2]
    blocks = [value[:, k * part : (k + 1) * part] for k in range(4)]
    core = here_ref[0] == 1
    chip = here_ref[1] == 1
    for k in range(2):
        first = jnp.where(core, blocks[1 - k], blocks[k])
        second = jnp.where(core, blocks[3 - k], blocks[2 + k])
        near_ref[k] = jnp.where(chip, second, first)
        away_ref[k] = jnp.where(chip, first, second)


def norm_back(upstream, normed, rstd, gain, total, count):
    return gain * rstd * (upstream - total[0:1] / count - normed * (total[1:2] / count))


def head_back_kernel(
    count,
    upstream_ref,
    mine_ref,
    other_ref,
    head_ref,
    head_total_ref,
    gain_ref,
    shift_ref,
    here_ref,
    sums_ref,
    low_ref,
    near_ref,
    away_ref,
):
    total = gathered_pair(mine_ref, other_ref)
    sums_ref[...] = total
    width = head_ref.shape[1]
    stats = head_total_ref[...]
    normed, rstd, _ = fold(head_ref[...], gain_ref[...], shift_ref[...], stats, count)
    grad = norm_back(upstream_ref[...], normed, rstd, gain_ref[...], total[:, 0:width], count)
    low = grad.astype(jnp.bfloat16)
    low_ref[...] = low
    split_columns(low.astype(jnp.float32), here_ref, near_ref, away_ref)


def pool_back_kernel(
    count,
    grad_ref,
    weight_ref,
    expanded_ref,
    total_ref,
    gain_ref,
    shift_ref,
    pixels_ref,
    upstream_ref,
    out_ref,
):
    rows = expanded_ref.shape[0] // 9
    total = total_ref[...]
    grad_output = dot(grad_ref[...], weight_ref[...], ((1,), (1,))) / 9.0
    first = None
    second = None
    for place in range(9):
        block = slice(place * rows, (place + 1) * rows)
        normed, _, pre = fold(expanded_ref[block, :], gain_ref[...], shift_ref[...], total, count)
        upstream = gelu_slope(pre + pixels_ref[block, :].astype(jnp.float32)) * grad_output
        upstream_ref[block, :] = upstream.astype(jnp.bfloat16)
        weighted = upstream * normed
        first = upstream if first is None else first + upstream
        second = weighted if second is None else second + weighted
    spread(out_ref, column_sums(first, second))


def expand_back_kernel(
    count,
    upstream_ref,
    back_mine_ref,
    back_other_ref,
    expanded_ref,
    total_ref,
    gain_ref,
    weight_ref,
    act_ref,
    conved_ref,
    conved_sums_ref,
    conved_gain_ref,
    conved_shift_ref,
    here_ref,
    sums_ref,
    keep_ref,
    send_ref,
    next_ref,
    out_ref,
):
    step = pl.program_id(0)
    back = gathered_pair(back_mine_ref, back_other_ref)
    sums_ref[...] = back
    stats = total_ref[...]
    normed, rstd, _ = fold(expanded_ref[...], gain_ref[...], 0.0, stats, count)
    grad = norm_back(
        upstream_ref[...].astype(jnp.float32), normed, rstd, gain_ref[...], back, count
    ).astype(jnp.bfloat16)
    part = dot(grad, weight_ref[...], ((1,), (1,)))
    value = dot(act_ref[...], grad, ((0,), (0,)))
    half = value.shape[1] // 2
    flip = here_ref[0] == 1
    keep_ref[0] = jnp.where(flip, value[:, half:], value[:, :half])
    send_ref[0] = jnp.where(flip, value[:, :half], value[:, half:])

    @pl.when(step == 0)
    def _():
        next_ref[...] = part

    @pl.when(step > 0)
    def _():
        next_ref[...] += part

    @pl.when(step == pl.num_programs(0) - 1)
    def _():
        conved, _, pre = fold(
            conved_ref[...], conved_gain_ref[...], conved_shift_ref[...], conved_sums_ref[...], count
        )
        upstream = gelu_slope(pre) * next_ref[...]
        next_ref[...] = upstream
        spread(out_ref, column_sums(upstream, upstream * conved))


def conved_back_kernel(
    count,
    upstream_ref,
    back_ref,
    conved_ref,
    sums_ref,
    gain_ref,
    here_ref,
    total_ref,
    low_ref,
    near_ref,
    away_ref,
):
    back = gathered(back_ref)
    total_ref[...] = back
    normed, rstd, _ = fold(conved_ref[...], gain_ref[...], 0.0, sums_ref[...], count)
    low = norm_back(upstream_ref[...], normed, rstd, gain_ref[...], back, count).astype(jnp.bfloat16)
    low_ref[...] = low
    split_columns(low.astype(jnp.float32), here_ref, near_ref, away_ref)


def spatial_back_kernel(
    count,
    low_ref,
    weight_ref,
    reduced_ref,
    reduced_sums_ref,
    reduced_gain_ref,
    reduced_shift_ref,
    next_ref,
    out_ref,
):
    neck = reduced_ref.shape[1]
    rows = reduced_ref.shape[0] // 9
    for offset, here, there in sorted(pairs(), key=lambda p: p[0] != 4):
        value = dot(
            take(low_ref, here, rows), weight_ref[offset * neck : (offset + 1) * neck, :], ((1,), (1,))
        )
        if offset == 4:
            next_ref[...] = value
        else:
            add_rows(next_ref, there, rows, value)
    reduced, _, pre = fold(
        reduced_ref[...], reduced_gain_ref[...], reduced_shift_ref[...], reduced_sums_ref[...], count
    )
    upstream = gelu_slope(pre) * next_ref[...]
    next_ref[...] = upstream
    spread(out_ref, column_sums(upstream, upstream * reduced))


def spatial_weight_kernel(
    here_ref, act_ref, near_ref, away_ref, core_ref, keep_ref, send_ref, left_ref, right_ref
):
    devices = act_ref.shape[0]
    rows = act_ref.shape[1] // 9
    neck = act_ref.shape[2]
    me = here_ref[0] + 2 * here_ref[1]
    grads = (near_ref, core_ref, away_ref, core_ref)
    for k in range(devices):
        source = me ^ k
        for place in range(9):
            block = slice(place * rows, (place + 1) * rows)
            goal = slice((place * devices + k) * rows, (place * devices + k + 1) * rows)
            left_ref[goal, :] = act_ref[source, block, :].astype(jnp.bfloat16)
            right_ref[goal, :] = grads[k][k // 2 if k % 2 else 0, block, :].astype(jnp.bfloat16)
    size = keep_ref.shape[1]
    mine = here_ref[2]
    for offset, here, there in pairs():
        value = dot(
            take(right_ref, here, rows * devices), take(left_ref, there, rows * devices), ((0,), (0,))
        ).T
        start = offset * neck
        end = start + neck
        while start < end:
            owner = start // size
            stop = min(end, (owner + 1) * size)
            piece = value[start - offset * neck : stop - offset * neck, :]
            lines = slice(start - owner * size, stop - owner * size)

            @pl.when(mine == owner % 2)
            def _():
                keep_ref[owner // 2, lines, :] = piece

            @pl.when(mine != owner % 2)
            def _():
                send_ref[owner // 2, lines, :] = piece

            start = stop


def hidden_weight_kernel(here_ref, pooled_ref, near_ref, y_ref, x_ref, xy_ref, core_ref, out_ref):
    deep, size, _ = out_ref.shape
    me = here_ref[0] + 2 * here_ref[1] + 4 * here_ref[2]
    places = [(0, near_ref, 0), (4, y_ref, 0), (2, x_ref, 0), (6, xy_ref, 0)]
    places += [(1, core_ref, 0), (5, core_ref, 1), (3, core_ref, 2), (7, core_ref, 3)]
    right = jnp.concatenate([ref[k].astype(jnp.bfloat16) for _, ref, k in places], 0)
    for m in range(deep):
        start = pl.multiple_of((2 * m + here_ref[2]) * size, size)
        left = jnp.concatenate(
            [pooled_ref[me ^ mask, :, pl.ds(start, size)].astype(jnp.bfloat16) for mask, _, _ in places], 0
        )
        out_ref[m] = dot(left, right, ((0,), (0,)))


def half_kernel(here_ref, keep_ref, come_ref, mine_ref, other_ref):
    mine = here_ref[1]
    mine_ref[...] = keep_ref[mine] + come_ref[mine]
    other_ref[...] = keep_ref[1 - mine] + come_ref[1 - mine]


def cut_kernel(here_ref, keep_ref, come_ref, mine_ref, *other_refs):
    mine = here_ref[2]
    for x, other_ref in enumerate(other_refs):
        for k in range(mine_ref.shape[1]):
            mine_ref[x, k] = keep_ref[x, 2 * k + mine] + come_ref[x, 2 * k + mine]
            other_ref[k] = keep_ref[x, 2 * k + 1 - mine] + come_ref[x, 2 * k + 1 - mine]


def join_kernel(here_ref, keep_ref, first_ref, second_ref, mine_ref, other_ref):
    mine = here_ref[1]
    flip = mine == 1
    first = first_ref[...]
    second = second_ref[...]
    mine_ref[...] = keep_ref[mine] + jnp.where(flip, second, first)
    other_ref[...] = keep_ref[1 - mine] + jnp.where(flip, first, second)


def side_kernel(here_ref, keep_ref, come_ref, mine_ref, other_ref):
    mine = here_ref[2]
    for k in range(mine_ref.shape[0]):
        mine_ref[k] = keep_ref[2 * k + mine] + come_ref[2 * k + mine]
        other_ref[k] = keep_ref[2 * k + 1 - mine] + come_ref[2 * k + 1 - mine]


def across_kernel(here_ref, keep_ref, come_ref, *out_refs):
    deep = out_refs[0].shape[0]
    for m, out_ref in enumerate(out_refs):
        column = here_ref[1] ^ (m & 1)
        side = here_ref[2] ^ (m >> 1)
        for k in range(deep):
            out_ref[k] = keep_ref[column, 2 * k + side] + come_ref[column, 2 * k + side]


def along_kernel(here_ref, *refs):
    deep = refs[0].shape[0]
    ins, outs = refs[:-deep], refs[-deep:]
    for m, out_ref in enumerate(outs):
        place = here_ref[3] ^ m
        total = ins[0][place]
        for ref in ins[1:]:
            total = total + ref[place]
        out_ref[...] = total


def reduce_back_kernel(
    count,
    upstream_ref,
    back_ref,
    reduced_ref,
    sums_ref,
    gain_ref,
    pixels_ref,
    here_ref,
    total_ref,
    low_ref,
    keep_ref,
    send_ref,
):
    back = gathered(back_ref)
    total_ref[...] = back
    normed, rstd, _ = fold(reduced_ref[...], gain_ref[...], 0.0, sums_ref[...], count)
    low = norm_back(upstream_ref[...], normed, rstd, gain_ref[...], back, count).astype(jnp.bfloat16)
    low_ref[...] = low
    part = keep_ref.shape[2]
    value = dot(pixels_ref[...], low, ((0,), (0,)))
    flip = here_ref[0] == 1
    for k in range(keep_ref.shape[0]):
        even = value[:, 2 * k * part : (2 * k + 1) * part]
        odd = value[:, (2 * k + 1) * part : (2 * k + 2) * part]
        keep_ref[k] = jnp.where(flip, odd, even)
        send_ref[k] = jnp.where(flip, even, odd)


def canvas_kernel(low_ref, weight_ref, upstream_ref, out_ref):
    rows = low_ref.shape[0] // 9
    size = out_ref.shape[2]
    value = dot(low_ref[...], weight_ref[...], ((1,), (1,))) + upstream_ref[...].astype(jnp.float32)
    value = value.astype(jnp.bfloat16)
    for place, corners in tile_places():
        for k, (i, j) in enumerate(corners):
            start = place * rows + k * size
            out_ref[i, j] = value[start : start + size, :]


MADE = []
SCALARS = pl.BlockSpec(memory_space=pltpu.SMEM)
ARRAY = pl.BlockSpec(memory_space=pltpu.VMEM)


def run(kernel, outs, args, scratch=(), flops=0, moved=0, after=(), free=(), **grid):
    if "grid" not in grid:
        kinds = [SCALARS if a.ndim == 1 and a.dtype == jnp.int32 else ARRAY for a in args]
        grid["in_specs"] = kinds
    if len(after) > 0:
        inner = kernel
        count = len(args)
        grid["in_specs"] = list(grid["in_specs"]) + [pl.BlockSpec(memory_space=pl.ANY)] * len(after)
        args = tuple(args) + tuple(after)
        skip = len(after)

        def kernel(*refs):
            inner(*refs[:count], *refs[count + skip :])

    loose = grid.pop("loose", ())
    args = [
        a
        if (a.ndim == 1 and a.dtype == jnp.int32)
        or any(a is other for other in (*loose, *after))
        or any(a is other for other in MADE)
        else pinned(a)
        for a in args
    ]
    made = pl.pallas_call(
        kernel,
        out_shape=outs,
        scratch_shapes=list(scratch),
        compiler_params=pltpu.CompilerParams(vmem_limit_bytes=VMEM_BYTES),
        cost_estimate=pl.CostEstimate(flops=1, bytes_accessed=1, transcendentals=0),
        **grid,
    )(*args)
    for out, value in zip(jax.tree.leaves(outs), jax.tree.leaves(made)):
        if out.memory_space == pltpu.VMEM:
            MADE.append(value)
    return made


def f32(*shape):
    return pltpu.HBM(shape, jnp.float32)


def b16(*shape):
    return pltpu.HBM(shape, jnp.bfloat16)


def near32(*shape):
    return pltpu.VMEM(shape, jnp.float32)


def near16(*shape):
    return pltpu.VMEM(shape, jnp.bfloat16)


def to_all(block):
    return lax.all_to_all(block, AXES, 0, 0, tiled=True)


def to_all_pair(block):
    count = lax.axis_size("grp") * lax.axis_size("in")
    groups = [list(range(k, count, 2)) for k in range(2)]
    mine = lax.all_to_all(block, AXES, 0, 0, tiled=True, axis_index_groups=groups)
    return mine, swap_bit(mine, 0)


def pick(value, bit, axis=0):
    mine = lax.dynamic_index_in_dim(value, my_bit(bit), axis, keepdims=False)
    other = lax.dynamic_index_in_dim(value, 1 - my_bit(bit), axis, keepdims=False)
    return mine, other


def teams(bits):
    count = lax.axis_size("grp") * lax.axis_size("in")
    spans = [0]
    for bit in bits:
        spans = spans + [m | (1 << bit) for m in spans]
    used = sum(1 << bit for bit in bits)
    return [[base | m for m in sorted(spans)] for base in range(count) if base & used == 0]


def pinned(value):
    return pltpu.with_memory_space_constraint(value, pltpu.HBM)


def swap_mask(value, mask):
    count = lax.axis_size("grp") * lax.axis_size("in")
    return lax.ppermute(value, AXES, [(i, i ^ mask) for i in range(count)])


def spread_plane(here, keep, come):
    deep = keep.shape[1] // 2
    parts = run(across_kernel, (f32(deep, *keep.shape[2:]),) * 4, (here, keep, come), moved=4 * keep.size * 3, loose=(come,))
    return [parts[0]] + [
        swap_mask(pinned(parts[m]), 2 * m) for m in range(1, 4)
    ]


def spread_line(here, parts):
    deep = parts[0].shape[0]
    shape = parts[0].shape[1:]
    cut = run(
        along_kernel,
        (f32(*shape),) * deep,
        (here, *parts),
        moved=4 * parts[0].size * (len(parts) + 1),
        loose=parts[1:],
    )
    return [cut[0]] + [swap_mask(cut[m], 8 * m) for m in range(1, deep)]


def together(*values):
    return lax.optimization_barrier(values)


def total_of(parts):
    value = parts[0]
    for part in parts[1:]:
        value = value + part
    return value


def fast(
    canvas,
    reduce_weight,
    gain_first,
    shift_first,
    spatial_weight,
    gain_second,
    shift_second,
    expand_weight,
    gain_third,
    shift_third,
    hidden_weight,
    gain_head,
    shift_head,
    embed_weight,
    embed_bias,
    prototypes,
    queued,
    crop_ids,
    partner,
):
    MADE.clear()
    inner = lax.axis_size("in")
    outer = lax.axis_size("grp")
    devices = inner * outer
    low_bits = bits_of("in")
    canvases = canvas.shape[0]
    channels = canvas.shape[-1]
    neck = reduce_weight.shape[1]
    hidden = hidden_weight.shape[1]
    width = embed_weight.shape[1]
    rows = canvases * SIDE * SIDE
    crops = canvases * CROPS
    protos = prototypes.shape[0]
    wide = -(-protos // (128 * outer)) * 128 * outer
    count = float(rows * devices)
    crop_count = float(crops * devices)
    gain_first, shift_first, gain_second, shift_second = (
        v.reshape(1, -1) for v in (gain_first, shift_first, gain_second, shift_second)
    )
    gain_third, shift_third, gain_head, shift_head, embed_bias = (
        v.reshape(1, -1) for v in (gain_third, shift_third, gain_head, shift_head, embed_bias)
    )
    proto_wide = jnp.pad(prototypes, ((0, wide - protos), (0, 0)))
    field = canvas.transpose(1, 2, 0, 3)

    index = lax.axis_index("grp") * inner + lax.axis_index("in")
    here = jnp.stack([index & 1, (index >> 1) & 1, (index >> 2) & 1, index >> 3]).astype(jnp.int32)
    quadrants = crop_ids[:, :: SIDE // 2, :: SIDE // 2].reshape(canvases, CROPS).T
    wanted = jnp.sum(
        (quadrants[:, None, :] == jnp.arange(CROPS, dtype=jnp.int32)[None, :, None])
        * partner.T[None, :, :],
        1,
    ).reshape(crops, 1)
    held = quadrants.reshape(1, crops)

    pixels, reduced, sums = run(
        reduce_kernel,
        (near16(rows, channels), f32(rows, neck), near32(devices, 2, neck)),
        (field, reduce_weight),
        flops=2 * rows * channels * neck,
        moved=12_000_000,
    )
    first_sums = to_all(sums)
    first_total, act_wide, conved, sums = run(
        functools.partial(spatial_kernel, count),
        (near32(2, neck), f32(rows, neck), f32(rows, neck), near32(devices, 2, neck)),
        (reduced, first_sums, gain_first, shift_first, spatial_weight),
        loose=(first_sums, spatial_weight),
        scratch=[pltpu.VMEM((rows, neck), jnp.bfloat16)],
        flops=11 * rows * neck * neck,
        moved=12_000_000,
    )
    act_all = lax.all_gather(act_wide, "in")
    second_sums = to_all(sums)
    second_total, act_second, expanded, sums = run(
        functools.partial(expand_kernel, count),
        (near32(2, neck), near16(rows, neck), f32(rows, channels), near32(devices // 2, 2, channels)),
        (conved, second_sums, gain_second, shift_second, expand_weight),
        loose=(second_sums, expand_weight),
        flops=2 * rows * channels * neck,
        moved=12_000_000,
    )
    third_mine, third_other = to_all_pair(sums)
    block = channels // outer
    chunk = 2 * block
    chunks = channels // chunk
    columns = lambda n: pl.BlockSpec((n, chunk), lambda k: (0, k))
    stats = lambda n: pl.BlockSpec((n, 2, chunk), lambda k: (0, 0, k))
    whole = lambda *shape: pl.BlockSpec(shape, lambda k: (0,) * len(shape))
    third_total, pooled, head_pre, sums = run(
        functools.partial(pool_kernel, count),
        (near32(2, channels), f32(crops, channels), f32(crops, hidden), near32(devices // 2, 2, hidden)),
        (expanded, third_mine, third_other, gain_third, shift_third, pixels, hidden_weight),
        loose=(third_mine, third_other),
        flops=2 * crops * channels * hidden,
        moved=18_000_000,
        grid=(chunks,),
        in_specs=[
            columns(rows),
            stats(devices // 2),
            stats(devices // 2),
            columns(1),
            columns(1),
            columns(rows),
            pl.BlockSpec((chunk, hidden), lambda k: (k, 0)),
        ],
        out_specs=[
            columns(2),
            columns(crops),
            whole(crops, hidden),
            whole(devices // 2, 2, hidden),
        ],
    )
    pooled_all = lax.all_gather(pooled, AXES, axis_index_groups=teams(range(low_bits + 1)))
    head_mine, head_other = to_all_pair(sums)
    real = crops + queued.shape[0]
    mass_rows = -(-real // 8) * 8
    head_total, act_head, embedded, scores, mass, sums = run(
        functools.partial(score_kernel, crop_count, protos),
        (
            near32(2, hidden),
            near16(crops, hidden),
            f32(crops, width),
            f32(crops, wide),
            near32(mass_rows, wide),
            near32(devices // 2, 1, wide),
        ),
        (
            head_pre,
            head_mine,
            head_other,
            gain_head,
            shift_head,
            embed_weight,
            embed_bias,
            proto_wide,
            queued,
        ),
        loose=(head_mine, head_other, embed_weight, proto_wide),
        flops=2 * crops * width * (hidden + wide),
        moved=6_000_000,
    )
    for _ in range(ITERS - 1):
        column_mine, column_other = to_all_pair(sums)
        mass, sums = run(
            functools.partial(sweep_kernel, protos, real),
            (near32(mass_rows, wide), near32(devices // 2, 1, wide)),
            (mass, column_mine, column_other),
            loose=(column_mine, column_other, mass),
            moved=3_000_000,
        )
    column_mine, column_other = to_all_pair(sums)
    loss, small_keep, small_send, upstream, sums = run(
        functools.partial(loss_kernel, crop_count, protos),
        (
            f32(crops, 1),
            f32(inner // 2, outer, width // inner, (wide + hidden) // outer),
            f32(inner // 2, outer, width // inner, (wide + hidden) // outer),
            f32(crops, hidden),
            near32(devices // 2, 2, hidden + width),
        ),
        (
            mass,
            column_mine,
            column_other,
            here,
            wanted,
            held,
            scores,
            embedded,
            proto_wide,
            act_head,
            embed_weight,
            head_pre,
            head_total,
            gain_head,
            shift_head,
        ),
        loose=(column_mine, column_other, mass),
        flops=6 * crops * width * (hidden + wide),
        moved=9_000_000,
    )
    back_mine, back_other = to_all_pair(sums)
    small = spread_plane(here, small_keep, swap_mask(small_send, 1))
    part = hidden // inner
    head_sums, grad_head, head_near, head_away = run(
        functools.partial(head_back_kernel, crop_count),
        (f32(2, hidden + width), near16(crops, hidden), f32(2, crops, part), f32(2, crops, part)),
        (upstream, back_mine, back_other, head_pre, head_total, gain_head, shift_head, here),
        loose=(back_mine, back_other),
        after=(small[0],),
        moved=3_000_000,
    )
    grad_pre_out, sums = run(
        functools.partial(pool_back_kernel, count),
        (near16(rows, channels), near32(devices // 2, 2, channels)),
        (
            grad_head,
            hidden_weight,
            expanded,
            third_total,
            gain_third,
            shift_third,
            pixels,
        ),
        flops=2 * crops * channels * hidden,
        moved=20_000_000,
        after=(small[0],),
        grid=(chunks,),
        in_specs=[
            whole(crops, hidden),
            pl.BlockSpec((chunk, hidden), lambda k: (k, 0)),
            columns(rows),
            columns(2),
            columns(1),
            columns(1),
            columns(rows),
        ],
        out_specs=[columns(rows), stats(devices // 2)],
    )
    back_mine, back_other = to_all_pair(together(sums, *small[1:])[0])
    part = channels // inner
    columns = lambda n: pl.BlockSpec((n, 2 * part), lambda k: (0, k))
    stats = lambda n: pl.BlockSpec((n, 2, 2 * part), lambda k: (0, 0, k))
    def joined(keep, send, size):
        shape = (inner // 2, outer, size // outer, -1)
        return keep.reshape(shape), swap_mask(send, 1).reshape(shape)

    third_back, expand_keep, expand_send, upstream, sums = run(
        functools.partial(expand_back_kernel, count),
        (
            f32(2, channels),
            f32(inner // 2, neck, part),
            f32(inner // 2, neck, part),
            f32(rows, neck),
            near32(devices, 2, neck),
        ),
        (
            grad_pre_out,
            back_mine,
            back_other,
            expanded,
            third_total,
            gain_third,
            expand_weight,
            act_second,
            conved,
            second_total,
            gain_second,
            shift_second,
            here,
        ),
        flops=4 * rows * channels * neck,
        moved=22_000_000,
        loose=(back_mine, back_other),
        grid=(inner // 2,),
        in_specs=[
            columns(rows),
            stats(devices // 2),
            stats(devices // 2),
            columns(rows),
            columns(2),
            columns(1),
            columns(neck),
            whole(rows, neck),
            whole(rows, neck),
            whole(2, neck),
            whole(1, neck),
            whole(1, neck),
            SCALARS,
        ],
        out_specs=[
            columns(2),
            pl.BlockSpec((1, neck, part), lambda k: (k, 0, 0)),
            pl.BlockSpec((1, neck, part), lambda k: (k, 0, 0)),
            whole(rows, neck),
            whole(devices, 2, neck),
        ],
    )
    back = to_all(sums)
    moved = [head_near] + [
        swap_mask(v, mask) for v, mask in ((head_near, 4), (head_away, 2), (head_away, 6))
    ]
    core_grads = swap_mask(jnp.stack([v[1] for v in moved]), 1)
    keep, come = joined(expand_keep, expand_send, neck)
    shape = (outer // 2, *keep.shape[2:])
    expand_kept, *expand_sent = run(
        cut_kernel, (f32(inner // 2, *shape), f32(*shape), f32(*shape)), (here, keep, come), loose=(come,)
    )
    expand_first = swap_mask(pinned(expand_sent[0]), 4)
    second_back, grad_conved, conved_near, conved_away = run(
        functools.partial(conved_back_kernel, count),
        (
            f32(2, neck),
            near16(rows, neck),
            f32(2, rows, neck // inner),
            f32(2, rows, neck // inner),
        ),
        (upstream, back, conved, second_total, gain_second, here),
        loose=(back,),
        after=(expand_sent[0], *moved[1:]),
    )
    away = swap_mask(conved_away, 2)
    expand_second = swap_mask(pinned(expand_sent[1]), 4)
    upstream, sums = run(
        functools.partial(spatial_back_kernel, count),
        (f32(rows, neck), near32(devices, 2, neck)),
        (
            grad_conved,
            spatial_weight,
            reduced,
            first_total,
            gain_first,
            shift_first,
        ),
        loose=(spatial_weight,),
    )
    small = spread_line(here, small)
    hidden_local = run(
        hidden_weight_kernel,
        f32(outer // 2, channels // outer, hidden // inner),
        (here, pooled_all, *moved, core_grads),
        loose=(*moved[1:], core_grads),
        flops=crops * 2 * inner * channels * hidden // inner,
        moved=7_000_000,
    )
    sums, away, expand_first, expand_second, hidden_local, *small = together(
        sums, away, expand_first, expand_second, hidden_local, *small
    )
    small = total_of(small)
    hidden_grad = lax.psum_scatter(
        hidden_local, "grp", axis_index_groups=[list(range(k, outer, 2)) for k in range(2)]
    )
    back = to_all(sums)
    expand_kept, sent = run(
        join_kernel,
        (f32(*expand_kept.shape[1:]),) * 2,
        (here, expand_kept, expand_first, expand_second),
        loose=(expand_first, expand_second),
    )
    expand_come = swap_mask(pinned(sent), 2)
    core = swap_mask(jnp.stack([conved_near[1], away[1]]), 1)
    spatial_keep, spatial_send = run(
        spatial_weight_kernel,
        (f32(outer // 2, 9 * neck // outer, neck // inner),) * 2,
        (here, act_all, conved_near, away, core),
        loose=(away, core),
        scratch=[
            pltpu.VMEM((rows * inner, neck), jnp.bfloat16),
            pltpu.VMEM((rows * inner, neck // inner), jnp.bfloat16),
        ],
        after=(sent,),
    )
    spatial_come = swap_mask(pinned(spatial_send), 4)
    first_back, grad_reduced, reduce_keep, reduce_send = run(
        functools.partial(reduce_back_kernel, count),
        (
            f32(2, neck),
            near16(rows, neck),
            f32(inner // 2, channels, neck // inner),
            f32(inner // 2, channels, neck // inner),
        ),
        (upstream, back, reduced, first_total, gain_first, pixels, here),
        loose=(back,),
        flops=2 * rows * channels * neck,
        moved=12_000_000,
        after=(spatial_send,),
    )
    reduce_send, expand_come = together(reduce_send, expand_come)
    keep, come = joined(reduce_keep, reduce_send, channels)
    kept, sent = run(half_kernel, (f32(*keep.shape[1:]),) * 2, (here, keep, come), loose=(come,))
    come = swap_mask(pinned(sent), 2)
    expand_parts = spread_line(here, [expand_kept, expand_come])
    canvas_grad = run(
        canvas_kernel,
        b16(SIDE, SIDE, canvases, channels),
        (grad_reduced, reduce_weight, grad_pre_out),
        after=(sent, expand_parts[0]),
    )
    first = wide // outer
    sent = jnp.broadcast_to(small[None, :, :first], (outer, width // inner, first))
    sent, _ = together(sent, kept)
    sent = lax.all_to_all(sent, "grp", 0, 0, tiled=True)
    come, spatial_come, canvas_grad, sent, hidden_grad, *expand_parts = together(
        come, spatial_come, canvas_grad, sent, hidden_grad, *expand_parts
    )
    kept, other = run(
        side_kernel,
        (f32(kept.shape[0] // 2, *kept.shape[1:]),) * 2,
        (here, kept, come),
        loose=(come,),
    )
    come = swap_mask(pinned(other), 4)
    spatial_parts = spread_line(here, [spatial_keep, spatial_come])
    reduce_parts = spread_line(here, [kept, come])
    ends = together(*reduce_parts, *spatial_parts, *expand_parts)
    deep = outer // 2
    reduce_parts, spatial_parts, expand_parts = ends[:deep], ends[deep : 2 * deep], ends[2 * deep :]
    spatial_grad = total_of(spatial_parts)
    expand_grad = total_of(expand_parts)
    reduce_grad = total_of(reduce_parts)
    canvas_grad = canvas_grad.transpose(2, 0, 1, 3)
    embed_grad = small[:, first:].T
    prototypes_grad = sent.transpose(1, 0, 2).reshape(width // inner, wide)[:, :protos].T
    ids = jnp.arange(CROPS, dtype=jnp.int32)
    crop_loss = jnp.sum(
        (quadrants.T[:, None, :] == ids[None, :, None]) * loss.reshape(CROPS, canvases).T[:, None, :], 2
    )
    return (
        crop_loss,
        canvas_grad,
        reduce_grad,
        spatial_grad,
        expand_grad,
        hidden_grad,
        embed_grad,
        head_sums[0, hidden:],
        prototypes_grad,
        first_back[1],
        first_back[0],
        second_back[1],
        second_back[0],
        third_back[1],
        third_back[0],
        head_sums[1, :hidden],
        head_sums[0, :hidden],
    )


def solution(mesh):
    placed = (
        P(("grp", "in"), None, None, None),
        P(),
        P(),
        P(),
        P(),
        P(),
        P(),
        P(),
        P(),
        P(),
        P(),
        P(),
        P(),
        P(),
        P(),
        P(),
        P(("grp", "in"), None),
        P(("grp", "in"), None, None),
        P(("grp", "in"), None),
    )
    lanes = 128 * mesh.shape["grp"]
    aligned = mesh.shape["in"] * 128 <= 512 and lanes * 2 <= 2048
    return jax.shard_map(
        fast if aligned else on_device,
        mesh=mesh,
        in_specs=placed,
        out_specs=(
            P(("grp", "in"), None),
            P(("grp", "in"), None, None, None),
            P("grp", "in"),
            P("grp", "in"),
            P("grp", "in"),
            P("grp", "in"),
            P("grp", "in"),
            P(),
            P(None, "in"),
            P(),
            P(),
            P(),
            P(),
            P(),
            P(),
            P(),
            P(),
        ),
        check_vma=False,
    )
```

```python
import functools

import jax
import jax.numpy as jnp
from jax import lax
from jax.experimental import pallas as pl
from jax.experimental.pallas import tpu as pltpu
from jax.sharding import PartitionSpec as P

SIDE = 6
CROPS = 4
ITERS = 3


BATCH_EPSILON = 1e-05
UNIT_EPSILON = 1e-06
SOFTMAX_WARMTH = 0.1
TRANSPORT_SMOOTH = 0.05
PRECISE = lax.Precision.HIGHEST
ROOT = 0.7978845608028654
CUBIC = 0.044715
VMEM_BYTES = 48 * 1024 * 1024


AXES = ("grp", "in")


def bits_of(axis):
    return lax.axis_size(axis).bit_length() - 1


def swap_bit(value, bit):
    count = lax.axis_size("grp") * lax.axis_size("in")
    return lax.ppermute(value, AXES, [(i, i ^ (1 << bit)) for i in range(count)])


def my_bit(bit):
    index = lax.axis_index("grp") * lax.axis_size("in") + lax.axis_index("in")
    return (index >> bit) & 1


def exchange_sum(block, groups):
    size = len(groups[0])
    spread = jnp.broadcast_to(block[None], (size,) + block.shape)
    moved = lax.all_to_all(spread, AXES, 0, 0, tiled=True, axis_index_groups=groups)
    return jnp.sum(moved, 0)


def all_sum(parts):
    count = lax.axis_size("grp") * lax.axis_size("in")
    sizes = [part.size for part in parts]
    flat = jnp.concatenate([part.reshape(-1) for part in parts])
    total = sum(sizes)
    small = total <= 1536
    unit = 1024 if small else 2048
    rows = -(-total // unit) * unit // 128
    flat = jnp.pad(flat, (0, rows * 128 - total)).reshape(rows, 128)
    if small:
        flat = exchange_sum(flat, [list(range(count))])
    else:
        core = my_bit(0)
        halves = flat.reshape(2, rows // 2, 128)
        mine = lax.dynamic_index_in_dim(halves, core, 0, keepdims=False)
        other = lax.dynamic_index_in_dim(halves, 1 - core, 0, keepdims=False)
        mine = mine + swap_bit(other, 0)
        mine = exchange_sum(mine, [list(range(k, count, 2)) for k in range(2)])
        other = swap_bit(mine, 0)
        flat = jnp.concatenate(
            [jnp.where(core == 0, mine, other), jnp.where(core == 0, other, mine)], 0
        )
    flat = flat.reshape(-1)
    sums = []
    start = 0
    for part, size in zip(parts, sizes):
        sums.append(flat[start : start + size].reshape(part.shape))
        start += size
    return sums


def scatter_sum(blocks, splits=2):
    low = bits_of("in")
    high = bits_of("grp")
    count = low + high
    rows = blocks.shape[2]
    columns = blocks.shape[3]
    inner = list(range(low))
    outer = list(range(low, count))
    orders = [inner + outer, inner[:1] + outer + inner[1:]][:splits]
    chunks = []
    for k, order in enumerate(orders):
        piece = blocks[:, :, k * (rows // splits) : (k + 1) * (rows // splits)]
        chunks.append((piece.reshape((2,) * count + (rows // splits, columns)), order))
    left = [list(inner[::-1] + outer[::-1]) for _ in orders]
    for stage in range(count):
        following = []
        for k, (piece, order) in enumerate(chunks):
            bit = order[stage]
            place = left[k].index(bit)
            left[k].remove(bit)
            mine = lax.dynamic_index_in_dim(piece, my_bit(bit), place, keepdims=False)
            other = lax.dynamic_index_in_dim(piece, 1 - my_bit(bit), place, keepdims=False)
            following.append((mine + swap_bit(other, bit), order))
        chunks = following
    return jnp.concatenate([piece for piece, _ in chunks], 0)


def blocked(grad):
    rows, columns = grad.shape
    inner = lax.axis_size("in")
    outer = lax.axis_size("grp")
    return grad.reshape(outer, rows // outer, inner, columns // inner).transpose(2, 0, 1, 3)


def contract_rows(left, right):
    return lax.dot_general(
        left, right, (((0,), (0,)), ((), ())), preferred_element_type=jnp.float32
    )


def gelu_back(before, upstream):
    ignored, backward = jax.vjp(jax.nn.gelu, before)
    return backward(upstream)[0]


def normalize(value, gain, shift):
    count = value.shape[0] * lax.axis_size("grp") * lax.axis_size("in")
    total, squares = all_sum((jnp.sum(value, 0), jnp.sum(value * value, 0)))
    middle = total / count
    rstd = lax.rsqrt(squares / count - middle * middle + BATCH_EPSILON)
    normed = (value - middle) * rstd
    return (normed, rstd, normed * gain + shift)


def norm_sums(upstream, normed):
    return all_sum((jnp.sum(upstream, 0), jnp.sum(upstream * normed, 0)))


def normalize_back(upstream, normed, rstd, gain, shift_sum, gain_sum):
    count = normed.shape[0] * lax.axis_size("grp") * lax.axis_size("in")
    return gain * rstd * (upstream - shift_sum / count - normed * gain_sum / count)


def tile_mask(vertical, lateral):
    tile_side = SIDE // 2
    position = jnp.arange(SIDE, dtype=jnp.int32) % tile_side
    row_valid = ((position + vertical - 1 >= 0) & (position + vertical - 1 < tile_side)).astype(
        jnp.float32
    )
    column_valid = ((position + lateral - 1 >= 0) & (position + lateral - 1 < tile_side)).astype(
        jnp.float32
    )
    return row_valid[:, None] * column_valid[None, :]


def columns(field, neck_width):
    canvas_grid = field.reshape(-1, SIDE, SIDE, neck_width)
    padded = jnp.pad(canvas_grid, ((0, 0), (1, 1), (1, 1), (0, 0)))
    windows = [
        padded[:, vertical : vertical + SIDE, lateral : lateral + SIDE, :]
        * tile_mask(vertical, lateral).astype(field.dtype)[None, :, :, None]
        for vertical in range(3)
        for lateral in range(3)
    ]
    return jnp.concatenate(windows, axis=-1).reshape(-1, 9 * neck_width)


def columns_back(grad_cols, neck_width):
    canvas_grid = grad_cols.reshape(-1, SIDE, SIDE, 9, neck_width)
    padded = jnp.zeros((canvas_grid.shape[0], SIDE + 2, SIDE + 2, neck_width), jnp.float32)
    for window in range(9):
        vertical = window // 3
        lateral = window % 3
        masked = canvas_grid[:, :, :, window, :] * tile_mask(vertical, lateral)[None, :, :, None]
        padded = padded.at[:, vertical : vertical + SIDE, lateral : lateral + SIDE, :].add(masked)
    return padded[:, 1:-1, 1:-1, :].reshape(-1, neck_width)


def normalize_rows(embedded):
    return embedded * lax.rsqrt(jnp.sum(embedded * embedded, axis=1, keepdims=True) + UNIT_EPSILON)


def on_device(
    canvas,
    reduce_weight,
    gain_first,
    shift_first,
    spatial_weight,
    gain_second,
    shift_second,
    expand_weight,
    gain_third,
    shift_third,
    hidden_weight,
    gain_head,
    shift_head,
    embed_weight,
    embed_bias,
    prototypes,
    queued,
    crop_ids,
    partner,
):
    canvases = canvas.shape[0]
    channels = canvas.shape[-1]
    neck_width = reduce_weight.shape[1]
    pixels = canvas.reshape(-1, channels)
    reduced = jnp.dot(pixels, reduce_weight, preferred_element_type=jnp.float32)
    normed_first, rstd_first, pre_first = normalize(reduced, gain_first, shift_first)
    act_first = jax.nn.gelu(pre_first).astype(jnp.bfloat16)
    cols_first = columns(act_first, neck_width)
    conved = jnp.dot(cols_first, spatial_weight, preferred_element_type=jnp.float32)
    normed_second, rstd_second, pre_second = normalize(conved, gain_second, shift_second)
    act_second = jax.nn.gelu(pre_second).astype(jnp.bfloat16)
    expanded = jnp.dot(act_second, expand_weight, preferred_element_type=jnp.float32)
    normed_third, rstd_third, pre_third = normalize(expanded, gain_third, shift_third)
    pre_out = pre_third + pixels.astype(jnp.float32)
    output = jax.nn.gelu(pre_out)
    member = (
        crop_ids.reshape(canvases, SIDE * SIDE, 1)
        == jnp.arange(CROPS, dtype=jnp.int32)[None, None, :]
    ).astype(jnp.float32)
    counts = jnp.sum(member, axis=1)[:, :, None]
    pooled = (
        jnp.einsum(
            "cpk,cpd->ckd",
            member,
            output.reshape(canvases, SIDE * SIDE, channels),
            precision=PRECISE,
        )
        / counts
    )
    pooled_low = pooled.reshape(-1, channels).astype(jnp.bfloat16)
    head_pre = jnp.dot(pooled_low, hidden_weight, preferred_element_type=jnp.float32)
    normed_head, rstd_head, pre_head = normalize(head_pre, gain_head, shift_head)
    act_head = jax.nn.gelu(pre_head).astype(jnp.bfloat16)
    embedded = jnp.dot(act_head, embed_weight, preferred_element_type=jnp.float32) + embed_bias
    normalized_features, unit_back = jax.vjp(normalize_rows, embedded)
    unit_low = normalized_features.astype(jnp.bfloat16)
    similarity_matrix = jnp.dot(unit_low, prototypes.T, preferred_element_type=jnp.float32)
    queue_similarity = jnp.dot(queued, prototypes.T, preferred_element_type=jnp.float32)
    crop_probability = jnp.exp(similarity_matrix / TRANSPORT_SMOOTH)
    queue_probability = jnp.exp(queue_similarity / TRANSPORT_SMOOTH)
    for sweep_index in range(ITERS):
        column = all_sum(
            (jnp.sum(crop_probability, 0) + jnp.sum(queue_probability, 0),)
        )[0]
        crop_probability = crop_probability / column
        queue_probability = queue_probability / column
        crop_probability = crop_probability / jnp.sum(crop_probability, axis=1, keepdims=True)
        queue_probability = queue_probability / jnp.sum(queue_probability, axis=1, keepdims=True)
    select = (partner[:, :, None] == jnp.arange(CROPS, dtype=jnp.int32)[None, None, :]).astype(
        jnp.float32
    )
    target = jnp.einsum(
        "cjk,ckp->cjp", select, crop_probability.reshape(canvases, CROPS, -1), precision=PRECISE
    ).reshape(-1, crop_probability.shape[1])
    scaled_similarity = similarity_matrix / SOFTMAX_WARMTH
    log_total = jax.nn.logsumexp(scaled_similarity, axis=1, keepdims=True)
    crop_loss = -jnp.sum(target * (scaled_similarity - log_total), axis=1)
    grad_scores = (
        (jnp.exp(scaled_similarity - log_total) * jnp.sum(target, axis=1, keepdims=True) - target)
        / SOFTMAX_WARMTH
    ).astype(jnp.bfloat16)
    grad_unit = jnp.dot(grad_scores, prototypes, preferred_element_type=jnp.float32)
    proto_local = contract_rows(grad_scores, unit_low)
    grad_embedded = unit_back(grad_unit)[0]
    grad_embedded_low = grad_embedded.astype(jnp.bfloat16)
    embed_local = contract_rows(act_head, grad_embedded_low)
    grad_act_head = jnp.dot(grad_embedded_low, embed_weight.T, preferred_element_type=jnp.float32)
    grad_pre_head = gelu_back(pre_head, grad_act_head)
    shift_head_grad, gain_head_grad, embed_bias_grad = all_sum(
        (
            jnp.sum(grad_pre_head, 0),
            jnp.sum(grad_pre_head * normed_head, 0),
            jnp.sum(grad_embedded, 0),
        )
    )
    grad_head = normalize_back(
        grad_pre_head, normed_head, rstd_head, gain_head, shift_head_grad, gain_head_grad
    ).astype(jnp.bfloat16)
    hidden_local = contract_rows(pooled_low, grad_head)
    grad_pooled = jnp.dot(grad_head, hidden_weight.T, preferred_element_type=jnp.float32)
    grad_output = jnp.einsum(
        "cpk,ckd->cpd",
        member,
        grad_pooled.reshape(canvases, CROPS, channels) / counts,
        precision=PRECISE,
    ).reshape(-1, channels)
    grad_pre_out = gelu_back(pre_out, grad_output)
    shift_third_grad, gain_third_grad = norm_sums(grad_pre_out, normed_third)
    grad_expanded = normalize_back(
        grad_pre_out, normed_third, rstd_third, gain_third, shift_third_grad, gain_third_grad
    ).astype(jnp.bfloat16)
    expand_local = contract_rows(act_second, grad_expanded)
    grad_pre_second = gelu_back(
        pre_second, jnp.dot(grad_expanded, expand_weight.T, preferred_element_type=jnp.float32)
    )
    shift_second_grad, gain_second_grad = norm_sums(grad_pre_second, normed_second)
    grad_conved = normalize_back(
        grad_pre_second,
        normed_second,
        rstd_second,
        gain_second,
        shift_second_grad,
        gain_second_grad,
    ).astype(jnp.bfloat16)
    spatial_local = contract_rows(cols_first, grad_conved)
    grad_act_first = columns_back(
        jnp.dot(grad_conved, spatial_weight.T, preferred_element_type=jnp.float32), neck_width
    )
    grad_pre_first = gelu_back(pre_first, grad_act_first)
    shift_first_grad, gain_first_grad = norm_sums(grad_pre_first, normed_first)
    grad_reduced = normalize_back(
        grad_pre_first, normed_first, rstd_first, gain_first, shift_first_grad, gain_first_grad
    ).astype(jnp.bfloat16)
    reduce_local = contract_rows(pixels, grad_reduced)
    canvas_grad = (
        (jnp.dot(grad_reduced, reduce_weight.T, preferred_element_type=jnp.float32) + grad_pre_out)
        .astype(jnp.bfloat16)
        .reshape(canvas.shape)
    )
    proto_part = lax.psum_scatter(proto_local, "in", scatter_dimension=1, tiled=True)
    prototypes_grad = lax.psum(proto_part, "grp")
    embed_grad = lax.psum_scatter(
        lax.psum_scatter(embed_local, "in", scatter_dimension=1, tiled=True),
        "grp",
        scatter_dimension=0,
        tiled=True,
    )
    hidden_grad = scatter_sum(blocked(hidden_local))
    expand_grad = scatter_sum(blocked(expand_local))
    spatial_grad = scatter_sum(blocked(spatial_local))
    reduce_grad = scatter_sum(blocked(reduce_local))
    return (
        crop_loss.reshape(canvases, CROPS),
        canvas_grad,
        reduce_grad,
        spatial_grad,
        expand_grad,
        hidden_grad,
        embed_grad,
        embed_bias_grad,
        prototypes_grad,
        gain_first_grad,
        shift_first_grad,
        gain_second_grad,
        shift_second_grad,
        gain_third_grad,
        shift_third_grad,
        gain_head_grad,
        shift_head_grad,
    )


def fold(value, gain, shift, total, count):
    middle = total[0:1] / count
    rstd = lax.rsqrt(total[1:2] / count - middle * middle + BATCH_EPSILON)
    normed = (value - middle) * rstd
    return normed, rstd, normed * gain + shift


def tanh_part(value):
    return jnp.tanh(ROOT * (value + CUBIC * (value * value * value)))


def gelu_of(value):
    return 0.5 * value * (1.0 + tanh_part(value))


def gelu_slope(value):
    bend = tanh_part(value)
    inner = ROOT * (1.0 + (3.0 * CUBIC) * (value * value))
    return 0.5 * (1.0 + bend) + 0.5 * value * (1.0 - bend * bend) * inner


def dot(left, right, dims=((1,), (0,))):
    return lax.dot_general(left, right, (dims, ((), ())), preferred_element_type=jnp.float32)


def column_sums(first, second):
    return jnp.concatenate(
        [jnp.sum(first, 0, keepdims=True), jnp.sum(second, 0, keepdims=True)], 0
    )


def spread(ref, value):
    ref[...] = jnp.broadcast_to(value[None], ref.shape)


def gathered(ref):
    return jnp.sum(ref[...], 0)


def gathered_pair(mine_ref, other_ref):
    return jnp.sum(mine_ref[...], 0) + jnp.sum(other_ref[...], 0)


def pairs():
    side = SIDE // 2
    for vertical in range(3):
        for lateral in range(3):
            here = []
            there = []
            for i in range(side):
                for j in range(side):
                    k = i + vertical - 1
                    m = j + lateral - 1
                    if 0 <= k < side and 0 <= m < side:
                        here.append(i * side + j)
                        there.append(k * side + m)
            yield 3 * vertical + lateral, here, there


def runs(places):
    out = []
    for place in places:
        if out and out[-1][0] + out[-1][1] == place:
            out[-1][1] += 1
        else:
            out.append([place, 1])
    return out


def take(ref, places, rows):
    parts = [ref[first * rows : (first + size) * rows, :] for first, size in runs(places)]
    return parts[0] if len(parts) == 1 else jnp.concatenate(parts, 0)


def add_rows(ref, places, rows, value):
    start = 0
    for first, size in runs(places):
        ref[first * rows : (first + size) * rows, :] += value[start : start + size * rows, :]
        start += size * rows


def tile_places():
    side = SIDE // 2
    for i in range(side):
        for j in range(side):
            yield i * side + j, [(a * side + i, b * side + j) for a in range(2) for b in range(2)]


def reduce_kernel(canvas_ref, weight_ref, pixels_ref, reduced_ref, sums_ref):
    rows = 4 * canvas_ref.shape[2]
    for place, corners in tile_places():
        pixels_ref[place * rows : (place + 1) * rows, :] = jnp.concatenate(
            [canvas_ref[i, j] for i, j in corners], 0
        )
    reduced = dot(pixels_ref[...], weight_ref[...])
    reduced_ref[...] = reduced
    spread(sums_ref, column_sums(reduced, reduced * reduced))


def spatial_kernel(
    count,
    reduced_ref,
    sums_ref,
    gain_ref,
    shift_ref,
    weight_ref,
    total_ref,
    wide_ref,
    conved_ref,
    out_ref,
    act_ref,
):
    neck = reduced_ref.shape[1]
    rows = reduced_ref.shape[0] // 9
    total = gathered(sums_ref)
    total_ref[...] = total
    pre = fold(reduced_ref[...], gain_ref[...], shift_ref[...], total, count)[2]
    act = gelu_of(pre).astype(jnp.bfloat16)
    act_ref[...] = act
    wide_ref[...] = act.astype(jnp.float32)
    for offset, here, there in sorted(pairs(), key=lambda p: p[0] != 4):
        part = dot(take(act_ref, there, rows), weight_ref[offset * neck : (offset + 1) * neck, :])
        if offset == 4:
            conved_ref[...] = part
        else:
            add_rows(conved_ref, here, rows, part)
    conved = conved_ref[...]
    spread(out_ref, column_sums(conved, conved * conved))


def expand_kernel(
    count, conved_ref, sums_ref, gain_ref, shift_ref, weight_ref, total_ref, act_ref, expanded_ref, out_ref
):
    total = gathered(sums_ref)
    total_ref[...] = total
    pre = fold(conved_ref[...], gain_ref[...], shift_ref[...], total, count)[2]
    act = gelu_of(pre).astype(jnp.bfloat16)
    act_ref[...] = act
    expanded = dot(act, weight_ref[...])
    expanded_ref[...] = expanded
    spread(out_ref, column_sums(expanded, expanded * expanded))


def pool_kernel(
    count,
    expanded_ref,
    mine_ref,
    other_ref,
    gain_ref,
    shift_ref,
    pixels_ref,
    weight_ref,
    total_ref,
    pooled_ref,
    head_ref,
    out_ref,
):
    step = pl.program_id(0)
    rows = expanded_ref.shape[0] // 9
    total = gathered_pair(mine_ref, other_ref)
    total_ref[...] = total
    pooled = None
    for place in range(9):
        block = slice(place * rows, (place + 1) * rows)
        pre = fold(expanded_ref[block, :], gain_ref[...], shift_ref[...], total, count)[2]
        part = gelu_of(pre + pixels_ref[block, :].astype(jnp.float32))
        pooled = part if pooled is None else pooled + part
    pooled = (pooled / 9.0).astype(jnp.bfloat16)
    pooled_ref[...] = pooled.astype(jnp.float32)
    head = dot(pooled, weight_ref[...])

    @pl.when(step == 0)
    def _():
        head_ref[...] = head

    @pl.when(step > 0)
    def _():
        head_ref[...] += head

    @pl.when(step == pl.num_programs(0) - 1)
    def _():
        value = head_ref[...]
        spread(out_ref, column_sums(value, value * value))


def score_kernel(
    count,
    protos,
    head_ref,
    mine_ref,
    other_ref,
    gain_ref,
    shift_ref,
    embed_ref,
    bias_ref,
    proto_ref,
    queued_ref,
    total_ref,
    act_ref,
    embedded_ref,
    scores_ref,
    mass_ref,
    out_ref,
):
    total = gathered_pair(mine_ref, other_ref)
    total_ref[...] = total
    pre = fold(head_ref[...], gain_ref[...], shift_ref[...], total, count)[2]
    act = gelu_of(pre).astype(jnp.bfloat16)
    act_ref[...] = act
    embedded = dot(act, embed_ref[...]) + bias_ref[...]
    embedded_ref[...] = embedded
    rnorm = lax.rsqrt(jnp.sum(embedded * embedded, 1, keepdims=True) + UNIT_EPSILON)
    unit = (embedded * rnorm).astype(jnp.bfloat16)
    crops = unit.shape[0]
    scores = dot(unit, proto_ref[...], ((1,), (1,)))
    scores_ref[...] = scores
    queue = dot(queued_ref[...], proto_ref[...], ((1,), (1,)))
    shape = scores.shape
    inside = lax.broadcasted_iota(jnp.int32, shape, 1) < protos
    mass = jnp.where(inside, jnp.exp(scores / TRANSPORT_SMOOTH), 0.0)
    mass_ref[0:crops, :] = mass
    queue_inside = lax.broadcasted_iota(jnp.int32, queue.shape, 1) < protos
    queue_mass = jnp.where(queue_inside, jnp.exp(queue / TRANSPORT_SMOOTH), 0.0)
    real = queue.shape[0]
    mass_ref[crops:, :] = jnp.zeros((mass_ref.shape[0] - crops, shape[1]), jnp.float32)
    mass_ref[crops : crops + real, :] = queue_mass
    spread(out_ref, jnp.sum(mass, 0, keepdims=True) + jnp.sum(queue_mass, 0, keepdims=True))


def balance(protos, mass, column):
    inside = lax.broadcasted_iota(jnp.int32, column.shape, 1) < protos
    mass = mass / jnp.where(inside, column, 1.0)
    row = jnp.sum(mass, 1, keepdims=True)
    return mass, row


def sweep_kernel(protos, real, mass_ref, mine_ref, other_ref, next_ref, out_ref):
    mass, row = balance(protos, mass_ref[...], gathered_pair(mine_ref, other_ref))
    used = lax.broadcasted_iota(jnp.int32, row.shape, 0) < real
    mass = mass / jnp.where(used, row, 1.0)
    next_ref[...] = mass
    spread(out_ref, jnp.sum(mass, 0, keepdims=True))


def loss_kernel(
    count,
    protos,
    mass_ref,
    mine_ref,
    other_ref,
    here_ref,
    wanted_ref,
    held_ref,
    scores_ref,
    embedded_ref,
    proto_ref,
    act_ref,
    embed_ref,
    head_ref,
    head_total_ref,
    gain_ref,
    shift_ref,
    loss_ref,
    keep_ref,
    send_ref,
    upstream_ref,
    out_ref,
):
    crops = scores_ref.shape[0]
    width = scores_ref.shape[1]
    mass, row = balance(protos, mass_ref[0:crops, :], gathered_pair(mine_ref, other_ref))
    codes = mass / row
    size = crops // CROPS
    row_place = lax.broadcasted_iota(jnp.int32, (crops, crops), 0) % size
    column_place = lax.broadcasted_iota(jnp.int32, (crops, crops), 1) % size
    chosen = (wanted_ref[...] == held_ref[...]) & (row_place == column_place)
    target = lax.dot_general(
        jnp.where(chosen, 1.0, 0.0),
        codes,
        (((1,), (0,)), ((), ())),
        precision=PRECISE,
        preferred_element_type=jnp.float32,
    )
    logits = scores_ref[...] / SOFTMAX_WARMTH
    inside = lax.broadcasted_iota(jnp.int32, logits.shape, 1) < protos
    top = jnp.max(jnp.where(inside, logits, -3.0e38), 1, keepdims=True)
    mass_of = jnp.where(inside, jnp.exp(logits - top), 0.0)
    log_total = jnp.log(jnp.sum(mass_of, 1, keepdims=True)) + top
    loss_ref[...] = -jnp.sum(target * (logits - log_total), 1, keepdims=True)
    share = jnp.sum(target, 1, keepdims=True)
    soft = jnp.where(inside, jnp.exp(logits - log_total), 0.0)
    grad_scores = ((soft * share - target) / SOFTMAX_WARMTH).astype(jnp.bfloat16)
    embedded = embedded_ref[...]
    rnorm = lax.rsqrt(jnp.sum(embedded * embedded, 1, keepdims=True) + UNIT_EPSILON)
    unit = embedded * rnorm
    grad_unit = dot(grad_scores, proto_ref[...])
    grad_embedded = rnorm * (grad_unit - unit * jnp.sum(grad_unit * unit, 1, keepdims=True))
    grad_low = grad_embedded.astype(jnp.bfloat16)
    proto_local = dot(unit.astype(jnp.bfloat16), grad_scores, ((0,), (0,)))
    embed_local = dot(grad_low, act_ref[...], ((0,), (0,)))
    across, outer, rows = keep_ref.shape[:3]
    first = width // outer
    second = embed_local.shape[1] // outer
    flip = here_ref[0] == 1
    for k in range(across):
        lines = [slice((2 * k + c) * rows, (2 * k + c + 1) * rows) for c in range(2)]
        for m in range(outer):
            for value, size, start in ((proto_local, first, 0), (embed_local, second, first)):
                even, odd = (value[line, m * size : (m + 1) * size] for line in lines)
                keep_ref[k, m, :, start : start + size] = jnp.where(flip, odd, even)
                send_ref[k, m, :, start : start + size] = jnp.where(flip, even, odd)
    total = head_total_ref[...]
    normed, _, pre = fold(head_ref[...], gain_ref[...], shift_ref[...], total, count)
    upstream = gelu_slope(pre) * dot(grad_low, embed_ref[...], ((1,), (1,)))
    upstream_ref[...] = upstream
    bias = jnp.sum(grad_embedded, 0, keepdims=True)
    sums = jnp.concatenate([column_sums(upstream, upstream * normed), jnp.concatenate([bias, bias], 0)], 1)
    spread(out_ref, sums)


def split_columns(value, here_ref, near_ref, away_ref):
    part = near_ref.shape[2]
    blocks = [value[:, k * part : (k + 1) * part] for k in range(4)]
    core = here_ref[0] == 1
    chip = here_ref[1] == 1
    for k in range(2):
        first = jnp.where(core, blocks[1 - k], blocks[k])
        second = jnp.where(core, blocks[3 - k], blocks[2 + k])
        near_ref[k] = jnp.where(chip, second, first)
        away_ref[k] = jnp.where(chip, first, second)


def norm_back(upstream, normed, rstd, gain, total, count):
    return gain * rstd * (upstream - total[0:1] / count - normed * (total[1:2] / count))


def head_back_kernel(
    count,
    upstream_ref,
    mine_ref,
    other_ref,
    head_ref,
    head_total_ref,
    gain_ref,
    shift_ref,
    here_ref,
    sums_ref,
    low_ref,
    near_ref,
    away_ref,
):
    total = gathered_pair(mine_ref, other_ref)
    sums_ref[...] = total
    width = head_ref.shape[1]
    stats = head_total_ref[...]
    normed, rstd, _ = fold(head_ref[...], gain_ref[...], shift_ref[...], stats, count)
    grad = norm_back(upstream_ref[...], normed, rstd, gain_ref[...], total[:, 0:width], count)
    low = grad.astype(jnp.bfloat16)
    low_ref[...] = low
    split_columns(low.astype(jnp.float32), here_ref, near_ref, away_ref)


def pool_back_kernel(
    count,
    grad_ref,
    weight_ref,
    expanded_ref,
    total_ref,
    gain_ref,
    shift_ref,
    pixels_ref,
    upstream_ref,
    out_ref,
):
    rows = expanded_ref.shape[0] // 9
    total = total_ref[...]
    grad_output = dot(grad_ref[...], weight_ref[...], ((1,), (1,))) / 9.0
    first = None
    second = None
    for place in range(9):
        block = slice(place * rows, (place + 1) * rows)
        normed, _, pre = fold(expanded_ref[block, :], gain_ref[...], shift_ref[...], total, count)
        upstream = gelu_slope(pre + pixels_ref[block, :].astype(jnp.float32)) * grad_output
        upstream_ref[block, :] = upstream.astype(jnp.bfloat16)
        weighted = upstream * normed
        first = upstream if first is None else first + upstream
        second = weighted if second is None else second + weighted
    spread(out_ref, column_sums(first, second))


def expand_back_kernel(
    count,
    upstream_ref,
    back_mine_ref,
    back_other_ref,
    expanded_ref,
    total_ref,
    gain_ref,
    weight_ref,
    act_ref,
    conved_ref,
    conved_sums_ref,
    conved_gain_ref,
    conved_shift_ref,
    here_ref,
    sums_ref,
    keep_ref,
    send_ref,
    next_ref,
    out_ref,
):
    step = pl.program_id(0)
    back = gathered_pair(back_mine_ref, back_other_ref)
    sums_ref[...] = back
    stats = total_ref[...]
    normed, rstd, _ = fold(expanded_ref[...], gain_ref[...], 0.0, stats, count)
    grad = norm_back(
        upstream_ref[...].astype(jnp.float32), normed, rstd, gain_ref[...], back, count
    ).astype(jnp.bfloat16)
    part = dot(grad, weight_ref[...], ((1,), (1,)))
    value = dot(act_ref[...], grad, ((0,), (0,)))
    half = value.shape[1] // 2
    flip = here_ref[0] == 1
    keep_ref[0] = jnp.where(flip, value[:, half:], value[:, :half])
    send_ref[0] = jnp.where(flip, value[:, :half], value[:, half:])

    @pl.when(step == 0)
    def _():
        next_ref[...] = part

    @pl.when(step > 0)
    def _():
        next_ref[...] += part

    @pl.when(step == pl.num_programs(0) - 1)
    def _():
        conved, _, pre = fold(
            conved_ref[...], conved_gain_ref[...], conved_shift_ref[...], conved_sums_ref[...], count
        )
        upstream = gelu_slope(pre) * next_ref[...]
        next_ref[...] = upstream
        spread(out_ref, column_sums(upstream, upstream * conved))


def conved_back_kernel(
    count,
    upstream_ref,
    back_ref,
    conved_ref,
    sums_ref,
    gain_ref,
    here_ref,
    total_ref,
    low_ref,
    near_ref,
    away_ref,
):
    back = gathered(back_ref)
    total_ref[...] = back
    normed, rstd, _ = fold(conved_ref[...], gain_ref[...], 0.0, sums_ref[...], count)
    low = norm_back(upstream_ref[...], normed, rstd, gain_ref[...], back, count).astype(jnp.bfloat16)
    low_ref[...] = low
    split_columns(low.astype(jnp.float32), here_ref, near_ref, away_ref)


def spatial_back_kernel(
    count,
    low_ref,
    weight_ref,
    reduced_ref,
    reduced_sums_ref,
    reduced_gain_ref,
    reduced_shift_ref,
    next_ref,
    out_ref,
):
    neck = reduced_ref.shape[1]
    rows = reduced_ref.shape[0] // 9
    for offset, here, there in sorted(pairs(), key=lambda p: p[0] != 4):
        value = dot(
            take(low_ref, here, rows), weight_ref[offset * neck : (offset + 1) * neck, :], ((1,), (1,))
        )
        if offset == 4:
            next_ref[...] = value
        else:
            add_rows(next_ref, there, rows, value)
    reduced, _, pre = fold(
        reduced_ref[...], reduced_gain_ref[...], reduced_shift_ref[...], reduced_sums_ref[...], count
    )
    upstream = gelu_slope(pre) * next_ref[...]
    next_ref[...] = upstream
    spread(out_ref, column_sums(upstream, upstream * reduced))


def spatial_weight_kernel(
    here_ref, act_ref, near_ref, away_ref, core_ref, keep_ref, send_ref, left_ref, right_ref
):
    devices = act_ref.shape[0]
    rows = act_ref.shape[1] // 9
    neck = act_ref.shape[2]
    me = here_ref[0] + 2 * here_ref[1]
    grads = (near_ref, core_ref, away_ref, core_ref)
    for k in range(devices):
        source = me ^ k
        for place in range(9):
            block = slice(place * rows, (place + 1) * rows)
            goal = slice((place * devices + k) * rows, (place * devices + k + 1) * rows)
            left_ref[goal, :] = act_ref[source, block, :].astype(jnp.bfloat16)
            right_ref[goal, :] = grads[k][k // 2 if k % 2 else 0, block, :].astype(jnp.bfloat16)
    size = keep_ref.shape[1]
    mine = here_ref[2]
    for offset, here, there in pairs():
        value = dot(
            take(right_ref, here, rows * devices), take(left_ref, there, rows * devices), ((0,), (0,))
        ).T
        start = offset * neck
        end = start + neck
        while start < end:
            owner = start // size
            stop = min(end, (owner + 1) * size)
            piece = value[start - offset * neck : stop - offset * neck, :]
            lines = slice(start - owner * size, stop - owner * size)

            @pl.when(mine == owner % 2)
            def _():
                keep_ref[owner // 2, lines, :] = piece

            @pl.when(mine != owner % 2)
            def _():
                send_ref[owner // 2, lines, :] = piece

            start = stop


def hidden_weight_kernel(here_ref, pooled_ref, near_ref, y_ref, x_ref, xy_ref, core_ref, out_ref):
    deep, size, _ = out_ref.shape
    me = here_ref[0] + 2 * here_ref[1] + 4 * here_ref[2]
    places = [(0, near_ref, 0), (4, y_ref, 0), (2, x_ref, 0), (6, xy_ref, 0)]
    places += [(1, core_ref, 0), (5, core_ref, 1), (3, core_ref, 2), (7, core_ref, 3)]
    right = jnp.concatenate([ref[k].astype(jnp.bfloat16) for _, ref, k in places], 0)
    for m in range(deep):
        start = pl.multiple_of((2 * m + here_ref[2]) * size, size)
        left = jnp.concatenate(
            [pooled_ref[me ^ mask, :, pl.ds(start, size)].astype(jnp.bfloat16) for mask, _, _ in places], 0
        )
        out_ref[m] = dot(left, right, ((0,), (0,)))


def half_kernel(here_ref, keep_ref, come_ref, mine_ref, other_ref):
    mine = here_ref[1]
    mine_ref[...] = keep_ref[mine] + come_ref[mine]
    other_ref[...] = keep_ref[1 - mine] + come_ref[1 - mine]


def cut_kernel(here_ref, keep_ref, come_ref, mine_ref, *other_refs):
    mine = here_ref[2]
    for x, other_ref in enumerate(other_refs):
        for k in range(mine_ref.shape[1]):
            mine_ref[x, k] = keep_ref[x, 2 * k + mine] + come_ref[x, 2 * k + mine]
            other_ref[k] = keep_ref[x, 2 * k + 1 - mine] + come_ref[x, 2 * k + 1 - mine]


def join_kernel(here_ref, keep_ref, first_ref, second_ref, mine_ref, other_ref):
    mine = here_ref[1]
    flip = mine == 1
    first = first_ref[...]
    second = second_ref[...]
    mine_ref[...] = keep_ref[mine] + jnp.where(flip, second, first)
    other_ref[...] = keep_ref[1 - mine] + jnp.where(flip, first, second)


def side_kernel(here_ref, keep_ref, come_ref, mine_ref, other_ref):
    mine = here_ref[2]
    for k in range(mine_ref.shape[0]):
        mine_ref[k] = keep_ref[2 * k + mine] + come_ref[2 * k + mine]
        other_ref[k] = keep_ref[2 * k + 1 - mine] + come_ref[2 * k + 1 - mine]


def across_kernel(here_ref, keep_ref, come_ref, *out_refs):
    deep = out_refs[0].shape[0]
    for m, out_ref in enumerate(out_refs):
        column = here_ref[1] ^ (m & 1)
        side = here_ref[2] ^ (m >> 1)
        for k in range(deep):
            out_ref[k] = keep_ref[column, 2 * k + side] + come_ref[column, 2 * k + side]


def along_kernel(here_ref, *refs):
    deep = refs[0].shape[0]
    ins, outs = refs[:-deep], refs[-deep:]
    for m, out_ref in enumerate(outs):
        place = here_ref[3] ^ m
        total = ins[0][place]
        for ref in ins[1:]:
            total = total + ref[place]
        out_ref[...] = total


def reduce_back_kernel(
    count,
    upstream_ref,
    back_ref,
    reduced_ref,
    sums_ref,
    gain_ref,
    pixels_ref,
    here_ref,
    total_ref,
    low_ref,
    keep_ref,
    send_ref,
):
    back = gathered(back_ref)
    total_ref[...] = back
    normed, rstd, _ = fold(reduced_ref[...], gain_ref[...], 0.0, sums_ref[...], count)
    low = norm_back(upstream_ref[...], normed, rstd, gain_ref[...], back, count).astype(jnp.bfloat16)
    low_ref[...] = low
    part = keep_ref.shape[2]
    value = dot(pixels_ref[...], low, ((0,), (0,)))
    flip = here_ref[0] == 1
    for k in range(keep_ref.shape[0]):
        even = value[:, 2 * k * part : (2 * k + 1) * part]
        odd = value[:, (2 * k + 1) * part : (2 * k + 2) * part]
        keep_ref[k] = jnp.where(flip, odd, even)
        send_ref[k] = jnp.where(flip, even, odd)


def canvas_kernel(low_ref, weight_ref, upstream_ref, out_ref):
    rows = low_ref.shape[0] // 9
    size = out_ref.shape[2]
    value = dot(low_ref[...], weight_ref[...], ((1,), (1,))) + upstream_ref[...].astype(jnp.float32)
    value = value.astype(jnp.bfloat16)
    for place, corners in tile_places():
        for k, (i, j) in enumerate(corners):
            start = place * rows + k * size
            out_ref[i, j] = value[start : start + size, :]


MADE = []
SCALARS = pl.BlockSpec(memory_space=pltpu.SMEM)
ARRAY = pl.BlockSpec(memory_space=pltpu.VMEM)


def run(kernel, outs, args, scratch=(), flops=0, moved=0, after=(), free=(), **grid):
    if "grid" not in grid:
        kinds = [SCALARS if a.ndim == 1 and a.dtype == jnp.int32 else ARRAY for a in args]
        grid["in_specs"] = kinds
    if len(after) > 0:
        inner = kernel
        count = len(args)
        grid["in_specs"] = list(grid["in_specs"]) + [pl.BlockSpec(memory_space=pl.ANY)] * len(after)
        args = tuple(args) + tuple(after)
        skip = len(after)

        def kernel(*refs):
            inner(*refs[:count], *refs[count + skip :])

    loose = grid.pop("loose", ())
    args = [
        a
        if (a.ndim == 1 and a.dtype == jnp.int32)
        or any(a is other for other in (*loose, *after))
        or any(a is other for other in MADE)
        else pinned(a)
        for a in args
    ]
    made = pl.pallas_call(
        kernel,
        out_shape=outs,
        scratch_shapes=list(scratch),
        compiler_params=pltpu.CompilerParams(vmem_limit_bytes=VMEM_BYTES),
        cost_estimate=pl.CostEstimate(flops=1, bytes_accessed=1, transcendentals=0),
        **grid,
    )(*args)
    for out, value in zip(jax.tree.leaves(outs), jax.tree.leaves(made)):
        if out.memory_space == pltpu.VMEM:
            MADE.append(value)
    return made


def f32(*shape):
    return pltpu.HBM(shape, jnp.float32)


def b16(*shape):
    return pltpu.HBM(shape, jnp.bfloat16)


def near32(*shape):
    return pltpu.VMEM(shape, jnp.float32)


def near16(*shape):
    return pltpu.VMEM(shape, jnp.bfloat16)


def to_all(block):
    return lax.all_to_all(block, AXES, 0, 0, tiled=True)


def to_all_pair(block):
    count = lax.axis_size("grp") * lax.axis_size("in")
    groups = [list(range(k, count, 2)) for k in range(2)]
    mine = lax.all_to_all(block, AXES, 0, 0, tiled=True, axis_index_groups=groups)
    return mine, swap_bit(mine, 0)


def pick(value, bit, axis=0):
    mine = lax.dynamic_index_in_dim(value, my_bit(bit), axis, keepdims=False)
    other = lax.dynamic_index_in_dim(value, 1 - my_bit(bit), axis, keepdims=False)
    return mine, other


def teams(bits):
    count = lax.axis_size("grp") * lax.axis_size("in")
    spans = [0]
    for bit in bits:
        spans = spans + [m | (1 << bit) for m in spans]
    used = sum(1 << bit for bit in bits)
    return [[base | m for m in sorted(spans)] for base in range(count) if base & used == 0]


def pinned(value):
    return pltpu.with_memory_space_constraint(value, pltpu.HBM)


def swap_mask(value, mask):
    count = lax.axis_size("grp") * lax.axis_size("in")
    return lax.ppermute(value, AXES, [(i, i ^ mask) for i in range(count)])


def spread_plane(here, keep, come):
    deep = keep.shape[1] // 2
    parts = run(across_kernel, (f32(deep, *keep.shape[2:]),) * 4, (here, keep, come), moved=4 * keep.size * 3, loose=(come,))
    return [parts[0]] + [
        swap_mask(pinned(parts[m]), 2 * m) for m in range(1, 4)
    ]


def spread_line(here, parts):
    deep = parts[0].shape[0]
    shape = parts[0].shape[1:]
    cut = run(
        along_kernel,
        (f32(*shape),) * deep,
        (here, *parts),
        moved=4 * parts[0].size * (len(parts) + 1),
    )
    return [cut[0]] + [swap_mask(cut[m], 8 * m) for m in range(1, deep)]


def together(*values):
    return lax.optimization_barrier(values)


def total_of(parts):
    value = parts[0]
    for part in parts[1:]:
        value = value + part
    return value


def fast(
    canvas,
    reduce_weight,
    gain_first,
    shift_first,
    spatial_weight,
    gain_second,
    shift_second,
    expand_weight,
    gain_third,
    shift_third,
    hidden_weight,
    gain_head,
    shift_head,
    embed_weight,
    embed_bias,
    prototypes,
    queued,
    crop_ids,
    partner,
):
    MADE.clear()
    inner = lax.axis_size("in")
    outer = lax.axis_size("grp")
    devices = inner * outer
    low_bits = bits_of("in")
    canvases = canvas.shape[0]
    channels = canvas.shape[-1]
    neck = reduce_weight.shape[1]
    hidden = hidden_weight.shape[1]
    width = embed_weight.shape[1]
    rows = canvases * SIDE * SIDE
    crops = canvases * CROPS
    protos = prototypes.shape[0]
    wide = -(-protos // (128 * outer)) * 128 * outer
    count = float(rows * devices)
    crop_count = float(crops * devices)
    gain_first, shift_first, gain_second, shift_second = (
        v.reshape(1, -1) for v in (gain_first, shift_first, gain_second, shift_second)
    )
    gain_third, shift_third, gain_head, shift_head, embed_bias = (
        v.reshape(1, -1) for v in (gain_third, shift_third, gain_head, shift_head, embed_bias)
    )
    proto_wide = jnp.pad(prototypes, ((0, wide - protos), (0, 0)))
    field = canvas.transpose(1, 2, 0, 3)

    index = lax.axis_index("grp") * inner + lax.axis_index("in")
    here = jnp.stack([index & 1, (index >> 1) & 1, (index >> 2) & 1, index >> 3]).astype(jnp.int32)
    quadrants = crop_ids[:, :: SIDE // 2, :: SIDE // 2].reshape(canvases, CROPS).T
    wanted = jnp.sum(
        (quadrants[:, None, :] == jnp.arange(CROPS, dtype=jnp.int32)[None, :, None])
        * partner.T[None, :, :],
        1,
    ).reshape(crops, 1)
    held = quadrants.reshape(1, crops)

    pixels, reduced, sums = run(
        reduce_kernel,
        (near16(rows, channels), f32(rows, neck), near32(devices, 2, neck)),
        (field, reduce_weight),
        flops=2 * rows * channels * neck,
        moved=12_000_000,
    )
    first_sums = to_all(sums)
    first_total, act_wide, conved, sums = run(
        functools.partial(spatial_kernel, count),
        (near32(2, neck), f32(rows, neck), f32(rows, neck), near32(devices, 2, neck)),
        (reduced, first_sums, gain_first, shift_first, spatial_weight),
        loose=(first_sums, spatial_weight),
        scratch=[pltpu.VMEM((rows, neck), jnp.bfloat16)],
        flops=11 * rows * neck * neck,
        moved=12_000_000,
    )
    act_all = lax.all_gather(act_wide, "in")
    second_sums = to_all(sums)
    second_total, act_second, expanded, sums = run(
        functools.partial(expand_kernel, count),
        (near32(2, neck), near16(rows, neck), f32(rows, channels), near32(devices // 2, 2, channels)),
        (conved, second_sums, gain_second, shift_second, expand_weight),
        loose=(second_sums, expand_weight),
        flops=2 * rows * channels * neck,
        moved=12_000_000,
    )
    third_mine, third_other = to_all_pair(sums)
    block = channels // outer
    chunk = 2 * block
    chunks = channels // chunk
    columns = lambda n: pl.BlockSpec((n, chunk), lambda k: (0, k))
    stats = lambda n: pl.BlockSpec((n, 2, chunk), lambda k: (0, 0, k))
    whole = lambda *shape: pl.BlockSpec(shape, lambda k: (0,) * len(shape))
    third_total, pooled, head_pre, sums = run(
        functools.partial(pool_kernel, count),
        (near32(2, channels), f32(crops, channels), f32(crops, hidden), near32(devices // 2, 2, hidden)),
        (expanded, third_mine, third_other, gain_third, shift_third, pixels, hidden_weight),
        loose=(third_mine, third_other),
        flops=2 * crops * channels * hidden,
        moved=18_000_000,
        grid=(chunks,),
        in_specs=[
            columns(rows),
            stats(devices // 2),
            stats(devices // 2),
            columns(1),
            columns(1),
            columns(rows),
            pl.BlockSpec((chunk, hidden), lambda k: (k, 0)),
        ],
        out_specs=[
            columns(2),
            columns(crops),
            whole(crops, hidden),
            whole(devices // 2, 2, hidden),
        ],
    )
    pooled_all = lax.all_gather(pooled, AXES, axis_index_groups=teams(range(low_bits + 1)))
    head_mine, head_other = to_all_pair(sums)
    real = crops + queued.shape[0]
    mass_rows = -(-real // 8) * 8
    head_total, act_head, embedded, scores, mass, sums = run(
        functools.partial(score_kernel, crop_count, protos),
        (
            near32(2, hidden),
            near16(crops, hidden),
            f32(crops, width),
            f32(crops, wide),
            near32(mass_rows, wide),
            near32(devices // 2, 1, wide),
        ),
        (
            head_pre,
            head_mine,
            head_other,
            gain_head,
            shift_head,
            embed_weight,
            embed_bias,
            proto_wide,
            queued,
        ),
        loose=(head_mine, head_other, embed_weight, proto_wide),
        flops=2 * crops * width * (hidden + wide),
        moved=6_000_000,
    )
    for _ in range(ITERS - 1):
        column_mine, column_other = to_all_pair(sums)
        mass, sums = run(
            functools.partial(sweep_kernel, protos, real),
            (near32(mass_rows, wide), near32(devices // 2, 1, wide)),
            (mass, column_mine, column_other),
            loose=(column_mine, column_other, mass),
            moved=3_000_000,
        )
    column_mine, column_other = to_all_pair(sums)
    loss, small_keep, small_send, upstream, sums = run(
        functools.partial(loss_kernel, crop_count, protos),
        (
            f32(crops, 1),
            f32(inner // 2, outer, width // inner, (wide + hidden) // outer),
            f32(inner // 2, outer, width // inner, (wide + hidden) // outer),
            f32(crops, hidden),
            near32(devices // 2, 2, hidden + width),
        ),
        (
            mass,
            column_mine,
            column_other,
            here,
            wanted,
            held,
            scores,
            embedded,
            proto_wide,
            act_head,
            embed_weight,
            head_pre,
            head_total,
            gain_head,
            shift_head,
        ),
        loose=(column_mine, column_other, mass),
        flops=6 * crops * width * (hidden + wide),
        moved=9_000_000,
    )
    back_mine, back_other = to_all_pair(sums)
    small = spread_plane(here, small_keep, swap_mask(small_send, 1))
    part = hidden // inner
    head_sums, grad_head, head_near, head_away = run(
        functools.partial(head_back_kernel, crop_count),
        (f32(2, hidden + width), near16(crops, hidden), f32(2, crops, part), f32(2, crops, part)),
        (upstream, back_mine, back_other, head_pre, head_total, gain_head, shift_head, here),
        loose=(back_mine, back_other),
        after=(small[0],),
        moved=3_000_000,
    )
    grad_pre_out, sums = run(
        functools.partial(pool_back_kernel, count),
        (near16(rows, channels), near32(devices // 2, 2, channels)),
        (
            grad_head,
            hidden_weight,
            expanded,
            third_total,
            gain_third,
            shift_third,
            pixels,
        ),
        flops=2 * crops * channels * hidden,
        moved=20_000_000,
        after=(small[0],),
        grid=(chunks,),
        in_specs=[
            whole(crops, hidden),
            pl.BlockSpec((chunk, hidden), lambda k: (k, 0)),
            columns(rows),
            columns(2),
            columns(1),
            columns(1),
            columns(rows),
        ],
        out_specs=[columns(rows), stats(devices // 2)],
    )
    back_mine, back_other = to_all_pair(together(sums, *small[1:])[0])
    part = channels // inner
    columns = lambda n: pl.BlockSpec((n, 2 * part), lambda k: (0, k))
    stats = lambda n: pl.BlockSpec((n, 2, 2 * part), lambda k: (0, 0, k))
    def joined(keep, send, size):
        shape = (inner // 2, outer, size // outer, -1)
        return keep.reshape(shape), swap_mask(send, 1).reshape(shape)

    third_back, expand_keep, expand_send, upstream, sums = run(
        functools.partial(expand_back_kernel, count),
        (
            f32(2, channels),
            f32(inner // 2, neck, part),
            f32(inner // 2, neck, part),
            f32(rows, neck),
            near32(devices, 2, neck),
        ),
        (
            grad_pre_out,
            back_mine,
            back_other,
            expanded,
            third_total,
            gain_third,
            expand_weight,
            act_second,
            conved,
            second_total,
            gain_second,
            shift_second,
            here,
        ),
        flops=4 * rows * channels * neck,
        moved=22_000_000,
        loose=(back_mine, back_other),
        grid=(inner // 2,),
        in_specs=[
            columns(rows),
            stats(devices // 2),
            stats(devices // 2),
            columns(rows),
            columns(2),
            columns(1),
            columns(neck),
            whole(rows, neck),
            whole(rows, neck),
            whole(2, neck),
            whole(1, neck),
            whole(1, neck),
            SCALARS,
        ],
        out_specs=[
            columns(2),
            pl.BlockSpec((1, neck, part), lambda k: (k, 0, 0)),
            pl.BlockSpec((1, neck, part), lambda k: (k, 0, 0)),
            whole(rows, neck),
            whole(devices, 2, neck),
        ],
    )
    back = to_all(sums)
    moved = [head_near] + [
        swap_mask(v, mask) for v, mask in ((head_near, 4), (head_away, 2), (head_away, 6))
    ]
    core_grads = swap_mask(jnp.stack([v[1] for v in moved]), 1)
    keep, come = joined(expand_keep, expand_send, neck)
    shape = (outer // 2, *keep.shape[2:])
    expand_kept, *expand_sent = run(
        cut_kernel, (f32(inner // 2, *shape), f32(*shape), f32(*shape)), (here, keep, come), loose=(come,)
    )
    expand_first = swap_mask(pinned(expand_sent[0]), 4)
    second_back, grad_conved, conved_near, conved_away = run(
        functools.partial(conved_back_kernel, count),
        (
            f32(2, neck),
            near16(rows, neck),
            f32(2, rows, neck // inner),
            f32(2, rows, neck // inner),
        ),
        (upstream, back, conved, second_total, gain_second, here),
        loose=(back,),
        after=(expand_sent[0], *moved[1:]),
    )
    away = swap_mask(conved_away, 2)
    expand_second = swap_mask(pinned(expand_sent[1]), 4)
    upstream, sums = run(
        functools.partial(spatial_back_kernel, count),
        (f32(rows, neck), near32(devices, 2, neck)),
        (
            grad_conved,
            spatial_weight,
            reduced,
            first_total,
            gain_first,
            shift_first,
        ),
        loose=(spatial_weight,),
    )
    small = spread_line(here, small)
    hidden_local = run(
        hidden_weight_kernel,
        f32(outer // 2, channels // outer, hidden // inner),
        (here, pooled_all, *moved, core_grads),
        loose=(*moved[1:], core_grads),
        flops=crops * 2 * inner * channels * hidden // inner,
        moved=7_000_000,
    )
    sums, away, expand_first, expand_second, hidden_local, *small = together(
        sums, away, expand_first, expand_second, hidden_local, *small
    )
    small = total_of(small)
    hidden_grad = lax.psum_scatter(
        hidden_local, "grp", axis_index_groups=[list(range(k, outer, 2)) for k in range(2)]
    )
    back = to_all(sums)
    expand_kept, sent = run(
        join_kernel,
        (f32(*expand_kept.shape[1:]),) * 2,
        (here, expand_kept, expand_first, expand_second),
        loose=(expand_first, expand_second),
    )
    expand_come = swap_mask(pinned(sent), 2)
    core = swap_mask(jnp.stack([conved_near[1], away[1]]), 1)
    spatial_keep, spatial_send = run(
        spatial_weight_kernel,
        (f32(outer // 2, 9 * neck // outer, neck // inner),) * 2,
        (here, act_all, conved_near, away, core),
        scratch=[
            pltpu.VMEM((rows * inner, neck), jnp.bfloat16),
            pltpu.VMEM((rows * inner, neck // inner), jnp.bfloat16),
        ],
        after=(sent,),
    )
    spatial_come = swap_mask(pinned(spatial_send), 4)
    first_back, grad_reduced, reduce_keep, reduce_send = run(
        functools.partial(reduce_back_kernel, count),
        (
            f32(2, neck),
            near16(rows, neck),
            f32(inner // 2, channels, neck // inner),
            f32(inner // 2, channels, neck // inner),
        ),
        (upstream, back, reduced, first_total, gain_first, pixels, here),
        loose=(back,),
        flops=2 * rows * channels * neck,
        moved=12_000_000,
        after=(spatial_send,),
    )
    reduce_send, expand_come = together(reduce_send, expand_come)
    keep, come = joined(reduce_keep, reduce_send, channels)
    kept, sent = run(half_kernel, (f32(*keep.shape[1:]),) * 2, (here, keep, come), loose=(come,))
    come = swap_mask(pinned(sent), 2)
    expand_parts = spread_line(here, [expand_kept, expand_come])
    canvas_grad = run(
        canvas_kernel,
        b16(SIDE, SIDE, canvases, channels),
        (grad_reduced, reduce_weight, grad_pre_out),
        after=(sent, expand_parts[0]),
    )
    first = wide // outer
    sent = jnp.broadcast_to(small[None, :, :first], (outer, width // inner, first))
    sent, _ = together(sent, kept)
    sent = lax.all_to_all(sent, "grp", 0, 0, tiled=True)
    come, spatial_come, canvas_grad, sent, hidden_grad, *expand_parts = together(
        come, spatial_come, canvas_grad, sent, hidden_grad, *expand_parts
    )
    kept, other = run(
        side_kernel,
        (f32(kept.shape[0] // 2, *kept.shape[1:]),) * 2,
        (here, kept, come),
        loose=(come,),
    )
    come = swap_mask(pinned(other), 4)
    spatial_parts = spread_line(here, [spatial_keep, spatial_come])
    reduce_parts = spread_line(here, [kept, come])
    ends = together(*reduce_parts, *spatial_parts, *expand_parts)
    deep = outer // 2
    reduce_parts, spatial_parts, expand_parts = ends[:deep], ends[deep : 2 * deep], ends[2 * deep :]
    spatial_grad = total_of(spatial_parts)
    expand_grad = total_of(expand_parts)
    reduce_grad = total_of(reduce_parts)
    canvas_grad = canvas_grad.transpose(2, 0, 1, 3)
    embed_grad = small[:, first:].T
    prototypes_grad = sent.transpose(1, 0, 2).reshape(width // inner, wide)[:, :protos].T
    ids = jnp.arange(CROPS, dtype=jnp.int32)
    crop_loss = jnp.sum(
        (quadrants.T[:, None, :] == ids[None, :, None]) * loss.reshape(CROPS, canvases).T[:, None, :], 2
    )
    return (
        crop_loss,
        canvas_grad,
        reduce_grad,
        spatial_grad,
        expand_grad,
        hidden_grad,
        embed_grad,
        head_sums[0, hidden:],
        prototypes_grad,
        first_back[1],
        first_back[0],
        second_back[1],
        second_back[0],
        third_back[1],
        third_back[0],
        head_sums[1, :hidden],
        head_sums[0, :hidden],
    )


def solution(mesh):
    placed = (
        P(("grp", "in"), None, None, None),
        P(),
        P(),
        P(),
        P(),
        P(),
        P(),
        P(),
        P(),
        P(),
        P(),
        P(),
        P(),
        P(),
        P(),
        P(),
        P(("grp", "in"), None),
        P(("grp", "in"), None, None),
        P(("grp", "in"), None),
    )
    lanes = 128 * mesh.shape["grp"]
    aligned = mesh.shape["in"] * 128 <= 512 and lanes * 2 <= 2048
    return jax.shard_map(
        fast if aligned else on_device,
        mesh=mesh,
        in_specs=placed,
        out_specs=(
            P(("grp", "in"), None),
            P(("grp", "in"), None, None, None),
            P("grp", "in"),
            P("grp", "in"),
            P("grp", "in"),
            P("grp", "in"),
            P("grp", "in"),
            P(),
            P(None, "in"),
            P(),
            P(),
            P(),
            P(),
            P(),
            P(),
            P(),
            P(),
        ),
        check_vma=False,
    )
```

```python
import functools

import jax
import jax.numpy as jnp
from jax import lax
from jax.experimental import pallas as pl
from jax.experimental.pallas import tpu as pltpu
from jax.sharding import PartitionSpec as P

SIDE = 6
CROPS = 4
ITERS = 3


BATCH_EPSILON = 1e-05
UNIT_EPSILON = 1e-06
SOFTMAX_WARMTH = 0.1
TRANSPORT_SMOOTH = 0.05
PRECISE = lax.Precision.HIGHEST
ROOT = 0.7978845608028654
CUBIC = 0.044715
VMEM_BYTES = 48 * 1024 * 1024


AXES = ("grp", "in")


def bits_of(axis):
    return lax.axis_size(axis).bit_length() - 1


def swap_bit(value, bit):
    count = lax.axis_size("grp") * lax.axis_size("in")
    return lax.ppermute(value, AXES, [(i, i ^ (1 << bit)) for i in range(count)])


def my_bit(bit):
    index = lax.axis_index("grp") * lax.axis_size("in") + lax.axis_index("in")
    return (index >> bit) & 1


def exchange_sum(block, groups):
    size = len(groups[0])
    spread = jnp.broadcast_to(block[None], (size,) + block.shape)
    moved = lax.all_to_all(spread, AXES, 0, 0, tiled=True, axis_index_groups=groups)
    return jnp.sum(moved, 0)


def all_sum(parts):
    count = lax.axis_size("grp") * lax.axis_size("in")
    sizes = [part.size for part in parts]
    flat = jnp.concatenate([part.reshape(-1) for part in parts])
    total = sum(sizes)
    small = total <= 1536
    unit = 1024 if small else 2048
    rows = -(-total // unit) * unit // 128
    flat = jnp.pad(flat, (0, rows * 128 - total)).reshape(rows, 128)
    if small:
        flat = exchange_sum(flat, [list(range(count))])
    else:
        core = my_bit(0)
        halves = flat.reshape(2, rows // 2, 128)
        mine = lax.dynamic_index_in_dim(halves, core, 0, keepdims=False)
        other = lax.dynamic_index_in_dim(halves, 1 - core, 0, keepdims=False)
        mine = mine + swap_bit(other, 0)
        mine = exchange_sum(mine, [list(range(k, count, 2)) for k in range(2)])
        other = swap_bit(mine, 0)
        flat = jnp.concatenate(
            [jnp.where(core == 0, mine, other), jnp.where(core == 0, other, mine)], 0
        )
    flat = flat.reshape(-1)
    sums = []
    start = 0
    for part, size in zip(parts, sizes):
        sums.append(flat[start : start + size].reshape(part.shape))
        start += size
    return sums


def scatter_sum(blocks, splits=2):
    low = bits_of("in")
    high = bits_of("grp")
    count = low + high
    rows = blocks.shape[2]
    columns = blocks.shape[3]
    inner = list(range(low))
    outer = list(range(low, count))
    orders = [inner + outer, inner[:1] + outer + inner[1:]][:splits]
    chunks = []
    for k, order in enumerate(orders):
        piece = blocks[:, :, k * (rows // splits) : (k + 1) * (rows // splits)]
        chunks.append((piece.reshape((2,) * count + (rows // splits, columns)), order))
    left = [list(inner[::-1] + outer[::-1]) for _ in orders]
    for stage in range(count):
        following = []
        for k, (piece, order) in enumerate(chunks):
            bit = order[stage]
            place = left[k].index(bit)
            left[k].remove(bit)
            mine = lax.dynamic_index_in_dim(piece, my_bit(bit), place, keepdims=False)
            other = lax.dynamic_index_in_dim(piece, 1 - my_bit(bit), place, keepdims=False)
            following.append((mine + swap_bit(other, bit), order))
        chunks = following
    return jnp.concatenate([piece for piece, _ in chunks], 0)


def blocked(grad):
    rows, columns = grad.shape
    inner = lax.axis_size("in")
    outer = lax.axis_size("grp")
    return grad.reshape(outer, rows // outer, inner, columns // inner).transpose(2, 0, 1, 3)


def contract_rows(left, right):
    return lax.dot_general(
        left, right, (((0,), (0,)), ((), ())), preferred_element_type=jnp.float32
    )


def gelu_back(before, upstream):
    ignored, backward = jax.vjp(jax.nn.gelu, before)
    return backward(upstream)[0]


def normalize(value, gain, shift):
    count = value.shape[0] * lax.axis_size("grp") * lax.axis_size("in")
    total, squares = all_sum((jnp.sum(value, 0), jnp.sum(value * value, 0)))
    middle = total / count
    rstd = lax.rsqrt(squares / count - middle * middle + BATCH_EPSILON)
    normed = (value - middle) * rstd
    return (normed, rstd, normed * gain + shift)


def norm_sums(upstream, normed):
    return all_sum((jnp.sum(upstream, 0), jnp.sum(upstream * normed, 0)))


def normalize_back(upstream, normed, rstd, gain, shift_sum, gain_sum):
    count = normed.shape[0] * lax.axis_size("grp") * lax.axis_size("in")
    return gain * rstd * (upstream - shift_sum / count - normed * gain_sum / count)


def tile_mask(vertical, lateral):
    tile_side = SIDE // 2
    position = jnp.arange(SIDE, dtype=jnp.int32) % tile_side
    row_valid = ((position + vertical - 1 >= 0) & (position + vertical - 1 < tile_side)).astype(
        jnp.float32
    )
    column_valid = ((position + lateral - 1 >= 0) & (position + lateral - 1 < tile_side)).astype(
        jnp.float32
    )
    return row_valid[:, None] * column_valid[None, :]


def columns(field, neck_width):
    canvas_grid = field.reshape(-1, SIDE, SIDE, neck_width)
    padded = jnp.pad(canvas_grid, ((0, 0), (1, 1), (1, 1), (0, 0)))
    windows = [
        padded[:, vertical : vertical + SIDE, lateral : lateral + SIDE, :]
        * tile_mask(vertical, lateral).astype(field.dtype)[None, :, :, None]
        for vertical in range(3)
        for lateral in range(3)
    ]
    return jnp.concatenate(windows, axis=-1).reshape(-1, 9 * neck_width)


def columns_back(grad_cols, neck_width):
    canvas_grid = grad_cols.reshape(-1, SIDE, SIDE, 9, neck_width)
    padded = jnp.zeros((canvas_grid.shape[0], SIDE + 2, SIDE + 2, neck_width), jnp.float32)
    for window in range(9):
        vertical = window // 3
        lateral = window % 3
        masked = canvas_grid[:, :, :, window, :] * tile_mask(vertical, lateral)[None, :, :, None]
        padded = padded.at[:, vertical : vertical + SIDE, lateral : lateral + SIDE, :].add(masked)
    return padded[:, 1:-1, 1:-1, :].reshape(-1, neck_width)


def normalize_rows(embedded):
    return embedded * lax.rsqrt(jnp.sum(embedded * embedded, axis=1, keepdims=True) + UNIT_EPSILON)


def on_device(
    canvas,
    reduce_weight,
    gain_first,
    shift_first,
    spatial_weight,
    gain_second,
    shift_second,
    expand_weight,
    gain_third,
    shift_third,
    hidden_weight,
    gain_head,
    shift_head,
    embed_weight,
    embed_bias,
    prototypes,
    queued,
    crop_ids,
    partner,
):
    canvases = canvas.shape[0]
    channels = canvas.shape[-1]
    neck_width = reduce_weight.shape[1]
    pixels = canvas.reshape(-1, channels)
    reduced = jnp.dot(pixels, reduce_weight, preferred_element_type=jnp.float32)
    normed_first, rstd_first, pre_first = normalize(reduced, gain_first, shift_first)
    act_first = jax.nn.gelu(pre_first).astype(jnp.bfloat16)
    cols_first = columns(act_first, neck_width)
    conved = jnp.dot(cols_first, spatial_weight, preferred_element_type=jnp.float32)
    normed_second, rstd_second, pre_second = normalize(conved, gain_second, shift_second)
    act_second = jax.nn.gelu(pre_second).astype(jnp.bfloat16)
    expanded = jnp.dot(act_second, expand_weight, preferred_element_type=jnp.float32)
    normed_third, rstd_third, pre_third = normalize(expanded, gain_third, shift_third)
    pre_out = pre_third + pixels.astype(jnp.float32)
    output = jax.nn.gelu(pre_out)
    member = (
        crop_ids.reshape(canvases, SIDE * SIDE, 1)
        == jnp.arange(CROPS, dtype=jnp.int32)[None, None, :]
    ).astype(jnp.float32)
    counts = jnp.sum(member, axis=1)[:, :, None]
    pooled = (
        jnp.einsum(
            "cpk,cpd->ckd",
            member,
            output.reshape(canvases, SIDE * SIDE, channels),
            precision=PRECISE,
        )
        / counts
    )
    pooled_low = pooled.reshape(-1, channels).astype(jnp.bfloat16)
    head_pre = jnp.dot(pooled_low, hidden_weight, preferred_element_type=jnp.float32)
    normed_head, rstd_head, pre_head = normalize(head_pre, gain_head, shift_head)
    act_head = jax.nn.gelu(pre_head).astype(jnp.bfloat16)
    embedded = jnp.dot(act_head, embed_weight, preferred_element_type=jnp.float32) + embed_bias
    normalized_features, unit_back = jax.vjp(normalize_rows, embedded)
    unit_low = normalized_features.astype(jnp.bfloat16)
    similarity_matrix = jnp.dot(unit_low, prototypes.T, preferred_element_type=jnp.float32)
    queue_similarity = jnp.dot(queued, prototypes.T, preferred_element_type=jnp.float32)
    crop_probability = jnp.exp(similarity_matrix / TRANSPORT_SMOOTH)
    queue_probability = jnp.exp(queue_similarity / TRANSPORT_SMOOTH)
    for sweep_index in range(ITERS):
        column = all_sum(
            (jnp.sum(crop_probability, 0) + jnp.sum(queue_probability, 0),)
        )[0]
        crop_probability = crop_probability / column
        queue_probability = queue_probability / column
        crop_probability = crop_probability / jnp.sum(crop_probability, axis=1, keepdims=True)
        queue_probability = queue_probability / jnp.sum(queue_probability, axis=1, keepdims=True)
    select = (partner[:, :, None] == jnp.arange(CROPS, dtype=jnp.int32)[None, None, :]).astype(
        jnp.float32
    )
    target = jnp.einsum(
        "cjk,ckp->cjp", select, crop_probability.reshape(canvases, CROPS, -1), precision=PRECISE
    ).reshape(-1, crop_probability.shape[1])
    scaled_similarity = similarity_matrix / SOFTMAX_WARMTH
    log_total = jax.nn.logsumexp(scaled_similarity, axis=1, keepdims=True)
    crop_loss = -jnp.sum(target * (scaled_similarity - log_total), axis=1)
    grad_scores = (
        (jnp.exp(scaled_similarity - log_total) * jnp.sum(target, axis=1, keepdims=True) - target)
        / SOFTMAX_WARMTH
    ).astype(jnp.bfloat16)
    grad_unit = jnp.dot(grad_scores, prototypes, preferred_element_type=jnp.float32)
    proto_local = contract_rows(grad_scores, unit_low)
    grad_embedded = unit_back(grad_unit)[0]
    grad_embedded_low = grad_embedded.astype(jnp.bfloat16)
    embed_local = contract_rows(act_head, grad_embedded_low)
    grad_act_head = jnp.dot(grad_embedded_low, embed_weight.T, preferred_element_type=jnp.float32)
    grad_pre_head = gelu_back(pre_head, grad_act_head)
    shift_head_grad, gain_head_grad, embed_bias_grad = all_sum(
        (
            jnp.sum(grad_pre_head, 0),
            jnp.sum(grad_pre_head * normed_head, 0),
            jnp.sum(grad_embedded, 0),
        )
    )
    grad_head = normalize_back(
        grad_pre_head, normed_head, rstd_head, gain_head, shift_head_grad, gain_head_grad
    ).astype(jnp.bfloat16)
    hidden_local = contract_rows(pooled_low, grad_head)
    grad_pooled = jnp.dot(grad_head, hidden_weight.T, preferred_element_type=jnp.float32)
    grad_output = jnp.einsum(
        "cpk,ckd->cpd",
        member,
        grad_pooled.reshape(canvases, CROPS, channels) / counts,
        precision=PRECISE,
    ).reshape(-1, channels)
    grad_pre_out = gelu_back(pre_out, grad_output)
    shift_third_grad, gain_third_grad = norm_sums(grad_pre_out, normed_third)
    grad_expanded = normalize_back(
        grad_pre_out, normed_third, rstd_third, gain_third, shift_third_grad, gain_third_grad
    ).astype(jnp.bfloat16)
    expand_local = contract_rows(act_second, grad_expanded)
    grad_pre_second = gelu_back(
        pre_second, jnp.dot(grad_expanded, expand_weight.T, preferred_element_type=jnp.float32)
    )
    shift_second_grad, gain_second_grad = norm_sums(grad_pre_second, normed_second)
    grad_conved = normalize_back(
        grad_pre_second,
        normed_second,
        rstd_second,
        gain_second,
        shift_second_grad,
        gain_second_grad,
    ).astype(jnp.bfloat16)
    spatial_local = contract_rows(cols_first, grad_conved)
    grad_act_first = columns_back(
        jnp.dot(grad_conved, spatial_weight.T, preferred_element_type=jnp.float32), neck_width
    )
    grad_pre_first = gelu_back(pre_first, grad_act_first)
    shift_first_grad, gain_first_grad = norm_sums(grad_pre_first, normed_first)
    grad_reduced = normalize_back(
        grad_pre_first, normed_first, rstd_first, gain_first, shift_first_grad, gain_first_grad
    ).astype(jnp.bfloat16)
    reduce_local = contract_rows(pixels, grad_reduced)
    canvas_grad = (
        (jnp.dot(grad_reduced, reduce_weight.T, preferred_element_type=jnp.float32) + grad_pre_out)
        .astype(jnp.bfloat16)
        .reshape(canvas.shape)
    )
    proto_part = lax.psum_scatter(proto_local, "in", scatter_dimension=1, tiled=True)
    prototypes_grad = lax.psum(proto_part, "grp")
    embed_grad = lax.psum_scatter(
        lax.psum_scatter(embed_local, "in", scatter_dimension=1, tiled=True),
        "grp",
        scatter_dimension=0,
        tiled=True,
    )
    hidden_grad = scatter_sum(blocked(hidden_local))
    expand_grad = scatter_sum(blocked(expand_local))
    spatial_grad = scatter_sum(blocked(spatial_local))
    reduce_grad = scatter_sum(blocked(reduce_local))
    return (
        crop_loss.reshape(canvases, CROPS),
        canvas_grad,
        reduce_grad,
        spatial_grad,
        expand_grad,
        hidden_grad,
        embed_grad,
        embed_bias_grad,
        prototypes_grad,
        gain_first_grad,
        shift_first_grad,
        gain_second_grad,
        shift_second_grad,
        gain_third_grad,
        shift_third_grad,
        gain_head_grad,
        shift_head_grad,
    )


def fold(value, gain, shift, total, count):
    middle = total[0:1] / count
    rstd = lax.rsqrt(total[1:2] / count - middle * middle + BATCH_EPSILON)
    normed = (value - middle) * rstd
    return normed, rstd, normed * gain + shift


def tanh_part(value):
    return jnp.tanh(ROOT * (value + CUBIC * (value * value * value)))


def gelu_of(value):
    return 0.5 * value * (1.0 + tanh_part(value))


def gelu_slope(value):
    bend = tanh_part(value)
    inner = ROOT * (1.0 + (3.0 * CUBIC) * (value * value))
    return 0.5 * (1.0 + bend) + 0.5 * value * (1.0 - bend * bend) * inner


def dot(left, right, dims=((1,), (0,))):
    return lax.dot_general(left, right, (dims, ((), ())), preferred_element_type=jnp.float32)


def column_sums(first, second):
    return jnp.concatenate(
        [jnp.sum(first, 0, keepdims=True), jnp.sum(second, 0, keepdims=True)], 0
    )


def spread(ref, value):
    ref[...] = jnp.broadcast_to(value[None], ref.shape)


def gathered(ref):
    return jnp.sum(ref[...], 0)


def gathered_pair(mine_ref, other_ref):
    return jnp.sum(mine_ref[...], 0) + jnp.sum(other_ref[...], 0)


def pairs():
    side = SIDE // 2
    for vertical in range(3):
        for lateral in range(3):
            here = []
            there = []
            for i in range(side):
                for j in range(side):
                    k = i + vertical - 1
                    m = j + lateral - 1
                    if 0 <= k < side and 0 <= m < side:
                        here.append(i * side + j)
                        there.append(k * side + m)
            yield 3 * vertical + lateral, here, there


def runs(places):
    out = []
    for place in places:
        if out and out[-1][0] + out[-1][1] == place:
            out[-1][1] += 1
        else:
            out.append([place, 1])
    return out


def take(ref, places, rows):
    parts = [ref[first * rows : (first + size) * rows, :] for first, size in runs(places)]
    return parts[0] if len(parts) == 1 else jnp.concatenate(parts, 0)


def add_rows(ref, places, rows, value):
    start = 0
    for first, size in runs(places):
        ref[first * rows : (first + size) * rows, :] += value[start : start + size * rows, :]
        start += size * rows


def tile_places():
    side = SIDE // 2
    for i in range(side):
        for j in range(side):
            yield i * side + j, [(a * side + i, b * side + j) for a in range(2) for b in range(2)]


def reduce_kernel(canvas_ref, weight_ref, pixels_ref, reduced_ref, sums_ref):
    rows = 4 * canvas_ref.shape[2]
    for place, corners in tile_places():
        pixels_ref[place * rows : (place + 1) * rows, :] = jnp.concatenate(
            [canvas_ref[i, j] for i, j in corners], 0
        )
    reduced = dot(pixels_ref[...], weight_ref[...])
    reduced_ref[...] = reduced
    spread(sums_ref, column_sums(reduced, reduced * reduced))


def spatial_kernel(
    count,
    reduced_ref,
    sums_ref,
    gain_ref,
    shift_ref,
    weight_ref,
    total_ref,
    wide_ref,
    conved_ref,
    out_ref,
    act_ref,
):
    neck = reduced_ref.shape[1]
    rows = reduced_ref.shape[0] // 9
    total = gathered(sums_ref)
    total_ref[...] = total
    pre = fold(reduced_ref[...], gain_ref[...], shift_ref[...], total, count)[2]
    act = gelu_of(pre).astype(jnp.bfloat16)
    act_ref[...] = act
    wide_ref[...] = act.astype(jnp.float32)
    for offset, here, there in sorted(pairs(), key=lambda p: p[0] != 4):
        part = dot(take(act_ref, there, rows), weight_ref[offset * neck : (offset + 1) * neck, :])
        if offset == 4:
            conved_ref[...] = part
        else:
            add_rows(conved_ref, here, rows, part)
    conved = conved_ref[...]
    spread(out_ref, column_sums(conved, conved * conved))


def expand_kernel(
    count, conved_ref, sums_ref, gain_ref, shift_ref, weight_ref, total_ref, act_ref, expanded_ref, out_ref
):
    total = gathered(sums_ref)
    total_ref[...] = total
    pre = fold(conved_ref[...], gain_ref[...], shift_ref[...], total, count)[2]
    act = gelu_of(pre).astype(jnp.bfloat16)
    act_ref[...] = act
    expanded = dot(act, weight_ref[...])
    expanded_ref[...] = expanded
    spread(out_ref, column_sums(expanded, expanded * expanded))


def pool_kernel(
    count,
    expanded_ref,
    mine_ref,
    other_ref,
    gain_ref,
    shift_ref,
    pixels_ref,
    weight_ref,
    total_ref,
    pooled_ref,
    head_ref,
    out_ref,
):
    step = pl.program_id(0)
    rows = expanded_ref.shape[0] // 9
    total = gathered_pair(mine_ref, other_ref)
    total_ref[...] = total
    pooled = None
    for place in range(9):
        block = slice(place * rows, (place + 1) * rows)
        pre = fold(expanded_ref[block, :], gain_ref[...], shift_ref[...], total, count)[2]
        part = gelu_of(pre + pixels_ref[block, :].astype(jnp.float32))
        pooled = part if pooled is None else pooled + part
    pooled = (pooled / 9.0).astype(jnp.bfloat16)
    pooled_ref[...] = pooled.astype(jnp.float32)
    head = dot(pooled, weight_ref[...])

    @pl.when(step == 0)
    def _():
        head_ref[...] = head

    @pl.when(step > 0)
    def _():
        head_ref[...] += head

    @pl.when(step == pl.num_programs(0) - 1)
    def _():
        value = head_ref[...]
        spread(out_ref, column_sums(value, value * value))


def score_kernel(
    count,
    protos,
    head_ref,
    mine_ref,
    other_ref,
    gain_ref,
    shift_ref,
    embed_ref,
    bias_ref,
    proto_ref,
    queued_ref,
    total_ref,
    act_ref,
    embedded_ref,
    scores_ref,
    mass_ref,
    out_ref,
):
    total = gathered_pair(mine_ref, other_ref)
    total_ref[...] = total
    pre = fold(head_ref[...], gain_ref[...], shift_ref[...], total, count)[2]
    act = gelu_of(pre).astype(jnp.bfloat16)
    act_ref[...] = act
    embedded = dot(act, embed_ref[...]) + bias_ref[...]
    embedded_ref[...] = embedded
    rnorm = lax.rsqrt(jnp.sum(embedded * embedded, 1, keepdims=True) + UNIT_EPSILON)
    unit = (embedded * rnorm).astype(jnp.bfloat16)
    crops = unit.shape[0]
    scores = dot(unit, proto_ref[...], ((1,), (1,)))
    scores_ref[...] = scores
    queue = dot(queued_ref[...], proto_ref[...], ((1,), (1,)))
    shape = scores.shape
    inside = lax.broadcasted_iota(jnp.int32, shape, 1) < protos
    mass = jnp.where(inside, jnp.exp(scores / TRANSPORT_SMOOTH), 0.0)
    mass_ref[0:crops, :] = mass
    queue_inside = lax.broadcasted_iota(jnp.int32, queue.shape, 1) < protos
    queue_mass = jnp.where(queue_inside, jnp.exp(queue / TRANSPORT_SMOOTH), 0.0)
    real = queue.shape[0]
    mass_ref[crops:, :] = jnp.zeros((mass_ref.shape[0] - crops, shape[1]), jnp.float32)
    mass_ref[crops : crops + real, :] = queue_mass
    spread(out_ref, jnp.sum(mass, 0, keepdims=True) + jnp.sum(queue_mass, 0, keepdims=True))


def balance(protos, mass, column):
    inside = lax.broadcasted_iota(jnp.int32, column.shape, 1) < protos
    mass = mass / jnp.where(inside, column, 1.0)
    row = jnp.sum(mass, 1, keepdims=True)
    return mass, row


def sweep_kernel(protos, real, mass_ref, mine_ref, other_ref, next_ref, out_ref):
    mass, row = balance(protos, mass_ref[...], gathered_pair(mine_ref, other_ref))
    used = lax.broadcasted_iota(jnp.int32, row.shape, 0) < real
    mass = mass / jnp.where(used, row, 1.0)
    next_ref[...] = mass
    spread(out_ref, jnp.sum(mass, 0, keepdims=True))


def loss_kernel(
    count,
    protos,
    mass_ref,
    mine_ref,
    other_ref,
    here_ref,
    wanted_ref,
    held_ref,
    scores_ref,
    embedded_ref,
    proto_ref,
    act_ref,
    embed_ref,
    head_ref,
    head_total_ref,
    gain_ref,
    shift_ref,
    loss_ref,
    keep_ref,
    send_ref,
    upstream_ref,
    out_ref,
):
    crops = scores_ref.shape[0]
    width = scores_ref.shape[1]
    mass, row = balance(protos, mass_ref[0:crops, :], gathered_pair(mine_ref, other_ref))
    codes = mass / row
    size = crops // CROPS
    row_place = lax.broadcasted_iota(jnp.int32, (crops, crops), 0) % size
    column_place = lax.broadcasted_iota(jnp.int32, (crops, crops), 1) % size
    chosen = (wanted_ref[...] == held_ref[...]) & (row_place == column_place)
    target = lax.dot_general(
        jnp.where(chosen, 1.0, 0.0),
        codes,
        (((1,), (0,)), ((), ())),
        precision=PRECISE,
        preferred_element_type=jnp.float32,
    )
    logits = scores_ref[...] / SOFTMAX_WARMTH
    inside = lax.broadcasted_iota(jnp.int32, logits.shape, 1) < protos
    top = jnp.max(jnp.where(inside, logits, -3.0e38), 1, keepdims=True)
    mass_of = jnp.where(inside, jnp.exp(logits - top), 0.0)
    log_total = jnp.log(jnp.sum(mass_of, 1, keepdims=True)) + top
    loss_ref[...] = -jnp.sum(target * (logits - log_total), 1, keepdims=True)
    share = jnp.sum(target, 1, keepdims=True)
    soft = jnp.where(inside, jnp.exp(logits - log_total), 0.0)
    grad_scores = ((soft * share - target) / SOFTMAX_WARMTH).astype(jnp.bfloat16)
    embedded = embedded_ref[...]
    rnorm = lax.rsqrt(jnp.sum(embedded * embedded, 1, keepdims=True) + UNIT_EPSILON)
    unit = embedded * rnorm
    grad_unit = dot(grad_scores, proto_ref[...])
    grad_embedded = rnorm * (grad_unit - unit * jnp.sum(grad_unit * unit, 1, keepdims=True))
    grad_low = grad_embedded.astype(jnp.bfloat16)
    proto_local = dot(unit.astype(jnp.bfloat16), grad_scores, ((0,), (0,)))
    embed_local = dot(grad_low, act_ref[...], ((0,), (0,)))
    across, outer, rows = keep_ref.shape[:3]
    first = width // outer
    second = embed_local.shape[1] // outer
    flip = here_ref[0] == 1
    for k in range(across):
        lines = [slice((2 * k + c) * rows, (2 * k + c + 1) * rows) for c in range(2)]
        for m in range(outer):
            for value, size, start in ((proto_local, first, 0), (embed_local, second, first)):
                even, odd = (value[line, m * size : (m + 1) * size] for line in lines)
                keep_ref[k, m, :, start : start + size] = jnp.where(flip, odd, even)
                send_ref[k, m, :, start : start + size] = jnp.where(flip, even, odd)
    total = head_total_ref[...]
    normed, _, pre = fold(head_ref[...], gain_ref[...], shift_ref[...], total, count)
    upstream = gelu_slope(pre) * dot(grad_low, embed_ref[...], ((1,), (1,)))
    upstream_ref[...] = upstream
    bias = jnp.sum(grad_embedded, 0, keepdims=True)
    sums = jnp.concatenate([column_sums(upstream, upstream * normed), jnp.concatenate([bias, bias], 0)], 1)
    spread(out_ref, sums)


def split_columns(value, here_ref, near_ref, away_ref):
    part = near_ref.shape[2]
    blocks = [value[:, k * part : (k + 1) * part] for k in range(4)]
    core = here_ref[0] == 1
    chip = here_ref[1] == 1
    for k in range(2):
        first = jnp.where(core, blocks[1 - k], blocks[k])
        second = jnp.where(core, blocks[3 - k], blocks[2 + k])
        near_ref[k] = jnp.where(chip, second, first)
        away_ref[k] = jnp.where(chip, first, second)


def norm_back(upstream, normed, rstd, gain, total, count):
    return gain * rstd * (upstream - total[0:1] / count - normed * (total[1:2] / count))


def head_back_kernel(
    count,
    upstream_ref,
    mine_ref,
    other_ref,
    head_ref,
    head_total_ref,
    gain_ref,
    shift_ref,
    here_ref,
    sums_ref,
    low_ref,
    near_ref,
    away_ref,
):
    total = gathered_pair(mine_ref, other_ref)
    sums_ref[...] = total
    width = head_ref.shape[1]
    stats = head_total_ref[...]
    normed, rstd, _ = fold(head_ref[...], gain_ref[...], shift_ref[...], stats, count)
    grad = norm_back(upstream_ref[...], normed, rstd, gain_ref[...], total[:, 0:width], count)
    low = grad.astype(jnp.bfloat16)
    low_ref[...] = low
    split_columns(low.astype(jnp.float32), here_ref, near_ref, away_ref)


def pool_back_kernel(
    count,
    grad_ref,
    weight_ref,
    expanded_ref,
    total_ref,
    gain_ref,
    shift_ref,
    pixels_ref,
    upstream_ref,
    out_ref,
):
    rows = expanded_ref.shape[0] // 9
    total = total_ref[...]
    grad_output = dot(grad_ref[...], weight_ref[...], ((1,), (1,))) / 9.0
    first = None
    second = None
    for place in range(9):
        block = slice(place * rows, (place + 1) * rows)
        normed, _, pre = fold(expanded_ref[block, :], gain_ref[...], shift_ref[...], total, count)
        upstream = gelu_slope(pre + pixels_ref[block, :].astype(jnp.float32)) * grad_output
        upstream_ref[block, :] = upstream.astype(jnp.bfloat16)
        weighted = upstream * normed
        first = upstream if first is None else first + upstream
        second = weighted if second is None else second + weighted
    spread(out_ref, column_sums(first, second))


def expand_back_kernel(
    count,
    upstream_ref,
    back_mine_ref,
    back_other_ref,
    expanded_ref,
    total_ref,
    gain_ref,
    weight_ref,
    act_ref,
    conved_ref,
    conved_sums_ref,
    conved_gain_ref,
    conved_shift_ref,
    here_ref,
    sums_ref,
    keep_ref,
    send_ref,
    next_ref,
    out_ref,
):
    step = pl.program_id(0)
    back = gathered_pair(back_mine_ref, back_other_ref)
    sums_ref[...] = back
    stats = total_ref[...]
    normed, rstd, _ = fold(expanded_ref[...], gain_ref[...], 0.0, stats, count)
    grad = norm_back(
        upstream_ref[...].astype(jnp.float32), normed, rstd, gain_ref[...], back, count
    ).astype(jnp.bfloat16)
    part = dot(grad, weight_ref[...], ((1,), (1,)))
    value = dot(act_ref[...], grad, ((0,), (0,)))
    half = value.shape[1] // 2
    flip = here_ref[0] == 1
    keep_ref[0] = jnp.where(flip, value[:, half:], value[:, :half])
    send_ref[0] = jnp.where(flip, value[:, :half], value[:, half:])

    @pl.when(step == 0)
    def _():
        next_ref[...] = part

    @pl.when(step > 0)
    def _():
        next_ref[...] += part

    @pl.when(step == pl.num_programs(0) - 1)
    def _():
        conved, _, pre = fold(
            conved_ref[...], conved_gain_ref[...], conved_shift_ref[...], conved_sums_ref[...], count
        )
        upstream = gelu_slope(pre) * next_ref[...]
        next_ref[...] = upstream
        spread(out_ref, column_sums(upstream, upstream * conved))


def conved_back_kernel(
    count,
    upstream_ref,
    back_ref,
    conved_ref,
    sums_ref,
    gain_ref,
    here_ref,
    total_ref,
    low_ref,
    near_ref,
    away_ref,
):
    back = gathered(back_ref)
    total_ref[...] = back
    normed, rstd, _ = fold(conved_ref[...], gain_ref[...], 0.0, sums_ref[...], count)
    low = norm_back(upstream_ref[...], normed, rstd, gain_ref[...], back, count).astype(jnp.bfloat16)
    low_ref[...] = low
    split_columns(low.astype(jnp.float32), here_ref, near_ref, away_ref)


def spatial_back_kernel(
    count,
    low_ref,
    weight_ref,
    reduced_ref,
    reduced_sums_ref,
    reduced_gain_ref,
    reduced_shift_ref,
    next_ref,
    out_ref,
):
    neck = reduced_ref.shape[1]
    rows = reduced_ref.shape[0] // 9
    for offset, here, there in sorted(pairs(), key=lambda p: p[0] != 4):
        value = dot(
            take(low_ref, here, rows), weight_ref[offset * neck : (offset + 1) * neck, :], ((1,), (1,))
        )
        if offset == 4:
            next_ref[...] = value
        else:
            add_rows(next_ref, there, rows, value)
    reduced, _, pre = fold(
        reduced_ref[...], reduced_gain_ref[...], reduced_shift_ref[...], reduced_sums_ref[...], count
    )
    upstream = gelu_slope(pre) * next_ref[...]
    next_ref[...] = upstream
    spread(out_ref, column_sums(upstream, upstream * reduced))


def spatial_weight_kernel(
    here_ref, act_ref, near_ref, away_ref, core_ref, keep_ref, send_ref, left_ref, right_ref
):
    devices = act_ref.shape[0]
    rows = act_ref.shape[1] // 9
    neck = act_ref.shape[2]
    me = here_ref[0] + 2 * here_ref[1]
    grads = (near_ref, core_ref, away_ref, core_ref)
    for k in range(devices):
        source = me ^ k
        for place in range(9):
            block = slice(place * rows, (place + 1) * rows)
            goal = slice((place * devices + k) * rows, (place * devices + k + 1) * rows)
            left_ref[goal, :] = act_ref[source, block, :].astype(jnp.bfloat16)
            right_ref[goal, :] = grads[k][k // 2 if k % 2 else 0, block, :].astype(jnp.bfloat16)
    size = keep_ref.shape[1]
    mine = here_ref[2]
    for offset, here, there in pairs():
        value = dot(
            take(right_ref, here, rows * devices), take(left_ref, there, rows * devices), ((0,), (0,))
        ).T
        start = offset * neck
        end = start + neck
        while start < end:
            owner = start // size
            stop = min(end, (owner + 1) * size)
            piece = value[start - offset * neck : stop - offset * neck, :]
            lines = slice(start - owner * size, stop - owner * size)

            @pl.when(mine == owner % 2)
            def _():
                keep_ref[owner // 2, lines, :] = piece

            @pl.when(mine != owner % 2)
            def _():
                send_ref[owner // 2, lines, :] = piece

            start = stop


def hidden_weight_kernel(here_ref, pooled_ref, near_ref, y_ref, x_ref, xy_ref, core_ref, out_ref):
    deep, size, _ = out_ref.shape
    me = here_ref[0] + 2 * here_ref[1] + 4 * here_ref[2]
    places = [(0, near_ref, 0), (4, y_ref, 0), (2, x_ref, 0), (6, xy_ref, 0)]
    places += [(1, core_ref, 0), (5, core_ref, 1), (3, core_ref, 2), (7, core_ref, 3)]
    right = jnp.concatenate([ref[k].astype(jnp.bfloat16) for _, ref, k in places], 0)
    for m in range(deep):
        start = pl.multiple_of((2 * m + here_ref[2]) * size, size)
        left = jnp.concatenate(
            [pooled_ref[me ^ mask, :, pl.ds(start, size)].astype(jnp.bfloat16) for mask, _, _ in places], 0
        )
        out_ref[m] = dot(left, right, ((0,), (0,)))


def half_kernel(here_ref, keep_ref, come_ref, mine_ref, other_ref):
    mine = here_ref[1]
    mine_ref[...] = keep_ref[mine] + come_ref[mine]
    other_ref[...] = keep_ref[1 - mine] + come_ref[1 - mine]


def cut_kernel(here_ref, keep_ref, come_ref, mine_ref, *other_refs):
    mine = here_ref[2]
    for x, other_ref in enumerate(other_refs):
        for k in range(mine_ref.shape[1]):
            mine_ref[x, k] = keep_ref[x, 2 * k + mine] + come_ref[x, 2 * k + mine]
            other_ref[k] = keep_ref[x, 2 * k + 1 - mine] + come_ref[x, 2 * k + 1 - mine]


def join_kernel(here_ref, keep_ref, first_ref, second_ref, mine_ref, other_ref):
    mine = here_ref[1]
    flip = mine == 1
    first = first_ref[...]
    second = second_ref[...]
    mine_ref[...] = keep_ref[mine] + jnp.where(flip, second, first)
    other_ref[...] = keep_ref[1 - mine] + jnp.where(flip, first, second)


def side_kernel(here_ref, keep_ref, come_ref, mine_ref, other_ref):
    mine = here_ref[2]
    for k in range(mine_ref.shape[0]):
        mine_ref[k] = keep_ref[2 * k + mine] + come_ref[2 * k + mine]
        other_ref[k] = keep_ref[2 * k + 1 - mine] + come_ref[2 * k + 1 - mine]


def across_kernel(here_ref, keep_ref, come_ref, *out_refs):
    deep = out_refs[0].shape[0]
    for m, out_ref in enumerate(out_refs):
        column = here_ref[1] ^ (m & 1)
        side = here_ref[2] ^ (m >> 1)
        for k in range(deep):
            out_ref[k] = keep_ref[column, 2 * k + side] + come_ref[column, 2 * k + side]


def along_kernel(here_ref, *refs):
    deep = refs[0].shape[0]
    ins, outs = refs[:-deep], refs[-deep:]
    for m, out_ref in enumerate(outs):
        place = here_ref[3] ^ m
        total = ins[0][place]
        for ref in ins[1:]:
            total = total + ref[place]
        out_ref[...] = total


def reduce_back_kernel(
    count,
    upstream_ref,
    back_ref,
    reduced_ref,
    sums_ref,
    gain_ref,
    pixels_ref,
    here_ref,
    total_ref,
    low_ref,
    keep_ref,
    send_ref,
):
    back = gathered(back_ref)
    total_ref[...] = back
    normed, rstd, _ = fold(reduced_ref[...], gain_ref[...], 0.0, sums_ref[...], count)
    low = norm_back(upstream_ref[...], normed, rstd, gain_ref[...], back, count).astype(jnp.bfloat16)
    low_ref[...] = low
    part = keep_ref.shape[2]
    value = dot(pixels_ref[...], low, ((0,), (0,)))
    flip = here_ref[0] == 1
    for k in range(keep_ref.shape[0]):
        even = value[:, 2 * k * part : (2 * k + 1) * part]
        odd = value[:, (2 * k + 1) * part : (2 * k + 2) * part]
        keep_ref[k] = jnp.where(flip, odd, even)
        send_ref[k] = jnp.where(flip, even, odd)


def canvas_kernel(low_ref, weight_ref, upstream_ref, out_ref):
    rows = low_ref.shape[0] // 9
    size = out_ref.shape[2]
    value = dot(low_ref[...], weight_ref[...], ((1,), (1,))) + upstream_ref[...].astype(jnp.float32)
    value = value.astype(jnp.bfloat16)
    for place, corners in tile_places():
        for k, (i, j) in enumerate(corners):
            start = place * rows + k * size
            out_ref[i, j] = value[start : start + size, :]


MADE = []
SCALARS = pl.BlockSpec(memory_space=pltpu.SMEM)
ARRAY = pl.BlockSpec(memory_space=pltpu.VMEM)


def run(kernel, outs, args, scratch=(), flops=0, moved=0, after=(), free=(), **grid):
    if "grid" not in grid:
        kinds = [SCALARS if a.ndim == 1 and a.dtype == jnp.int32 else ARRAY for a in args]
        grid["in_specs"] = kinds
    if len(after) > 0:
        inner = kernel
        count = len(args)
        grid["in_specs"] = list(grid["in_specs"]) + [pl.BlockSpec(memory_space=pl.ANY)] * len(after)
        args = tuple(args) + tuple(after)
        skip = len(after)

        def kernel(*refs):
            inner(*refs[:count], *refs[count + skip :])

    loose = grid.pop("loose", ())
    args = [
        a
        if (a.ndim == 1 and a.dtype == jnp.int32)
        or any(a is other for other in (*loose, *after))
        or any(a is other for other in MADE)
        else pinned(a)
        for a in args
    ]
    made = pl.pallas_call(
        kernel,
        out_shape=outs,
        scratch_shapes=list(scratch),
        compiler_params=pltpu.CompilerParams(vmem_limit_bytes=VMEM_BYTES),
        cost_estimate=pl.CostEstimate(flops=1, bytes_accessed=1, transcendentals=0),
        **grid,
    )(*args)
    for out, value in zip(jax.tree.leaves(outs), jax.tree.leaves(made)):
        if out.memory_space == pltpu.VMEM:
            MADE.append(value)
    return made


def f32(*shape):
    return pltpu.HBM(shape, jnp.float32)


def b16(*shape):
    return pltpu.HBM(shape, jnp.bfloat16)


def near32(*shape):
    return pltpu.VMEM(shape, jnp.float32)


def near16(*shape):
    return pltpu.VMEM(shape, jnp.bfloat16)


def to_all(block):
    return lax.all_to_all(block, AXES, 0, 0, tiled=True)


def to_all_pair(block):
    count = lax.axis_size("grp") * lax.axis_size("in")
    groups = [list(range(k, count, 2)) for k in range(2)]
    mine = lax.all_to_all(block, AXES, 0, 0, tiled=True, axis_index_groups=groups)
    return mine, swap_bit(mine, 0)


def pick(value, bit, axis=0):
    mine = lax.dynamic_index_in_dim(value, my_bit(bit), axis, keepdims=False)
    other = lax.dynamic_index_in_dim(value, 1 - my_bit(bit), axis, keepdims=False)
    return mine, other


def teams(bits):
    count = lax.axis_size("grp") * lax.axis_size("in")
    spans = [0]
    for bit in bits:
        spans = spans + [m | (1 << bit) for m in spans]
    used = sum(1 << bit for bit in bits)
    return [[base | m for m in sorted(spans)] for base in range(count) if base & used == 0]


def pinned(value):
    return pltpu.with_memory_space_constraint(value, pltpu.HBM)


def swap_mask(value, mask):
    count = lax.axis_size("grp") * lax.axis_size("in")
    return lax.ppermute(value, AXES, [(i, i ^ mask) for i in range(count)])


def spread_plane(here, keep, come):
    deep = keep.shape[1] // 2
    parts = run(across_kernel, (f32(deep, *keep.shape[2:]),) * 4, (here, keep, come), moved=4 * keep.size * 3, loose=(come,))
    return [parts[0]] + [
        swap_mask(pinned(parts[m]), 2 * m) for m in range(1, 4)
    ]


def spread_line(here, parts):
    deep = parts[0].shape[0]
    shape = parts[0].shape[1:]
    cut = run(
        along_kernel,
        (f32(*shape),) * deep,
        (here, *parts),
        moved=4 * parts[0].size * (len(parts) + 1),
    )
    return [cut[0]] + [swap_mask(cut[m], 8 * m) for m in range(1, deep)]


def together(*values):
    return lax.optimization_barrier(values)


def total_of(parts):
    value = parts[0]
    for part in parts[1:]:
        value = value + part
    return value


def fast(
    canvas,
    reduce_weight,
    gain_first,
    shift_first,
    spatial_weight,
    gain_second,
    shift_second,
    expand_weight,
    gain_third,
    shift_third,
    hidden_weight,
    gain_head,
    shift_head,
    embed_weight,
    embed_bias,
    prototypes,
    queued,
    crop_ids,
    partner,
):
    MADE.clear()
    inner = lax.axis_size("in")
    outer = lax.axis_size("grp")
    devices = inner * outer
    low_bits = bits_of("in")
    canvases = canvas.shape[0]
    channels = canvas.shape[-1]
    neck = reduce_weight.shape[1]
    hidden = hidden_weight.shape[1]
    width = embed_weight.shape[1]
    rows = canvases * SIDE * SIDE
    crops = canvases * CROPS
    protos = prototypes.shape[0]
    wide = -(-protos // (128 * outer)) * 128 * outer
    count = float(rows * devices)
    crop_count = float(crops * devices)
    gain_first, shift_first, gain_second, shift_second = (
        v.reshape(1, -1) for v in (gain_first, shift_first, gain_second, shift_second)
    )
    gain_third, shift_third, gain_head, shift_head, embed_bias = (
        v.reshape(1, -1) for v in (gain_third, shift_third, gain_head, shift_head, embed_bias)
    )
    proto_wide = jnp.pad(prototypes, ((0, wide - protos), (0, 0)))
    field = canvas.transpose(1, 2, 0, 3)

    index = lax.axis_index("grp") * inner + lax.axis_index("in")
    here = jnp.stack([index & 1, (index >> 1) & 1, (index >> 2) & 1, index >> 3]).astype(jnp.int32)
    quadrants = crop_ids[:, :: SIDE // 2, :: SIDE // 2].reshape(canvases, CROPS).T
    wanted = jnp.sum(
        (quadrants[:, None, :] == jnp.arange(CROPS, dtype=jnp.int32)[None, :, None])
        * partner.T[None, :, :],
        1,
    ).reshape(crops, 1)
    held = quadrants.reshape(1, crops)

    pixels, reduced, sums = run(
        reduce_kernel,
        (near16(rows, channels), f32(rows, neck), near32(devices, 2, neck)),
        (field, reduce_weight),
        flops=2 * rows * channels * neck,
        moved=12_000_000,
    )
    first_sums = to_all(sums)
    first_total, act_wide, conved, sums = run(
        functools.partial(spatial_kernel, count),
        (near32(2, neck), f32(rows, neck), f32(rows, neck), near32(devices, 2, neck)),
        (reduced, first_sums, gain_first, shift_first, spatial_weight),
        loose=(first_sums, spatial_weight),
        scratch=[pltpu.VMEM((rows, neck), jnp.bfloat16)],
        flops=11 * rows * neck * neck,
        moved=12_000_000,
    )
    act_all = lax.all_gather(act_wide, "in")
    second_sums = to_all(sums)
    second_total, act_second, expanded, sums = run(
        functools.partial(expand_kernel, count),
        (near32(2, neck), near16(rows, neck), f32(rows, channels), near32(devices // 2, 2, channels)),
        (conved, second_sums, gain_second, shift_second, expand_weight),
        loose=(second_sums, expand_weight),
        flops=2 * rows * channels * neck,
        moved=12_000_000,
    )
    third_mine, third_other = to_all_pair(sums)
    block = channels // outer
    chunk = 2 * block
    chunks = channels // chunk
    columns = lambda n: pl.BlockSpec((n, chunk), lambda k: (0, k))
    stats = lambda n: pl.BlockSpec((n, 2, chunk), lambda k: (0, 0, k))
    whole = lambda *shape: pl.BlockSpec(shape, lambda k: (0,) * len(shape))
    third_total, pooled, head_pre, sums = run(
        functools.partial(pool_kernel, count),
        (near32(2, channels), f32(crops, channels), f32(crops, hidden), near32(devices // 2, 2, hidden)),
        (expanded, third_mine, third_other, gain_third, shift_third, pixels, hidden_weight),
        loose=(third_mine, third_other),
        flops=2 * crops * channels * hidden,
        moved=18_000_000,
        grid=(chunks,),
        in_specs=[
            columns(rows),
            stats(devices // 2),
            stats(devices // 2),
            columns(1),
            columns(1),
            columns(rows),
            pl.BlockSpec((chunk, hidden), lambda k: (k, 0)),
        ],
        out_specs=[
            columns(2),
            columns(crops),
            whole(crops, hidden),
            whole(devices // 2, 2, hidden),
        ],
    )
    pooled_all = lax.all_gather(pooled, AXES, axis_index_groups=teams(range(low_bits + 1)))
    head_mine, head_other = to_all_pair(sums)
    real = crops + queued.shape[0]
    mass_rows = -(-real // 8) * 8
    head_total, act_head, embedded, scores, mass, sums = run(
        functools.partial(score_kernel, crop_count, protos),
        (
            near32(2, hidden),
            near16(crops, hidden),
            f32(crops, width),
            f32(crops, wide),
            near32(mass_rows, wide),
            near32(devices // 2, 1, wide),
        ),
        (
            head_pre,
            head_mine,
            head_other,
            gain_head,
            shift_head,
            embed_weight,
            embed_bias,
            proto_wide,
            queued,
        ),
        loose=(head_mine, head_other, embed_weight, proto_wide),
        flops=2 * crops * width * (hidden + wide),
        moved=6_000_000,
    )
    for _ in range(ITERS - 1):
        column_mine, column_other = to_all_pair(sums)
        mass, sums = run(
            functools.partial(sweep_kernel, protos, real),
            (near32(mass_rows, wide), near32(devices // 2, 1, wide)),
            (mass, column_mine, column_other),
            loose=(column_mine, column_other, mass),
            moved=3_000_000,
        )
    column_mine, column_other = to_all_pair(sums)
    loss, small_keep, small_send, upstream, sums = run(
        functools.partial(loss_kernel, crop_count, protos),
        (
            f32(crops, 1),
            f32(inner // 2, outer, width // inner, (wide + hidden) // outer),
            f32(inner // 2, outer, width // inner, (wide + hidden) // outer),
            f32(crops, hidden),
            near32(devices // 2, 2, hidden + width),
        ),
        (
            mass,
            column_mine,
            column_other,
            here,
            wanted,
            held,
            scores,
            embedded,
            proto_wide,
            act_head,
            embed_weight,
            head_pre,
            head_total,
            gain_head,
            shift_head,
        ),
        loose=(column_mine, column_other, mass),
        flops=6 * crops * width * (hidden + wide),
        moved=9_000_000,
    )
    back_mine, back_other = to_all_pair(sums)
    small = spread_plane(here, small_keep, swap_mask(small_send, 1))
    part = hidden // inner
    head_sums, grad_head, head_near, head_away = run(
        functools.partial(head_back_kernel, crop_count),
        (f32(2, hidden + width), near16(crops, hidden), f32(2, crops, part), f32(2, crops, part)),
        (upstream, back_mine, back_other, head_pre, head_total, gain_head, shift_head, here),
        loose=(back_mine, back_other),
        after=(small[0],),
        moved=3_000_000,
    )
    grad_pre_out, sums = run(
        functools.partial(pool_back_kernel, count),
        (near16(rows, channels), near32(devices // 2, 2, channels)),
        (
            grad_head,
            hidden_weight,
            expanded,
            third_total,
            gain_third,
            shift_third,
            pixels,
        ),
        flops=2 * crops * channels * hidden,
        moved=20_000_000,
        after=(small[0],),
        grid=(chunks,),
        in_specs=[
            whole(crops, hidden),
            pl.BlockSpec((chunk, hidden), lambda k: (k, 0)),
            columns(rows),
            columns(2),
            columns(1),
            columns(1),
            columns(rows),
        ],
        out_specs=[columns(rows), stats(devices // 2)],
    )
    back_mine, back_other = to_all_pair(together(sums, *small[1:])[0])
    part = channels // inner
    columns = lambda n: pl.BlockSpec((n, 2 * part), lambda k: (0, k))
    stats = lambda n: pl.BlockSpec((n, 2, 2 * part), lambda k: (0, 0, k))
    def joined(keep, send, size):
        shape = (inner // 2, outer, size // outer, -1)
        return keep.reshape(shape), swap_mask(send, 1).reshape(shape)

    third_back, expand_keep, expand_send, upstream, sums = run(
        functools.partial(expand_back_kernel, count),
        (
            f32(2, channels),
            f32(inner // 2, neck, part),
            f32(inner // 2, neck, part),
            f32(rows, neck),
            near32(devices, 2, neck),
        ),
        (
            grad_pre_out,
            back_mine,
            back_other,
            expanded,
            third_total,
            gain_third,
            expand_weight,
            act_second,
            conved,
            second_total,
            gain_second,
            shift_second,
            here,
        ),
        flops=4 * rows * channels * neck,
        moved=22_000_000,
        loose=(back_mine, back_other),
        grid=(inner // 2,),
        in_specs=[
            columns(rows),
            stats(devices // 2),
            stats(devices // 2),
            columns(rows),
            columns(2),
            columns(1),
            columns(neck),
            whole(rows, neck),
            whole(rows, neck),
            whole(2, neck),
            whole(1, neck),
            whole(1, neck),
            SCALARS,
        ],
        out_specs=[
            columns(2),
            pl.BlockSpec((1, neck, part), lambda k: (k, 0, 0)),
            pl.BlockSpec((1, neck, part), lambda k: (k, 0, 0)),
            whole(rows, neck),
            whole(devices, 2, neck),
        ],
    )
    back = to_all(sums)
    moved = [head_near] + [
        swap_mask(v, mask) for v, mask in ((head_near, 4), (head_away, 2), (head_away, 6))
    ]
    core_grads = swap_mask(jnp.stack([v[1] for v in moved]), 1)
    keep, come = joined(expand_keep, expand_send, neck)
    shape = (outer // 2, *keep.shape[2:])
    expand_kept, *expand_sent = run(
        cut_kernel, (f32(inner // 2, *shape), f32(*shape), f32(*shape)), (here, keep, come), loose=(come,)
    )
    expand_first = swap_mask(pinned(expand_sent[0]), 4)
    second_back, grad_conved, conved_near, conved_away = run(
        functools.partial(conved_back_kernel, count),
        (
            f32(2, neck),
            near16(rows, neck),
            f32(2, rows, neck // inner),
            f32(2, rows, neck // inner),
        ),
        (upstream, back, conved, second_total, gain_second, here),
        loose=(back,),
        after=(expand_sent[0], *moved[1:]),
    )
    away = swap_mask(conved_away, 2)
    expand_second = swap_mask(pinned(expand_sent[1]), 4)
    upstream, sums = run(
        functools.partial(spatial_back_kernel, count),
        (f32(rows, neck), near32(devices, 2, neck)),
        (
            grad_conved,
            spatial_weight,
            reduced,
            first_total,
            gain_first,
            shift_first,
        ),
        loose=(spatial_weight,),
    )
    small = spread_line(here, small)
    hidden_local = run(
        hidden_weight_kernel,
        f32(outer // 2, channels // outer, hidden // inner),
        (here, pooled_all, *moved, core_grads),
        flops=crops * 2 * inner * channels * hidden // inner,
        moved=7_000_000,
    )
    sums, away, expand_first, expand_second, hidden_local, *small = together(
        sums, away, expand_first, expand_second, hidden_local, *small
    )
    small = total_of(small)
    hidden_grad = lax.psum_scatter(
        hidden_local, "grp", axis_index_groups=[list(range(k, outer, 2)) for k in range(2)]
    )
    back = to_all(sums)
    expand_kept, sent = run(
        join_kernel,
        (f32(*expand_kept.shape[1:]),) * 2,
        (here, expand_kept, expand_first, expand_second),
        loose=(expand_first, expand_second),
    )
    expand_come = swap_mask(pinned(sent), 2)
    core = swap_mask(jnp.stack([conved_near[1], away[1]]), 1)
    spatial_keep, spatial_send = run(
        spatial_weight_kernel,
        (f32(outer // 2, 9 * neck // outer, neck // inner),) * 2,
        (here, act_all, conved_near, away, core),
        scratch=[
            pltpu.VMEM((rows * inner, neck), jnp.bfloat16),
            pltpu.VMEM((rows * inner, neck // inner), jnp.bfloat16),
        ],
        after=(sent,),
    )
    spatial_come = swap_mask(pinned(spatial_send), 4)
    first_back, grad_reduced, reduce_keep, reduce_send = run(
        functools.partial(reduce_back_kernel, count),
        (
            f32(2, neck),
            near16(rows, neck),
            f32(inner // 2, channels, neck // inner),
            f32(inner // 2, channels, neck // inner),
        ),
        (upstream, back, reduced, first_total, gain_first, pixels, here),
        loose=(back,),
        flops=2 * rows * channels * neck,
        moved=12_000_000,
        after=(spatial_send,),
    )
    reduce_send, expand_come = together(reduce_send, expand_come)
    keep, come = joined(reduce_keep, reduce_send, channels)
    kept, sent = run(half_kernel, (f32(*keep.shape[1:]),) * 2, (here, keep, come), loose=(come,))
    come = swap_mask(pinned(sent), 2)
    expand_parts = spread_line(here, [expand_kept, expand_come])
    canvas_grad = run(
        canvas_kernel,
        b16(SIDE, SIDE, canvases, channels),
        (grad_reduced, reduce_weight, grad_pre_out),
        after=(sent, expand_parts[0]),
    )
    first = wide // outer
    sent = jnp.broadcast_to(small[None, :, :first], (outer, width // inner, first))
    sent, _ = together(sent, kept)
    sent = lax.all_to_all(sent, "grp", 0, 0, tiled=True)
    come, spatial_come, canvas_grad, sent, hidden_grad, *expand_parts = together(
        come, spatial_come, canvas_grad, sent, hidden_grad, *expand_parts
    )
    kept, other = run(
        side_kernel,
        (f32(kept.shape[0] // 2, *kept.shape[1:]),) * 2,
        (here, kept, come),
        loose=(come,),
    )
    come = swap_mask(pinned(other), 4)
    spatial_parts = spread_line(here, [spatial_keep, spatial_come])
    reduce_parts = spread_line(here, [kept, come])
    ends = together(*reduce_parts, *spatial_parts, *expand_parts)
    deep = outer // 2
    reduce_parts, spatial_parts, expand_parts = ends[:deep], ends[deep : 2 * deep], ends[2 * deep :]
    spatial_grad = total_of(spatial_parts)
    expand_grad = total_of(expand_parts)
    reduce_grad = total_of(reduce_parts)
    canvas_grad = canvas_grad.transpose(2, 0, 1, 3)
    embed_grad = small[:, first:].T
    prototypes_grad = sent.transpose(1, 0, 2).reshape(width // inner, wide)[:, :protos].T
    ids = jnp.arange(CROPS, dtype=jnp.int32)
    crop_loss = jnp.sum(
        (quadrants.T[:, None, :] == ids[None, :, None]) * loss.reshape(CROPS, canvases).T[:, None, :], 2
    )
    return (
        crop_loss,
        canvas_grad,
        reduce_grad,
        spatial_grad,
        expand_grad,
        hidden_grad,
        embed_grad,
        head_sums[0, hidden:],
        prototypes_grad,
        first_back[1],
        first_back[0],
        second_back[1],
        second_back[0],
        third_back[1],
        third_back[0],
        head_sums[1, :hidden],
        head_sums[0, :hidden],
    )


def solution(mesh):
    placed = (
        P(("grp", "in"), None, None, None),
        P(),
        P(),
        P(),
        P(),
        P(),
        P(),
        P(),
        P(),
        P(),
        P(),
        P(),
        P(),
        P(),
        P(),
        P(),
        P(("grp", "in"), None),
        P(("grp", "in"), None, None),
        P(("grp", "in"), None),
    )
    lanes = 128 * mesh.shape["grp"]
    aligned = mesh.shape["in"] * 128 <= 512 and lanes * 2 <= 2048
    return jax.shard_map(
        fast if aligned else on_device,
        mesh=mesh,
        in_specs=placed,
        out_specs=(
            P(("grp", "in"), None),
            P(("grp", "in"), None, None, None),
            P("grp", "in"),
            P("grp", "in"),
            P("grp", "in"),
            P("grp", "in"),
            P("grp", "in"),
            P(),
            P(None, "in"),
            P(),
            P(),
            P(),
            P(),
            P(),
            P(),
            P(),
            P(),
        ),
        check_vma=False,
    )
```
